32 devices in a mesh: turb: 2 (over x), age: 4 (over z), span: 4 (over y, core).
Axes of the slice: x: 2, y: 2, z: 4, core: 2. Of those that a mesh axis runs over, the one named last changes fastest.
Arguments:
- positions: float32 [3, 4, 3, 64, 512], P(None, 'turb', None, 'span', 'age'), may hold values from -6 to 6
- strengths: float32 [2, 4, 3, 64, 512], P(None, 'turb', None, 'span', 'age'), may hold values from -12 to 12
- core_radius: float32 [4, 3, 64, 512], P('turb', None, 'span', 'age'), may hold values from 0.3 to 1.5
- adjoint_seed: float32 [3, 4, 3, 64, 512], P(None, 'turb', None, 'span', 'age'), may hold values from -6 to 6
- pair_target: int32 [2, 4, 4, 128], P('turb', 'age', 'span'), may hold values from 0 to 95
- pair_owner: int32 [2, 4, 4, 128], P('turb', 'age', 'span'), may hold values from 0 to 7, as said below
- pair_source: int32 [2, 4, 4, 128], P('turb', 'age', 'span'), may hold values from 0 to 95
Outputs:
- advected: float32 [3, 4, 3, 64, 512], P(None, 'turb', None, 'span', 'age')
- grad_positions: float32 [3, 4, 3, 64, 512], P(None, 'turb', None, 'span', 'age')
- grad_strengths: float32 [2, 4, 3, 64, 512], P(None, 'turb', None, 'span', 'age')
The draws below stay inside these ranges and needn't reach their ends.
Inputs may be any that keep to these rules, and one draw needn't show every extreme that they name: `pair_owner`: at most 32 of the pairs of one device name one owner. One owner, the same for all devices, is named by exactly 32 pairs of every device.
All inputs are finite; a program needn't handle non-finite values.
Results may differ from the reference program's by a relative error of at most 0.0003.
Values sent between devices are 32-bit elements; how exact they have to be, the bound alone decides.
A program may use at most 64 MiB of HBM per device.

```python
import math
import jax
import jax.numpy as jnp
from jax import lax

TURB_DEV = 2
BLADES = 3
STA_DEV = 16
AGE_DEV = 128
REACH = 8
PAIRS = 128
NTURB = 4
STATIONS = 64
AGES = 512
GROUP = 8
CAP = 32
BLK = 96
N_TURB = 2
N_AGE = 4
N_SPAN = 4


def draw_pair_owner(key, part):
    hottest = jax.random.randint(jax.random.fold_in(key, 11), (), 0, GROUP)
    devices = N_TURB * N_AGE * N_SPAN
    keys = jax.random.split(jax.random.fold_in(key, 23), devices)

    def one_device(device_key):
        first_key, second_key = jax.random.split(device_key)
        others = jnp.arange((GROUP - 1) * CAP, dtype=jnp.int32) // CAP
        others = jnp.where(others >= hottest, others + 1, others)
        picked = jax.random.permutation(first_key, others)[:PAIRS - CAP]
        listed = jnp.concatenate([jnp.full((CAP,), hottest, dtype=jnp.int32), picked.astype(jnp.int32)])
        return jax.random.permutation(second_key, listed)
    return jax.vmap(one_device)(keys).reshape(N_TURB, N_AGE, N_SPAN, PAIRS).astype(jnp.int32)


def with_ends(entries, own_key, least, top_value):
    dims = entries.shape
    index_at = [jax.random.randint(jax.random.fold_in(own_key, axis), (), 0, dims[axis]) for axis in range(len(dims))]
    entries = entries.at[tuple(index_at)].set(least)
    longest = dims.index(max(dims))
    index_at[longest] = (index_at[longest] + 1) % dims[longest]
    return entries.at[tuple(index_at)].set(top_value)


def shard_levels(own_key, dims, pieces, low, high):
    def one(axis_at, parts):
        heights = jax.random.uniform(jax.random.fold_in(jax.random.fold_in(own_key, 6), axis_at), (parts,), jnp.float32, low / len(pieces), high / len(pieces))
        return jnp.repeat(jnp.exp(heights), dims[axis_at] // parts).reshape((-1,) + (1,) * (len(dims) - axis_at - 1))

    gain = one(*pieces[0])
    for cut in pieces[1:]:
        gain = gain * one(*cut)
    return gain


def centred(own_key, shape, width, bound, cuts=(), kind=jnp.bfloat16):
    loudness = shard_levels(own_key, shape, cuts, -0.22, 0.18) if cuts else 1.0
    entries = jax.random.normal(own_key, shape, jnp.float32) * width * loudness
    return jnp.minimum(jnp.maximum(entries, -bound), bound).astype(kind)


def setup_inputs(seed: int = 0) -> dict:
    streams_of = jax.random.split(jax.random.key(seed), 8)
    return {
        "positions": centred(streams_of[0], (3, NTURB, BLADES, STATIONS, AGES), 1.0, 6.0, ((1, 2), (3, 4), (4, 4)), jnp.float32),
        "strengths": centred(streams_of[1], (2, NTURB, BLADES, STATIONS, AGES), 2.0, 12.0, ((1, 2), (3, 4), (4, 4)), jnp.float32),
        "core_radius": jnp.clip(jnp.exp(math.log(1.5) - 1.60943787 * jax.random.uniform(streams_of[2], (NTURB, BLADES, STATIONS, AGES), jnp.float32) ** shard_levels(streams_of[2], (NTURB, BLADES, STATIONS, AGES), ((0, 2), (2, 4), (3, 4)), -0.2, 0.2)), 0.3, 1.5),
        "adjoint_seed": centred(streams_of[3], (3, NTURB, BLADES, STATIONS, AGES), 1.0, 6.0, ((1, 2), (3, 4), (4, 4)), jnp.float32),
        "pair_target": with_ends(jax.random.randint(streams_of[4], (N_TURB, N_AGE, N_SPAN, PAIRS), 0, BLK), jax.random.fold_in(streams_of[4], 1), 0, BLK - 1).astype(jnp.int32),
        "pair_owner": draw_pair_owner(jax.random.fold_in(streams_of[7], 71), 0),
        "pair_source": with_ends(jax.random.randint(streams_of[6], (N_TURB, N_AGE, N_SPAN, PAIRS), 0, BLK), jax.random.fold_in(streams_of[6], 1), 0, BLK - 1).astype(jnp.int32),
    }


time_step = 0.5
four_pi = 4.0 * math.pi
batch_rows = 128

def windows(payload):
    age_count = payload.shape[-1]
    padded = jnp.pad(payload, ((0, 0), (0, 0), (REACH, REACH)))
    stacked = jnp.stack([padded[:, :, REACH + offset:REACH + offset + age_count] for offset in range(-REACH, REACH)])
    shifted = jnp.arange(-REACH, REACH, dtype=jnp.int32)[:, None] + jnp.arange(age_count, dtype=jnp.int32)[None, :]
    inside = ((shifted >= 0) & (shifted < age_count)).astype(payload.dtype)
    return (stacked, inside)

def induced(targets, payload):
    stacked, inside = windows(payload)
    begins = stacked[:, :, 0:3]
    end_points = jnp.stack([stacked[:, :, 3:6], stacked[:, :, 6:9]])
    gammas = jnp.stack([stacked[:, :, 9], stacked[:, :, 10]]) * inside[None, :, None, :]
    core = jnp.where(inside[:, None, :] > 0, stacked[:, :, 11], 1.0)
    core_sq = core * core
    core_quad = core_sq * core_sq
    from_begin = targets[None] - begins
    from_end = targets[None, None] - end_points
    along = end_points - begins[None]
    near = from_begin[None]
    cross_x = near[..., 1, :] * from_end[..., 2, :] - near[..., 2, :] * from_end[..., 1, :]
    cross_y = near[..., 2, :] * from_end[..., 0, :] - near[..., 0, :] * from_end[..., 2, :]
    cross_z = near[..., 0, :] * from_end[..., 1, :] - near[..., 1, :] * from_end[..., 0, :]
    cross_sq = cross_x * cross_x + cross_y * cross_y + cross_z * cross_z
    length_sq = lax.optimization_barrier(jnp.sum(along * along, axis=-2)) + core_sq
    dist_begin = jnp.sqrt(lax.optimization_barrier(jnp.sum(from_begin * from_begin, axis=-2)) + core_sq)
    dist_end = jnp.sqrt(lax.optimization_barrier(jnp.sum(from_end * from_end, axis=-2)) + core_sq)
    projected = lax.optimization_barrier(jnp.sum(along * (near / dist_begin[None, :, :, None, :] - from_end / dist_end[..., None, :]), axis=-2))
    factor = gammas * projected / (four_pi * jnp.sqrt(cross_sq * cross_sq + core_quad * length_sq * length_sq))
    return jnp.stack([lax.optimization_barrier(jnp.sum(cross_x * factor, axis=(0, 1))), lax.optimization_barrier(jnp.sum(cross_y * factor, axis=(0, 1))), lax.optimization_barrier(jnp.sum(cross_z * factor, axis=(0, 1)))], axis=1)

def to_blocks(array):
    rows = array.shape[0]
    split = array.reshape(rows, N_TURB, TURB_DEV, BLADES, N_SPAN, STA_DEV, N_AGE, AGE_DEV)
    return jnp.transpose(split, (1, 6, 4, 2, 3, 5, 0, 7)).reshape(-1, rows, AGE_DEV)

def from_blocks(blocks):
    rows = blocks.shape[1]
    split = blocks.reshape(N_TURB, N_AGE, N_SPAN, TURB_DEV, BLADES, STA_DEV, rows, AGE_DEV)
    return jnp.transpose(split, (6, 0, 3, 4, 2, 5, 1, 7)).reshape(rows, N_TURB * TURB_DEV, BLADES, N_SPAN * STA_DEV, N_AGE * AGE_DEV)

def segment_data(nodes, circulation, core_radius):
    age_count = nodes.shape[-1]
    station_count = nodes.shape[3]
    trail_end = jnp.concatenate([nodes[..., 1:], jnp.zeros_like(nodes[..., :1])], axis=-1)
    shed_end = jnp.concatenate([nodes[:, :, :, 1:, :], jnp.zeros_like(nodes[:, :, :, :1, :])], axis=3)
    age_keep = (jnp.arange(age_count, dtype=jnp.int32) < age_count - 1).astype(nodes.dtype)
    station_keep = (jnp.arange(station_count, dtype=jnp.int32) < station_count - 1).astype(nodes.dtype)
    trail_gamma = circulation[0] * age_keep
    shed_gamma = circulation[1] * station_keep[:, None]
    return jnp.concatenate([nodes, trail_end, shed_end, trail_gamma[None], shed_gamma[None], core_radius[None]], axis=0)

def reference(positions, strengths, core_radius, adjoint_seed, pair_target, pair_owner, pair_source):
    devices = N_TURB * N_AGE * N_SPAN
    blocks_dev = TURB_DEV * BLADES * STA_DEV
    device_ids = jnp.arange(devices, dtype=jnp.int32)[:, None]
    target_index = (device_ids * blocks_dev + pair_target.reshape(devices, -1).astype(jnp.int32)).reshape(-1)
    span_ids = device_ids % N_SPAN
    source_index = ((pair_owner.reshape(devices, -1).astype(jnp.int32) * N_SPAN + span_ids) * blocks_dev + pair_source.reshape(devices, -1).astype(jnp.int32)).reshape(-1)
    total = target_index.shape[0]

    def batch_velocity(operands):
        return induced(operands[0], operands[1])

    def advect(nodes, circulation):
        payload = to_blocks(segment_data(nodes, circulation, core_radius))
        targets = to_blocks(nodes)
        pair_targets = targets[target_index].reshape(total // batch_rows, batch_rows, 3, AGE_DEV)
        pair_payload = payload[source_index].reshape(total // batch_rows, batch_rows, 12, AGE_DEV)
        velocity = lax.map(jax.checkpoint(batch_velocity), (pair_targets, pair_payload))
        summed = jnp.zeros_like(targets).at[target_index].add(velocity.reshape(total, 3, AGE_DEV))
        moved = nodes + time_step * from_blocks(summed)
        return moved.at[0].add(time_step)
    advected, pullback = jax.vjp(advect, positions, strengths)
    grad_positions, grad_strengths = pullback(adjoint_seed)
    return (advected, grad_positions, grad_strengths)
```

```python
import functools
import math

import jax
import jax.numpy as jnp
from jax import lax
from jax.experimental import pallas as pl
from jax.experimental.pallas import tpu as pltpu
from jax.sharding import PartitionSpec as P

REACH = 8


time_step = 0.5
four_pi = 4.0 * math.pi
batch_rows = 16


def shifted_2(value, axis, steps):
    count = lax.axis_size(axis)
    leading, last = (max(0, -steps), min(count, count - steps))
    return lax.ppermute(value, axis, [(source, source + steps) for source in range(leading, last)])


def windows(payload):
    age_count = payload.shape[-1]
    padded = jnp.pad(payload, ((0, 0), (0, 0), (REACH, REACH)))
    stacked = jnp.stack(
        [
            padded[:, :, REACH + offset : REACH + offset + age_count]
            for offset in range(-REACH, REACH)
        ]
    )
    shifted = (
        jnp.arange(-REACH, REACH, dtype=jnp.int32)[:, None]
        + jnp.arange(age_count, dtype=jnp.int32)[None, :]
    )
    inside = ((shifted >= 0) & (shifted < age_count)).astype(payload.dtype)
    return (stacked, inside)


def induced(targets, payload):
    stacked, inside = windows(payload)
    begins = stacked[:, :, 0:3]
    end_points = jnp.stack([stacked[:, :, 3:6], stacked[:, :, 6:9]])
    gammas = jnp.stack([stacked[:, :, 9], stacked[:, :, 10]]) * inside[None, :, None, :]
    core = jnp.where(inside[:, None, :] > 0, stacked[:, :, 11], 1.0)
    core_sq = core * core
    core_quad = core_sq * core_sq
    from_begin = targets[None] - begins
    from_end = targets[None, None] - end_points
    along = end_points - begins[None]
    near = from_begin[None]
    cross_x = near[..., 1, :] * from_end[..., 2, :] - near[..., 2, :] * from_end[..., 1, :]
    cross_y = near[..., 2, :] * from_end[..., 0, :] - near[..., 0, :] * from_end[..., 2, :]
    cross_z = near[..., 0, :] * from_end[..., 1, :] - near[..., 1, :] * from_end[..., 0, :]
    cross_sq = cross_x * cross_x + cross_y * cross_y + cross_z * cross_z
    length_sq = jnp.sum(along * along, axis=-2) + core_sq
    dist_begin = jnp.sqrt(jnp.sum(from_begin * from_begin, axis=-2) + core_sq)
    dist_end = jnp.sqrt(jnp.sum(from_end * from_end, axis=-2) + core_sq)
    projected = jnp.sum(
        along * (near / dist_begin[None, :, :, None, :] - from_end / dist_end[..., None, :]),
        axis=-2,
    )
    factor = (
        gammas
        * projected
        / (four_pi * jnp.sqrt(cross_sq * cross_sq + core_quad * length_sq * length_sq))
    )
    return jnp.stack(
        [
            jnp.sum(cross_x * factor, axis=(0, 1)),
            jnp.sum(cross_y * factor, axis=(0, 1)),
            jnp.sum(cross_z * factor, axis=(0, 1)),
        ],
        axis=1,
    )


def run_pairs(targets, payload, cotangent):
    number = targets.shape[0]
    age_count = targets.shape[-1]

    def one_batch(operands):
        velocity, pullback = jax.vjp(induced, operands[0], operands[1])
        grad_targets, grad_payload = pullback(operands[2])
        return (velocity, grad_targets, grad_payload)

    shaped = (
        targets.reshape(number // batch_rows, batch_rows, 3, age_count),
        payload.reshape(number // batch_rows, batch_rows, 12, age_count),
        cotangent.reshape(number // batch_rows, batch_rows, 3, age_count),
    )
    velocity, grad_targets, grad_payload = lax.map(one_batch, shaped)
    return (
        velocity.reshape(number, 3, age_count),
        grad_targets.reshape(number, 3, age_count),
        grad_payload.reshape(number, 12, age_count),
    )


def onehot_sum(indices, rows, values):
    selector = (jnp.arange(rows, dtype=jnp.int32)[:, None] == indices[None, :]).astype(jnp.float32)
    flat = values.reshape(values.shape[0], -1)
    summed = jnp.dot(
        selector, flat, precision=lax.Precision.HIGHEST, preferred_element_type=jnp.float32
    )
    return summed.reshape((rows,) + values.shape[1:])


def local_sparse(positions, strengths, core_radius, adjoint_seed, pair_target, pair_owner, pair_source):
    shape_here = positions.shape
    station_here = shape_here[3]
    age_here = shape_here[4]
    blocks_here = shape_here[1] * shape_here[2] * station_here
    group_size = lax.axis_size("turb") * lax.axis_size("age")
    pair_count = pair_target.shape[-1]
    capacity = 2 * pair_count // group_size
    target_ids = pair_target.reshape(pair_count)
    owner_ids = pair_owner.reshape(pair_count)
    source_ids = pair_source.reshape(pair_count)
    next_ages = shifted_2(positions[..., 0], "age", -1)
    next_stations = shifted_2(positions[:, :, :, 0, :], "span", -1)
    age_keep = (
        lax.axis_index("age") * age_here + jnp.arange(age_here, dtype=jnp.int32)
        < age_here * lax.axis_size("age") - 1
    ).astype(jnp.float32)
    station_keep = (
        lax.axis_index("span") * station_here + jnp.arange(station_here, dtype=jnp.int32)
        < station_here * lax.axis_size("span") - 1
    ).astype(jnp.float32)

    def build(nodes, after_age, after_station, circulation):
        trail_end = jnp.concatenate([nodes[..., 1:], after_age[..., None]], axis=-1)
        shed_end = jnp.concatenate([nodes[:, :, :, 1:, :], after_station[:, :, :, None, :]], axis=3)
        trail_gamma = circulation[0] * age_keep
        shed_gamma = circulation[1] * station_keep[:, None]
        stacked = jnp.concatenate(
            [nodes, trail_end, shed_end, trail_gamma[None], shed_gamma[None], core_radius[None]],
            axis=0,
        )
        return jnp.transpose(stacked.reshape(12, blocks_here, age_here), (1, 0, 2))

    payload, build_pullback = jax.vjp(build, positions, next_ages, next_stations, strengths)

    def to_rows(array):
        return jnp.transpose(array.reshape(array.shape[0], blocks_here, age_here), (1, 0, 2))

    def from_rows(array):
        return jnp.transpose(array, (1, 0, 2)).reshape(shape_here)

    target_blocks = to_rows(positions)
    seed_blocks = to_rows(adjoint_seed) * time_step
    owner_onehot = (owner_ids[:, None] == jnp.arange(group_size, dtype=jnp.int32)[None, :]).astype(
        jnp.int32
    )
    rank_within = jnp.sum((jnp.cumsum(owner_onehot, axis=0) - owner_onehot) * owner_onehot, axis=1)
    slot_index = owner_ids * capacity + rank_within
    request = (
        jnp.zeros((group_size * capacity,), jnp.int32)
        .at[slot_index]
        .set(source_ids)
        .reshape(group_size, capacity)
    )
    asked = lax.all_to_all(
        request, ("turb", "age"), split_axis=0, concat_axis=0, tiled=True
    ).reshape(group_size * capacity)
    pair_targets = target_blocks[target_ids]
    pair_seed = seed_blocks[target_ids]
    outgoing = (
        jnp.zeros((group_size * capacity, 6, age_here), jnp.float32)
        .at[slot_index]
        .set(jnp.concatenate([pair_targets, pair_seed], axis=1))
    )
    incoming = lax.all_to_all(
        outgoing.reshape(group_size, capacity, 6, age_here),
        ("turb", "age"),
        split_axis=0,
        concat_axis=0,
        tiled=True,
    )
    incoming = incoming.reshape(group_size * capacity, 6, age_here)
    slot_velocity, slot_grad, payload_terms = run_pairs(
        incoming[:, 0:3], payload[asked], incoming[:, 3:6]
    )
    results = jnp.concatenate([slot_velocity, slot_grad], axis=1).reshape(
        group_size, capacity, 6, age_here
    )
    answered = lax.all_to_all(
        results, ("turb", "age"), split_axis=0, concat_axis=0, tiled=True
    ).reshape(group_size * capacity, 6, age_here)[slot_index]
    pair_velocity = answered[:, 0:3]
    pair_grad = answered[:, 3:6]
    payload_grad = onehot_sum(asked, blocks_here, payload_terms)
    velocity = onehot_sum(target_ids, blocks_here, pair_velocity)
    target_grad = onehot_sum(target_ids, blocks_here, pair_grad)
    advected = positions + time_step * from_rows(velocity)
    advected = advected.at[0].add(time_step)
    grad_nodes, grad_after_age, grad_after_station, grad_strengths = build_pullback(payload_grad)
    from_prior_age = shifted_2(grad_after_age, "age", 1)
    from_prior_station = shifted_2(grad_after_station, "span", 1)
    grad_positions = adjoint_seed + grad_nodes + from_rows(target_grad)
    grad_positions = grad_positions.at[..., 0].add(from_prior_age)
    grad_positions = grad_positions.at[:, :, :, 0, :].add(from_prior_station)
    return (advected, grad_positions, grad_strengths)


TILE = 8
SRC_ROWS = 16
TGT_ROWS = 8


def cross(a, b):
    return (
        a[1] * b[2] - a[2] * b[1],
        a[2] * b[0] - a[0] * b[2],
        a[0] * b[1] - a[1] * b[0],
    )


def dot(a, b):
    return a[0] * b[0] + a[1] * b[1] + a[2] * b[2]


def segment(r0, r1, r2, inv1, cube1, gamma, core_sq, quad, quart, inside, w):
    c = cross(r0, r1)
    c_sq = dot(c, c)
    a = dot(r0, r1)
    b = dot(r0, r2)
    inv2 = lax.rsqrt(dot(r2, r2) + core_sq)
    proj = a * inv1 - b * inv2
    inv_d = lax.rsqrt(c_sq * c_sq + quart)
    inv_d = jnp.where(inside, inv_d, 0.0)
    q = dot(w, c)
    m = gamma * inv_d
    k = m * proj
    gp = m * q
    fd = (k * q) * (inv_d * inv_d)
    grad_gamma = proj * (q * inv_d)
    h = 2.0 * fd * c_sq
    gn2 = gp * b * (inv2 * inv2 * inv2)
    alpha = gp * (inv1 - inv2) - gn2
    beta = gn2 - gp * a * cube1
    delta = 2.0 * (gp * inv2 - fd * quad) + gn2
    gc = tuple(k * w[i] - h * c[i] for i in range(3))
    left = cross(gc, r0)
    right = cross(r1, gc)
    grad_r1 = tuple(left[i] + alpha * r0[i] + beta * r1[i] for i in range(3))
    grad_r0 = tuple(right[i] + alpha * r1[i] + delta * r0[i] for i in range(3))
    velocity = tuple(k * c[i] for i in range(3))
    return velocity, grad_r1, grad_r0, grad_gamma


def pair_tile(rows, ages):
    lane = lax.broadcasted_iota(jnp.int32, (TILE, ages), 1)
    begin = rows[0:3]
    core = rows[5]
    core_sq = core * core
    trail = [
        jnp.where(
            lane == ages - 1,
            pltpu.roll(rows[6 + i], ages - 1, 1),
            pltpu.roll(begin[i], ages - 1, 1),
        )
        for i in range(3)
    ]
    alongs = [[trail[i] - begin[i] for i in range(3)], [rows[9 + i] - begin[i] for i in range(3)]]
    gammas = [rows[3] * (1.0 / four_pi), rows[4] * (1.0 / four_pi)]
    core_quad = core_sq * core_sq
    lengths = [dot(r0, r0) + core_sq for r0 in alongs]
    quads = [core_quad * length for length in lengths]
    quarts = [quad * length for quad, length in zip(quads, lengths)]
    zero = jnp.zeros((TILE, ages), jnp.float32)
    sum_r1 = [zero] * 3
    sum_r0 = [[zero] * 3, [zero] * 3]
    sum_gamma = [zero, zero]
    out = [zero] * 6
    for offset in range(-REACH, REACH):
        shift = offset % ages
        moved = [pltpu.roll(x, shift, 1) if shift else x for x in rows[12:18]]
        target, w = moved[0:3], moved[3:6]
        if offset >= 0:
            inside = lane >= offset
        else:
            inside = lane < ages + offset
        r1 = [target[i] - begin[i] for i in range(3)]
        inv1 = lax.rsqrt(dot(r1, r1) + core_sq)
        cube1 = inv1 * inv1 * inv1
        vel = [None] * 3
        g1 = [None] * 3
        for kind in range(2):
            r0 = alongs[kind]
            r2 = [r1[i] - r0[i] for i in range(3)]
            v, d1, d0, dg = segment(
                r0, r1, r2, inv1, cube1, gammas[kind], core_sq,
                quads[kind], quarts[kind], inside, w,
            )
            vel = [v[i] if kind == 0 else vel[i] + v[i] for i in range(3)]
            g1 = [d1[i] if kind == 0 else g1[i] + d1[i] for i in range(3)]
            sum_r0[kind] = [sum_r0[kind][i] + d0[i] for i in range(3)]
            sum_gamma[kind] = sum_gamma[kind] + dg
        sum_r1 = [sum_r1[i] + g1[i] for i in range(3)]
        back = (-offset) % ages
        both = vel + g1
        out = [out[i] + (pltpu.roll(both[i], back, 1) if back else both[i]) for i in range(6)]
    grad_begin = [-(sum_r1[i] + sum_r0[0][i] + sum_r0[1][i]) for i in range(3)]
    grad_source = grad_begin + sum_r0[0] + sum_r0[1] + [g * (1.0 / four_pi) for g in sum_gamma]
    return grad_source, out


def pairs_kernel(
    group, blocks, stations, per_owner, grad_rows, index_ref, table_ref, seed_ref,
    grad_ref, out_ref, rows_buf, src_buf, tgt_buf, acc, tgt_acc,
):
    pairs = index_ref.shape[1]
    ages = table_ref.shape[-1]
    halo = blocks // stations
    acc[...] = jnp.zeros_like(acc)
    tgt_acc[...] = jnp.zeros_like(tgt_acc)

    def tile(t, _):
        for j in range(TILE):
            p = t * TILE + j
            src = index_ref[0, p]
            nxt = index_ref[1, p]
            shed = index_ref[2, p]
            shed_step = index_ref[3, p]
            own = index_ref[4, p]
            tgt = index_ref[5, p]
            for r in range(6):
                rows_buf[pl.ds(r * TILE + j, 1), :] = table_ref[pl.ds(src + r * blocks, 1), :]
            for r in range(3):
                rows_buf[pl.ds((6 + r) * TILE + j, 1), :] = table_ref[pl.ds(nxt + r * blocks, 1), :]
                rows_buf[pl.ds((9 + r) * TILE + j, 1), :] = table_ref[pl.ds(shed + r * shed_step, 1), :]
                rows_buf[pl.ds((12 + r) * TILE + j, 1), :] = table_ref[pl.ds(own + r * blocks, 1), :]
                rows_buf[pl.ds((15 + r) * TILE + j, 1), :] = seed_ref[pl.ds(tgt + r * blocks, 1), :]
        rows = [rows_buf[pl.ds(r * TILE, TILE), :] for r in range(18)]
        grad_source, out = pair_tile(rows, ages)
        for r in range(11):
            src_buf[pl.ds(t * (TILE * SRC_ROWS) + r, TILE, stride=SRC_ROWS), :] = grad_source[r]
        for r in range(6):
            tgt_buf[pl.ds(t * (TILE * TGT_ROWS) + r, TILE, stride=TGT_ROWS), :] = out[r]
        return 0

    lax.fori_loop(0, pairs // TILE, tile, 0)

    def scatter(p, _):
        at = pl.ds(pl.multiple_of(index_ref[6, p], SRC_ROWS), SRC_ROWS)
        acc[at, :] += src_buf[pl.ds(pl.multiple_of(p * SRC_ROWS, SRC_ROWS), SRC_ROWS), :]
        at = pl.ds(pl.multiple_of(index_ref[5, p] * TGT_ROWS, TGT_ROWS), TGT_ROWS)
        tgt_acc[at, :] += tgt_buf[pl.ds(pl.multiple_of(p * TGT_ROWS, TGT_ROWS), TGT_ROWS), :]
        return 0

    lax.fori_loop(0, pairs, scatter, 0, unroll=8)

    for c in range(6):
        for q in range(0, blocks, 8):
            out_ref[pl.ds(c * blocks + q, 8), :] = tgt_acc[pl.ds(q * TGT_ROWS + c, 8, stride=TGT_ROWS), :]

    lane = lax.broadcasted_iota(jnp.int32, (TILE, ages), 1)
    sub = lax.broadcasted_iota(jnp.int32, (TILE, ages), 0)

    def fold(o, _):
        prev = lax.rem(o + group - 1, group)

        def rows_of(owner, q, r):
            return acc[pl.ds((owner * blocks + q + 1) * SRC_ROWS + r, 8, stride=SRC_ROWS), :]

        base = o * grad_rows
        for q in range(0, blocks, 8):
            for c in range(3):
                trail = jnp.where(lane == ages - 1, rows_of(prev, q, 3 + c), rows_of(o, q, 3 + c))
                shed = rows_of(o, q - 1, 6 + c)
                if q % stations == 0:
                    shed = jnp.where(sub == 0, 0.0, shed)
                grad_ref[pl.ds(base + c * blocks + q, 8), :] = (
                    rows_of(o, q, c) + pltpu.roll(trail, 1, 1) + shed
                )
            for c in range(2):
                grad_ref[pl.ds(base + (3 + c) * blocks + q, 8), :] = rows_of(o, q, 9 + c)
        for c in range(3):
            for h in range(halo):
                row = (o * blocks + h * stations + stations) * SRC_ROWS + 6 + c
                grad_ref[pl.ds(base + 5 * blocks + c * halo + h, 1), :] = acc[pl.ds(row, 1), :]
        grad_ref[pl.ds(base + 5 * blocks + 3 * halo, grad_rows - 5 * blocks - 3 * halo), :] = (
            jnp.zeros((grad_rows - 5 * blocks - 3 * halo, ages), jnp.float32)
        )
        return 0

    lax.fori_loop(0, group, fold, 0)


def local_dense(positions, strengths, core_radius, adjoint_seed, pair_target, pair_owner, pair_source):
    shape_here = positions.shape
    stations = shape_here[3]
    ages = shape_here[4]
    blocks = shape_here[1] * shape_here[2] * stations
    halo = blocks // stations
    group = lax.axis_size("turb") * lax.axis_size("age")
    pairs = pair_target.shape[-1]
    per_owner = -(-(6 * blocks + 3 * halo) // 8) * 8
    grad_rows = -(-(5 * blocks + 3 * halo) // 8) * 8
    target_ids = pair_target.reshape(pairs)
    owner_ids = pair_owner.reshape(pairs)
    source_ids = pair_source.reshape(pairs)
    age_keep = (
        lax.axis_index("age") * ages + jnp.arange(ages, dtype=jnp.int32)
        < ages * lax.axis_size("age") - 1
    ).astype(jnp.float32)
    station_keep = (
        lax.axis_index("span") * stations + jnp.arange(stations, dtype=jnp.int32)
        < stations * lax.axis_size("span") - 1
    ).astype(jnp.float32)[:, None]
    me = lax.axis_index("turb") * lax.axis_size("age") + lax.axis_index("age")
    next_stations = shifted_2(positions[:, :, :, 0, :], "span", -1)
    payload = jnp.concatenate(
        [
            positions.reshape(3 * blocks, ages),
            (strengths[0] * age_keep).reshape(blocks, ages),
            (strengths[1] * station_keep).reshape(blocks, ages),
            core_radius.reshape(blocks, ages),
            next_stations.reshape(3 * halo, ages),
            jnp.zeros((per_owner - 6 * blocks - 3 * halo, ages), jnp.float32),
        ]
    )
    table = lax.all_gather(payload, ("turb", "age"), axis=0, tiled=True)
    station = source_ids % stations
    inner = station < stations - 1
    base = owner_ids * per_owner
    index = jnp.stack(
        [
            base + source_ids,
            (owner_ids + 1) % group * per_owner + source_ids,
            base + jnp.where(inner, source_ids + 1, 6 * blocks + source_ids // stations),
            jnp.where(inner, blocks, halo),
            me * per_owner + target_ids,
            target_ids,
            (owner_ids * blocks + source_ids + 1) * SRC_ROWS,
            target_ids,
        ]
    )
    seed_rows = adjoint_seed.reshape(3 * blocks, ages) * time_step
    vmem = pl.BlockSpec(memory_space=pltpu.VMEM)
    grads, sums = pl.pallas_call(
        functools.partial(pairs_kernel, group, blocks, stations, per_owner, grad_rows),
        out_shape=(
            jax.ShapeDtypeStruct((group * grad_rows, ages), jnp.float32),
            jax.ShapeDtypeStruct((6 * blocks, ages), jnp.float32),
        ),
        in_specs=[pl.BlockSpec(memory_space=pltpu.SMEM), vmem, vmem],
        out_specs=(vmem, vmem),
        scratch_shapes=[
            pltpu.VMEM((18 * TILE, ages), jnp.float32),
            pltpu.VMEM((pairs * SRC_ROWS, ages), jnp.float32),
            pltpu.VMEM((pairs * TGT_ROWS, ages), jnp.float32),
            pltpu.VMEM(((group * blocks + 1) * SRC_ROWS, ages), jnp.float32),
            pltpu.VMEM((blocks * TGT_ROWS, ages), jnp.float32),
        ],
        compiler_params=pltpu.CompilerParams(vmem_limit_bytes=40 * 1024 * 1024),
    )(index, table, seed_rows)
    mine = lax.psum_scatter(grads, ("turb", "age"), scatter_dimension=0, tiled=True)
    advected = positions + time_step * sums[: 3 * blocks].reshape(shape_here)
    advected = advected.at[0].add(time_step)
    grad_positions = (
        adjoint_seed
        + sums[3 * blocks :].reshape(shape_here)
        + mine[: 3 * blocks].reshape(shape_here)
    )
    from_prior = shifted_2(
        mine[5 * blocks : 5 * blocks + 3 * halo].reshape(shape_here[:3] + (ages,)), "span", 1
    )
    grad_positions = grad_positions.at[:, :, :, 0, :].add(from_prior)
    grad_strengths = mine[3 * blocks : 5 * blocks].reshape(strengths.shape)
    grad_strengths = grad_strengths * jnp.stack(
        [
            jnp.broadcast_to(age_keep[None], (stations, ages)),
            jnp.broadcast_to(station_keep, (stations, ages)),
        ]
    )[:, None, None]
    return (advected, grad_positions, grad_strengths)


def local(positions, strengths, core_radius, adjoint_seed, pair_target, pair_owner, pair_source):
    blocks = positions.shape[1] * positions.shape[2] * positions.shape[3]
    group = lax.axis_size("turb") * lax.axis_size("age")
    chosen = local_dense if group * blocks <= 8 * pair_target.shape[-1] else local_sparse
    return chosen(
        positions, strengths, core_radius, adjoint_seed, pair_target, pair_owner, pair_source
    )


def solution(mesh):
    placed = (
        P(None, "turb", None, "span", "age"),
        P(None, "turb", None, "span", "age"),
        P("turb", None, "span", "age"),
        P(None, "turb", None, "span", "age"),
        P("turb", "age", "span", None),
        P("turb", "age", "span", None),
        P("turb", "age", "span", None),
    )
    return jax.shard_map(
        local,
        mesh=mesh,
        in_specs=placed,
        out_specs=(
            P(None, "turb", None, "span", "age"),
            P(None, "turb", None, "span", "age"),
            P(None, "turb", None, "span", "age"),
        ),
        check_vma=False,
    )
```

```python
import functools
import math

import jax
import jax.numpy as jnp
from jax import lax
from jax.experimental import pallas as pl
from jax.experimental.pallas import tpu as pltpu
from jax.sharding import PartitionSpec as P

REACH = 8


time_step = 0.5
four_pi = 4.0 * math.pi
batch_rows = 16


def shifted_2(value, axis, steps):
    count = lax.axis_size(axis)
    leading, last = (max(0, -steps), min(count, count - steps))
    return lax.ppermute(value, axis, [(source, source + steps) for source in range(leading, last)])


def windows(payload):
    age_count = payload.shape[-1]
    padded = jnp.pad(payload, ((0, 0), (0, 0), (REACH, REACH)))
    stacked = jnp.stack(
        [
            padded[:, :, REACH + offset : REACH + offset + age_count]
            for offset in range(-REACH, REACH)
        ]
    )
    shifted = (
        jnp.arange(-REACH, REACH, dtype=jnp.int32)[:, None]
        + jnp.arange(age_count, dtype=jnp.int32)[None, :]
    )
    inside = ((shifted >= 0) & (shifted < age_count)).astype(payload.dtype)
    return (stacked, inside)


def induced(targets, payload):
    stacked, inside = windows(payload)
    begins = stacked[:, :, 0:3]
    end_points = jnp.stack([stacked[:, :, 3:6], stacked[:, :, 6:9]])
    gammas = jnp.stack([stacked[:, :, 9], stacked[:, :, 10]]) * inside[None, :, None, :]
    core = jnp.where(inside[:, None, :] > 0, stacked[:, :, 11], 1.0)
    core_sq = core * core
    core_quad = core_sq * core_sq
    from_begin = targets[None] - begins
    from_end = targets[None, None] - end_points
    along = end_points - begins[None]
    near = from_begin[None]
    cross_x = near[..., 1, :] * from_end[..., 2, :] - near[..., 2, :] * from_end[..., 1, :]
    cross_y = near[..., 2, :] * from_end[..., 0, :] - near[..., 0, :] * from_end[..., 2, :]
    cross_z = near[..., 0, :] * from_end[..., 1, :] - near[..., 1, :] * from_end[..., 0, :]
    cross_sq = cross_x * cross_x + cross_y * cross_y + cross_z * cross_z
    length_sq = jnp.sum(along * along, axis=-2) + core_sq
    dist_begin = jnp.sqrt(jnp.sum(from_begin * from_begin, axis=-2) + core_sq)
    dist_end = jnp.sqrt(jnp.sum(from_end * from_end, axis=-2) + core_sq)
    projected = jnp.sum(
        along * (near / dist_begin[None, :, :, None, :] - from_end / dist_end[..., None, :]),
        axis=-2,
    )
    factor = (
        gammas
        * projected
        / (four_pi * jnp.sqrt(cross_sq * cross_sq + core_quad * length_sq * length_sq))
    )
    return jnp.stack(
        [
            jnp.sum(cross_x * factor, axis=(0, 1)),
            jnp.sum(cross_y * factor, axis=(0, 1)),
            jnp.sum(cross_z * factor, axis=(0, 1)),
        ],
        axis=1,
    )


def run_pairs(targets, payload, cotangent):
    number = targets.shape[0]
    age_count = targets.shape[-1]

    def one_batch(operands):
        velocity, pullback = jax.vjp(induced, operands[0], operands[1])
        grad_targets, grad_payload = pullback(operands[2])
        return (velocity, grad_targets, grad_payload)

    shaped = (
        targets.reshape(number // batch_rows, batch_rows, 3, age_count),
        payload.reshape(number // batch_rows, batch_rows, 12, age_count),
        cotangent.reshape(number // batch_rows, batch_rows, 3, age_count),
    )
    velocity, grad_targets, grad_payload = lax.map(one_batch, shaped)
    return (
        velocity.reshape(number, 3, age_count),
        grad_targets.reshape(number, 3, age_count),
        grad_payload.reshape(number, 12, age_count),
    )


def onehot_sum(indices, rows, values):
    selector = (jnp.arange(rows, dtype=jnp.int32)[:, None] == indices[None, :]).astype(jnp.float32)
    flat = values.reshape(values.shape[0], -1)
    summed = jnp.dot(
        selector, flat, precision=lax.Precision.HIGHEST, preferred_element_type=jnp.float32
    )
    return summed.reshape((rows,) + values.shape[1:])


def local_sparse(positions, strengths, core_radius, adjoint_seed, pair_target, pair_owner, pair_source):
    shape_here = positions.shape
    station_here = shape_here[3]
    age_here = shape_here[4]
    blocks_here = shape_here[1] * shape_here[2] * station_here
    group_size = lax.axis_size("turb") * lax.axis_size("age")
    pair_count = pair_target.shape[-1]
    capacity = 2 * pair_count // group_size
    target_ids = pair_target.reshape(pair_count)
    owner_ids = pair_owner.reshape(pair_count)
    source_ids = pair_source.reshape(pair_count)
    next_ages = shifted_2(positions[..., 0], "age", -1)
    next_stations = shifted_2(positions[:, :, :, 0, :], "span", -1)
    age_keep = (
        lax.axis_index("age") * age_here + jnp.arange(age_here, dtype=jnp.int32)
        < age_here * lax.axis_size("age") - 1
    ).astype(jnp.float32)
    station_keep = (
        lax.axis_index("span") * station_here + jnp.arange(station_here, dtype=jnp.int32)
        < station_here * lax.axis_size("span") - 1
    ).astype(jnp.float32)

    def build(nodes, after_age, after_station, circulation):
        trail_end = jnp.concatenate([nodes[..., 1:], after_age[..., None]], axis=-1)
        shed_end = jnp.concatenate([nodes[:, :, :, 1:, :], after_station[:, :, :, None, :]], axis=3)
        trail_gamma = circulation[0] * age_keep
        shed_gamma = circulation[1] * station_keep[:, None]
        stacked = jnp.concatenate(
            [nodes, trail_end, shed_end, trail_gamma[None], shed_gamma[None], core_radius[None]],
            axis=0,
        )
        return jnp.transpose(stacked.reshape(12, blocks_here, age_here), (1, 0, 2))

    payload, build_pullback = jax.vjp(build, positions, next_ages, next_stations, strengths)

    def to_rows(array):
        return jnp.transpose(array.reshape(array.shape[0], blocks_here, age_here), (1, 0, 2))

    def from_rows(array):
        return jnp.transpose(array, (1, 0, 2)).reshape(shape_here)

    target_blocks = to_rows(positions)
    seed_blocks = to_rows(adjoint_seed) * time_step
    owner_onehot = (owner_ids[:, None] == jnp.arange(group_size, dtype=jnp.int32)[None, :]).astype(
        jnp.int32
    )
    rank_within = jnp.sum((jnp.cumsum(owner_onehot, axis=0) - owner_onehot) * owner_onehot, axis=1)
    slot_index = owner_ids * capacity + rank_within
    request = (
        jnp.zeros((group_size * capacity,), jnp.int32)
        .at[slot_index]
        .set(source_ids)
        .reshape(group_size, capacity)
    )
    asked = lax.all_to_all(
        request, ("turb", "age"), split_axis=0, concat_axis=0, tiled=True
    ).reshape(group_size * capacity)
    pair_targets = target_blocks[target_ids]
    pair_seed = seed_blocks[target_ids]
    outgoing = (
        jnp.zeros((group_size * capacity, 6, age_here), jnp.float32)
        .at[slot_index]
        .set(jnp.concatenate([pair_targets, pair_seed], axis=1))
    )
    incoming = lax.all_to_all(
        outgoing.reshape(group_size, capacity, 6, age_here),
        ("turb", "age"),
        split_axis=0,
        concat_axis=0,
        tiled=True,
    )
    incoming = incoming.reshape(group_size * capacity, 6, age_here)
    slot_velocity, slot_grad, payload_terms = run_pairs(
        incoming[:, 0:3], payload[asked], incoming[:, 3:6]
    )
    results = jnp.concatenate([slot_velocity, slot_grad], axis=1).reshape(
        group_size, capacity, 6, age_here
    )
    answered = lax.all_to_all(
        results, ("turb", "age"), split_axis=0, concat_axis=0, tiled=True
    ).reshape(group_size * capacity, 6, age_here)[slot_index]
    pair_velocity = answered[:, 0:3]
    pair_grad = answered[:, 3:6]
    payload_grad = onehot_sum(asked, blocks_here, payload_terms)
    velocity = onehot_sum(target_ids, blocks_here, pair_velocity)
    target_grad = onehot_sum(target_ids, blocks_here, pair_grad)
    advected = positions + time_step * from_rows(velocity)
    advected = advected.at[0].add(time_step)
    grad_nodes, grad_after_age, grad_after_station, grad_strengths = build_pullback(payload_grad)
    from_prior_age = shifted_2(grad_after_age, "age", 1)
    from_prior_station = shifted_2(grad_after_station, "span", 1)
    grad_positions = adjoint_seed + grad_nodes + from_rows(target_grad)
    grad_positions = grad_positions.at[..., 0].add(from_prior_age)
    grad_positions = grad_positions.at[:, :, :, 0, :].add(from_prior_station)
    return (advected, grad_positions, grad_strengths)


TILE = 8
SRC_ROWS = 16
TGT_ROWS = 8


def cross(a, b):
    return (
        a[1] * b[2] - a[2] * b[1],
        a[2] * b[0] - a[0] * b[2],
        a[0] * b[1] - a[1] * b[0],
    )


def dot(a, b):
    return a[0] * b[0] + a[1] * b[1] + a[2] * b[2]


def segment(r0, r1, r2, inv1, cube1, gamma, core_sq, quad, quart, inside, w):
    c = cross(r0, r1)
    c_sq = dot(c, c)
    a = dot(r0, r1)
    b = dot(r0, r2)
    inv2 = lax.rsqrt(dot(r2, r2) + core_sq)
    proj = a * inv1 - b * inv2
    inv_d = lax.rsqrt(c_sq * c_sq + quart)
    inv_d = jnp.where(inside, inv_d, 0.0)
    q = dot(w, c)
    m = gamma * inv_d
    k = m * proj
    gp = m * q
    fd = (k * q) * (inv_d * inv_d)
    grad_gamma = proj * (q * inv_d)
    h = 2.0 * fd * c_sq
    gn2 = gp * b * (inv2 * inv2 * inv2)
    alpha = gp * (inv1 - inv2) - gn2
    beta = gn2 - gp * a * cube1
    delta = 2.0 * (gp * inv2 - fd * quad) + gn2
    gc = tuple(k * w[i] - h * c[i] for i in range(3))
    left = cross(gc, r0)
    right = cross(r1, gc)
    grad_r1 = tuple(left[i] + alpha * r0[i] + beta * r1[i] for i in range(3))
    grad_r0 = tuple(right[i] + alpha * r1[i] + delta * r0[i] for i in range(3))
    velocity = tuple(k * c[i] for i in range(3))
    return velocity, grad_r1, grad_r0, grad_gamma


def pair_tile(rows, ages):
    lane = lax.broadcasted_iota(jnp.int32, (TILE, ages), 1)
    begin = rows[0:3]
    core = rows[5]
    core_sq = core * core
    trail = [
        jnp.where(
            lane == ages - 1,
            pltpu.roll(rows[6 + i], ages - 1, 1),
            pltpu.roll(begin[i], ages - 1, 1),
        )
        for i in range(3)
    ]
    alongs = [[trail[i] - begin[i] for i in range(3)], [rows[9 + i] - begin[i] for i in range(3)]]
    gammas = [rows[3] * (1.0 / four_pi), rows[4] * (1.0 / four_pi)]
    core_quad = core_sq * core_sq
    lengths = [dot(r0, r0) + core_sq for r0 in alongs]
    quads = [core_quad * length for length in lengths]
    quarts = [quad * length for quad, length in zip(quads, lengths)]
    zero = jnp.zeros((TILE, ages), jnp.float32)
    sum_r1 = [zero] * 3
    sum_r0 = [[zero] * 3, [zero] * 3]
    sum_gamma = [zero, zero]
    out = [zero] * 6
    for offset in range(-REACH, REACH):
        shift = offset % ages
        moved = [pltpu.roll(x, shift, 1) if shift else x for x in rows[12:18]]
        target, w = moved[0:3], moved[3:6]
        if offset >= 0:
            inside = lane >= offset
        else:
            inside = lane < ages + offset
        r1 = [target[i] - begin[i] for i in range(3)]
        inv1 = lax.rsqrt(dot(r1, r1) + core_sq)
        cube1 = inv1 * inv1 * inv1
        vel = [None] * 3
        g1 = [None] * 3
        for kind in range(2):
            r0 = alongs[kind]
            r2 = [r1[i] - r0[i] for i in range(3)]
            v, d1, d0, dg = segment(
                r0, r1, r2, inv1, cube1, gammas[kind], core_sq,
                quads[kind], quarts[kind], inside, w,
            )
            vel = [v[i] if kind == 0 else vel[i] + v[i] for i in range(3)]
            g1 = [d1[i] if kind == 0 else g1[i] + d1[i] for i in range(3)]
            sum_r0[kind] = [sum_r0[kind][i] + d0[i] for i in range(3)]
            sum_gamma[kind] = sum_gamma[kind] + dg
        sum_r1 = [sum_r1[i] + g1[i] for i in range(3)]
        back = (-offset) % ages
        both = vel + g1
        out = [out[i] + (pltpu.roll(both[i], back, 1) if back else both[i]) for i in range(6)]
    grad_begin = [-(sum_r1[i] + sum_r0[0][i] + sum_r0[1][i]) for i in range(3)]
    grad_source = grad_begin + sum_r0[0] + sum_r0[1] + [g * (1.0 / four_pi) for g in sum_gamma]
    return grad_source, out


def pairs_kernel(
    group, blocks, stations, per_owner, grad_rows, index_ref, table_ref, seed_ref,
    grad_ref, out_ref, rows_buf, src_buf, tgt_buf, acc, tgt_acc,
):
    pairs = index_ref.shape[1]
    ages = table_ref.shape[-1]
    halo = blocks // stations
    acc[...] = jnp.zeros_like(acc)
    tgt_acc[...] = jnp.zeros_like(tgt_acc)

    def tile(t, _):
        for j in range(TILE):
            p = t * TILE + j
            src = index_ref[0, p]
            nxt = index_ref[1, p]
            shed = index_ref[2, p]
            shed_step = index_ref[3, p]
            own = index_ref[4, p]
            tgt = index_ref[5, p]
            for r in range(6):
                rows_buf[pl.ds(r * TILE + j, 1), :] = table_ref[pl.ds(src + r * blocks, 1), :]
            for r in range(3):
                rows_buf[pl.ds((6 + r) * TILE + j, 1), :] = table_ref[pl.ds(nxt + r * blocks, 1), :]
                rows_buf[pl.ds((9 + r) * TILE + j, 1), :] = table_ref[pl.ds(shed + r * shed_step, 1), :]
                rows_buf[pl.ds((12 + r) * TILE + j, 1), :] = table_ref[pl.ds(own + r * blocks, 1), :]
                rows_buf[pl.ds((15 + r) * TILE + j, 1), :] = seed_ref[pl.ds(tgt + r * blocks, 1), :] * time_step
        rows = [rows_buf[pl.ds(r * TILE, TILE), :] for r in range(18)]
        grad_source, out = pair_tile(rows, ages)
        for r in range(11):
            src_buf[pl.ds(t * (TILE * SRC_ROWS) + r, TILE, stride=SRC_ROWS), :] = grad_source[r]
        for r in range(6):
            tgt_buf[pl.ds(t * (TILE * TGT_ROWS) + r, TILE, stride=TGT_ROWS), :] = out[r]
        return 0

    lax.fori_loop(0, pairs // TILE, tile, 0)

    def scatter(p, _):
        at = pl.ds(pl.multiple_of(index_ref[6, p], SRC_ROWS), SRC_ROWS)
        acc[at, :] += src_buf[pl.ds(pl.multiple_of(p * SRC_ROWS, SRC_ROWS), SRC_ROWS), :]
        at = pl.ds(pl.multiple_of(index_ref[5, p] * TGT_ROWS, TGT_ROWS), TGT_ROWS)
        tgt_acc[at, :] += tgt_buf[pl.ds(pl.multiple_of(p * TGT_ROWS, TGT_ROWS), TGT_ROWS), :]
        return 0

    lax.fori_loop(0, pairs, scatter, 0, unroll=8)

    for c in range(6):
        for q in range(0, blocks, 8):
            out_ref[pl.ds(c * blocks + q, 8), :] = tgt_acc[pl.ds(q * TGT_ROWS + c, 8, stride=TGT_ROWS), :]

    lane = lax.broadcasted_iota(jnp.int32, (TILE, ages), 1)
    sub = lax.broadcasted_iota(jnp.int32, (TILE, ages), 0)

    def fold(o, _):
        prev = lax.rem(o + group - 1, group)

        def rows_of(owner, q, r):
            return acc[pl.ds((owner * blocks + q + 1) * SRC_ROWS + r, 8, stride=SRC_ROWS), :]

        base = o * grad_rows
        for q in range(0, blocks, 8):
            for c in range(3):
                trail = jnp.where(lane == ages - 1, rows_of(prev, q, 3 + c), rows_of(o, q, 3 + c))
                shed = rows_of(o, q - 1, 6 + c)
                if q % stations == 0:
                    shed = jnp.where(sub == 0, 0.0, shed)
                grad_ref[pl.ds(base + c * blocks + q, 8), :] = (
                    rows_of(o, q, c) + pltpu.roll(trail, 1, 1) + shed
                )
            for c in range(2):
                grad_ref[pl.ds(base + (3 + c) * blocks + q, 8), :] = rows_of(o, q, 9 + c)
        for c in range(3):
            for h in range(halo):
                row = (o * blocks + h * stations + stations) * SRC_ROWS + 6 + c
                grad_ref[pl.ds(base + 5 * blocks + c * halo + h, 1), :] = acc[pl.ds(row, 1), :]
        grad_ref[pl.ds(base + 5 * blocks + 3 * halo, grad_rows - 5 * blocks - 3 * halo), :] = (
            jnp.zeros((grad_rows - 5 * blocks - 3 * halo, ages), jnp.float32)
        )
        return 0

    lax.fori_loop(0, group, fold, 0)


MESH = pl.DeviceIdType.MESH


def place():
    here = (lax.axis_index("turb"), lax.axis_index("age"), lax.axis_index("span"))
    spans = lax.axis_size("span")
    turb, age, span = here
    return (
        here,
        (1 - turb, age, span),
        (turb, age - 1, span),
        (turb, age + 1, span),
        (turb, age, lax.rem(span + spans - 1, spans)),
        (turb, age, lax.rem(span + 1, spans)),
    )


def greet(ages_count):
    here, other, below, above, prior, following = place()
    barrier = pltpu.get_barrier_semaphore()
    for device in (other, prior, following):
        pl.semaphore_signal(barrier, inc=1, device_id=device, device_id_type=MESH)

    @pl.when(here[1] > 0)
    def _():
        pl.semaphore_signal(barrier, inc=1, device_id=below, device_id_type=MESH)

    @pl.when(here[1] < ages_count - 1)
    def _():
        pl.semaphore_signal(barrier, inc=1, device_id=above, device_id_type=MESH)

    inner = (here[1] > 0).astype(jnp.int32) + (here[1] < ages_count - 1).astype(jnp.int32)
    pl.semaphore_wait(barrier, 3 + inner)


def keeps(stations, ages, shape):
    lane = lax.broadcasted_iota(jnp.int32, shape, 1)
    row = lax.broadcasted_iota(jnp.int32, shape, 0)
    last_age = lax.axis_index("age") == lax.axis_size("age") - 1
    last_station = lax.axis_index("span") == lax.axis_size("span") - 1
    trail = jnp.where(jnp.logical_and(last_age, lane == ages - 1), 0.0, 1.0)
    shed = jnp.where(jnp.logical_and(last_station, row % stations == stations - 1), 0.0, 1.0)
    return trail, shed


def gather_kernel(
    blocks, stations, per_owner, positions_ref, strengths_ref, core_ref, table_ref,
    halo_buf, halo_sems, send_sems, recv_sems,
):
    ages = table_ref.shape[-1]
    count = lax.axis_size("age")
    halo = blocks // stations
    here, other, below, above, prior, following = place()
    turb, age, span = here
    split = 5 * blocks
    me = turb * count + age
    mate = (1 - turb) * count + age
    extra = per_owner - 6 * blocks
    parts = ((0, split), (split, per_owner - split))

    def rows(owner, part):
        return pl.ds(pl.multiple_of(owner * per_owner + parts[part][0], 8), parts[part][1])

    def copy(owner, part, way):
        at = rows(owner, part)
        return pltpu.make_async_remote_copy(
            src_ref=table_ref.at[at],
            dst_ref=table_ref.at[at],
            send_sem=send_sems.at[way, part, owner],
            recv_sem=recv_sems.at[part, owner],
            device_id=(other, below, above)[way],
            device_id_type=MESH,
        )

    def arrive(owner, part):
        copy(owner, part, 0).wait_recv()

    base = me * per_owner
    halo_buf[...] = jnp.zeros_like(halo_buf)
    for k in range(3 * halo):
        halo_buf[pl.ds(k, 1), :] = positions_ref[pl.ds(k * stations, 1), :]
    table_ref[pl.ds(pl.multiple_of(base, 8), 3 * blocks), :] = positions_ref[...]
    trail, shed = keeps(stations, ages, (blocks, ages))
    table_ref[pl.ds(pl.multiple_of(base + 3 * blocks, 8), blocks), :] = (
        strengths_ref[pl.ds(0, blocks), :] * trail
    )
    table_ref[pl.ds(pl.multiple_of(base + 4 * blocks, 8), blocks), :] = (
        strengths_ref[pl.ds(blocks, blocks), :] * shed
    )
    table_ref[pl.ds(pl.multiple_of(base + 5 * blocks, 8), blocks), :] = core_ref[...]
    greet(count)
    halo_copy = pltpu.make_async_remote_copy(
        src_ref=halo_buf,
        dst_ref=table_ref.at[pl.ds(pl.multiple_of(base + 6 * blocks, 8), extra)],
        send_sem=halo_sems.at[0],
        recv_sem=halo_sems.at[1],
        device_id=prior,
        device_id_type=MESH,
    )
    halo_copy.start()

    has_below = age > 0
    has_above = age < count - 1

    @pl.when(has_below)
    def _():
        copy(me, 0, 1).start()

    @pl.when(has_above)
    def _():
        copy(me, 0, 2).start()

    copy(me, 0, 0).start()
    halo_copy.wait_recv()
    copy(me, 1, 0).start()

    @pl.when(has_below)
    def _():
        copy(me, 1, 1).start()

    @pl.when(has_above)
    def _():
        copy(me, 1, 2).start()

    arrive(mate, 1)

    @pl.when(has_below)
    def _():
        copy(mate, 1, 1).start()

    @pl.when(has_above)
    def _():
        copy(mate, 1, 2).start()

    for step in range(1, count):
        for way, sign in ((2, -1), (1, 1)):
            source = age + sign * step
            exists = source >= 0 if sign < 0 else source < count
            onward = has_above if way == 2 else has_below

            @pl.when(exists)
            def _(source=source, way=way, onward=onward):
                owner = turb * count + source
                arrive(owner, 0)

                @pl.when(onward)
                def _():
                    copy(owner, 0, way).start()

                copy(owner, 0, 0).start()

        for way, sign in ((2, -1), (1, 1)):
            source = age + sign * step
            exists = source >= 0 if sign < 0 else source < count
            onward = has_above if way == 2 else has_below

            @pl.when(exists)
            def _(source=source, way=way, onward=onward):
                for column in (turb, 1 - turb):
                    owner = column * count + source
                    arrive(owner, 1)

                    @pl.when(onward)
                    def _(owner=owner):
                        copy(owner, 1, way).start()

    for source in range(count):
        arrive((1 - turb) * count + source, 0)
    halo_copy.wait_send()
    copy(me, 1, 0).wait_send()
    for source in range(count):
        owner = turb * count + source
        copy(owner, 0, 0).wait_send()

        @pl.when(jnp.logical_and(source >= age, has_below))
        def _(source=source, owner=owner):
            copy(owner, 0, 1).wait_send()
            copy(owner, 1, 1).wait_send()
            copy((1 - turb) * count + source, 1, 1).wait_send()

        @pl.when(jnp.logical_and(source <= age, has_above))
        def _(source=source, owner=owner):
            copy(owner, 0, 2).wait_send()
            copy(owner, 1, 2).wait_send()
            copy((1 - turb) * count + source, 1, 2).wait_send()


def reduce_kernel(
    blocks, stations, grad_rows, early, grads_ref, sums_ref, positions_ref, seed_ref,
    advected_ref, positions_grad_ref, strengths_grad_ref,
    work, from_mate, from_below, from_above, late_buf, late_in, halo_out, halo_in,
    mate_sems, chain_send, chain_recv, late_sems, halo_sems,
):
    ages = grads_ref.shape[-1]
    count = lax.axis_size("age")
    halo = blocks // stations
    here, other, below, above, prior, following = place()
    turb, age, span = here
    late = grad_rows - early
    span_rows = early + 2 * late
    has_below = age > 0
    has_above = age < count - 1

    def part(column, dest, start, number):
        owner = column * count + dest
        return pl.ds(pl.multiple_of(owner * grad_rows + start, 8), number)

    def mate_copy(dest):
        return pltpu.make_async_remote_copy(
            src_ref=grads_ref.at[part(1 - turb, dest, 0, early)],
            dst_ref=from_mate.at[dest],
            send_sem=mate_sems.at[0, dest],
            recv_sem=mate_sems.at[1, dest],
            device_id=other,
            device_id_type=MESH,
        )

    def chain_copy(dest, upward):
        return pltpu.make_async_remote_copy(
            src_ref=work.at[dest],
            dst_ref=(from_below if upward else from_above).at[dest],
            send_sem=chain_send.at[dest],
            recv_sem=chain_recv.at[0 if upward else 1, dest],
            device_id=above if upward else below,
            device_id_type=MESH,
        )

    greet(count)
    for distance in range(count - 1, -1, -1):
        for sign in (1, -1) if distance else (1,):
            dest = age + sign * distance

            @pl.when(dest < count if sign > 0 else dest >= 0)
            def _(dest=dest):
                mate_copy(dest).start()

    def fill(dest):
        mate_copy(dest).wait_recv()
        work[dest, pl.ds(0, early), :] = (
            grads_ref[part(turb, dest, 0, early), :] + from_mate[dest]
        )
        work[dest, pl.ds(early, late), :] = grads_ref[part(turb, dest, early, late), :]
        work[dest, pl.ds(early + late, late), :] = grads_ref[part(1 - turb, dest, early, late), :]

    def add_below(dest):
        chain_copy(dest, True).wait_recv()
        work[dest] = work[dest] + from_below[dest]

    def add_above(dest):
        chain_copy(dest, False).wait_recv()
        work[dest] = work[dest] + from_above[dest]

    for distance in range(count - 1, 0, -1):
        up = age + distance
        down = age - distance

        @pl.when(up < count)
        def _(dest=up):
            fill(dest)
            pl.when(has_below)(lambda: add_below(dest))
            chain_copy(dest, True).start()

        @pl.when(down >= 0)
        def _(dest=down):
            fill(dest)
            pl.when(has_above)(lambda: add_above(dest))
            chain_copy(dest, False).start()

    fill(age)
    pl.when(has_below)(lambda: add_below(age))
    pl.when(has_above)(lambda: add_above(age))
    late_buf[...] = work[age, pl.ds(early + late, late), :]
    late_copy = pltpu.make_async_remote_copy(
        src_ref=late_buf,
        dst_ref=late_in,
        send_sem=late_sems.at[0],
        recv_sem=late_sems.at[1],
        device_id=other,
        device_id_type=MESH,
    )
    late_copy.start()
    advected_ref[...] = positions_ref[...] + time_step * sums_ref[pl.ds(0, 3 * blocks), :]
    advected_ref[pl.ds(0, blocks), :] = advected_ref[pl.ds(0, blocks), :] + time_step
    positions_grad_ref[...] = (
        seed_ref[...] + sums_ref[pl.ds(3 * blocks, 3 * blocks), :] + work[age, pl.ds(0, 3 * blocks), :]
    )
    late_copy.wait_recv()
    work[age, pl.ds(early, late), :] = work[age, pl.ds(early, late), :] + late_in[...]
    halo_out[...] = work[age, pl.ds(5 * blocks, grad_rows - 5 * blocks), :]
    halo_copy = pltpu.make_async_remote_copy(
        src_ref=halo_out,
        dst_ref=halo_in,
        send_sem=halo_sems.at[0],
        recv_sem=halo_sems.at[1],
        device_id=following,
        device_id_type=MESH,
    )
    halo_copy.start()
    trail, shed = keeps(stations, ages, (blocks, ages))
    strengths_grad_ref[pl.ds(0, blocks), :] = work[age, pl.ds(3 * blocks, blocks), :] * trail
    strengths_grad_ref[pl.ds(blocks, blocks), :] = work[age, pl.ds(4 * blocks, blocks), :] * shed
    halo_copy.wait_recv()
    for k in range(3 * halo):
        at = pl.ds(k * stations, 1)
        positions_grad_ref[at, :] = positions_grad_ref[at, :] + halo_in[pl.ds(k, 1), :]
    late_copy.wait_send()
    halo_copy.wait_send()
    for dest in range(count):
        mate_copy(dest).wait_send()
        pl.when(dest > age)(lambda dest=dest: chain_copy(dest, True).wait_send())
        pl.when(dest < age)(lambda dest=dest: chain_copy(dest, False).wait_send())


def local_dense(positions, strengths, core_radius, adjoint_seed, pair_target, pair_owner, pair_source):
    shape_here = positions.shape
    stations = shape_here[3]
    ages = shape_here[4]
    blocks = shape_here[1] * shape_here[2] * stations
    halo = blocks // stations
    count = lax.axis_size("age")
    group = lax.axis_size("turb") * count
    pairs = pair_target.shape[-1]
    per_owner = -(-(6 * blocks + 3 * halo) // 8) * 8
    grad_rows = -(-(5 * blocks + 3 * halo) // 8) * 8
    early = grad_rows * 5 // 6 // 8 * 8
    late = grad_rows - early
    target_ids = pair_target.reshape(pairs)
    owner_ids = pair_owner.reshape(pairs)
    source_ids = pair_source.reshape(pairs)
    me = lax.axis_index("turb") * count + lax.axis_index("age")
    vmem = pl.BlockSpec(memory_space=pltpu.VMEM)
    limit = 40 * 1024 * 1024
    dma = pltpu.SemaphoreType.DMA
    rows = positions.reshape(3 * blocks, ages)
    table = pl.pallas_call(
        functools.partial(gather_kernel, blocks, stations, per_owner),
        out_shape=jax.ShapeDtypeStruct((group * per_owner, ages), jnp.float32),
        in_specs=[vmem] * 3,
        out_specs=vmem,
        scratch_shapes=[
            pltpu.VMEM((per_owner - 6 * blocks, ages), jnp.float32),
            dma((2,)),
            dma((3, 2, group)),
            dma((2, group)),
        ],
        compiler_params=pltpu.CompilerParams(
            collective_id=0, has_side_effects=True, vmem_limit_bytes=limit
        ),
    )(rows, strengths.reshape(2 * blocks, ages), core_radius.reshape(blocks, ages))
    station = source_ids % stations
    inner = station < stations - 1
    base = owner_ids * per_owner
    index = jnp.stack(
        [
            base + source_ids,
            (owner_ids + 1) % group * per_owner + source_ids,
            base + jnp.where(inner, source_ids + 1, 6 * blocks + source_ids // stations),
            jnp.where(inner, blocks, halo),
            me * per_owner + target_ids,
            target_ids,
            (owner_ids * blocks + source_ids + 1) * SRC_ROWS,
            target_ids,
        ]
    )
    seeds = adjoint_seed.reshape(3 * blocks, ages)
    grads, sums = pl.pallas_call(
        functools.partial(pairs_kernel, group, blocks, stations, per_owner, grad_rows),
        out_shape=(
            jax.ShapeDtypeStruct((group * grad_rows, ages), jnp.float32),
            jax.ShapeDtypeStruct((6 * blocks, ages), jnp.float32),
        ),
        in_specs=[pl.BlockSpec(memory_space=pltpu.SMEM), vmem, vmem],
        out_specs=(vmem, vmem),
        scratch_shapes=[
            pltpu.VMEM((18 * TILE, ages), jnp.float32),
            pltpu.VMEM((pairs * SRC_ROWS, ages), jnp.float32),
            pltpu.VMEM((pairs * TGT_ROWS, ages), jnp.float32),
            pltpu.VMEM(((group * blocks + 1) * SRC_ROWS, ages), jnp.float32),
            pltpu.VMEM((blocks * TGT_ROWS, ages), jnp.float32),
        ],
        compiler_params=pltpu.CompilerParams(vmem_limit_bytes=limit),
    )(index, table, seeds)
    extra = grad_rows - 5 * blocks
    advected, grad_positions, grad_strengths = pl.pallas_call(
        functools.partial(reduce_kernel, blocks, stations, grad_rows, early),
        out_shape=(
            jax.ShapeDtypeStruct((3 * blocks, ages), jnp.float32),
            jax.ShapeDtypeStruct((3 * blocks, ages), jnp.float32),
            jax.ShapeDtypeStruct((2 * blocks, ages), jnp.float32),
        ),
        in_specs=[vmem] * 4,
        out_specs=(vmem, vmem, vmem),
        scratch_shapes=[
            pltpu.VMEM((count, early + 2 * late, ages), jnp.float32),
            pltpu.VMEM((count, early, ages), jnp.float32),
            pltpu.VMEM((count, early + 2 * late, ages), jnp.float32),
            pltpu.VMEM((count, early + 2 * late, ages), jnp.float32),
            pltpu.VMEM((late, ages), jnp.float32),
            pltpu.VMEM((late, ages), jnp.float32),
            pltpu.VMEM((extra, ages), jnp.float32),
            pltpu.VMEM((extra, ages), jnp.float32),
            dma((2, count)),
            dma((count,)),
            dma((2, count)),
            dma((2,)),
            dma((2,)),
        ],
        compiler_params=pltpu.CompilerParams(
            collective_id=1, has_side_effects=True, vmem_limit_bytes=limit
        ),
    )(grads, sums, rows, seeds)
    return (
        advected.reshape(shape_here),
        grad_positions.reshape(shape_here),
        grad_strengths.reshape(strengths.shape),
    )


def local(positions, strengths, core_radius, adjoint_seed, pair_target, pair_owner, pair_source):
    blocks = positions.shape[1] * positions.shape[2] * positions.shape[3]
    group = lax.axis_size("turb") * lax.axis_size("age")
    fits = lax.axis_size("turb") == 2 and lax.axis_size("span") > 2 and lax.axis_size("age") > 1
    dense = fits and group * blocks <= 8 * pair_target.shape[-1]
    chosen = local_dense if dense else local_sparse
    return chosen(
        positions, strengths, core_radius, adjoint_seed, pair_target, pair_owner, pair_source
    )


def solution(mesh):
    placed = (
        P(None, "turb", None, "span", "age"),
        P(None, "turb", None, "span", "age"),
        P("turb", None, "span", "age"),
        P(None, "turb", None, "span", "age"),
        P("turb", "age", "span", None),
        P("turb", "age", "span", None),
        P("turb", "age", "span", None),
    )
    return jax.shard_map(
        local,
        mesh=mesh,
        in_specs=placed,
        out_specs=(
            P(None, "turb", None, "span", "age"),
            P(None, "turb", None, "span", "age"),
            P(None, "turb", None, "span", "age"),
        ),
        check_vma=False,
    )
```

```python
import functools
import math

import jax
import jax.numpy as jnp
from jax import lax
from jax.experimental import pallas as pl
from jax.experimental.pallas import tpu as pltpu
from jax.sharding import PartitionSpec as P

REACH = 8


time_step = 0.5
four_pi = 4.0 * math.pi
batch_rows = 16


def shifted_2(value, axis, steps):
    count = lax.axis_size(axis)
    leading, last = (max(0, -steps), min(count, count - steps))
    return lax.ppermute(value, axis, [(source, source + steps) for source in range(leading, last)])


def windows(payload):
    age_count = payload.shape[-1]
    padded = jnp.pad(payload, ((0, 0), (0, 0), (REACH, REACH)))
    stacked = jnp.stack(
        [
            padded[:, :, REACH + offset : REACH + offset + age_count]
            for offset in range(-REACH, REACH)
        ]
    )
    shifted = (
        jnp.arange(-REACH, REACH, dtype=jnp.int32)[:, None]
        + jnp.arange(age_count, dtype=jnp.int32)[None, :]
    )
    inside = ((shifted >= 0) & (shifted < age_count)).astype(payload.dtype)
    return (stacked, inside)


def induced(targets, payload):
    stacked, inside = windows(payload)
    begins = stacked[:, :, 0:3]
    end_points = jnp.stack([stacked[:, :, 3:6], stacked[:, :, 6:9]])
    gammas = jnp.stack([stacked[:, :, 9], stacked[:, :, 10]]) * inside[None, :, None, :]
    core = jnp.where(inside[:, None, :] > 0, stacked[:, :, 11], 1.0)
    core_sq = core * core
    core_quad = core_sq * core_sq
    from_begin = targets[None] - begins
    from_end = targets[None, None] - end_points
    along = end_points - begins[None]
    near = from_begin[None]
    cross_x = near[..., 1, :] * from_end[..., 2, :] - near[..., 2, :] * from_end[..., 1, :]
    cross_y = near[..., 2, :] * from_end[..., 0, :] - near[..., 0, :] * from_end[..., 2, :]
    cross_z = near[..., 0, :] * from_end[..., 1, :] - near[..., 1, :] * from_end[..., 0, :]
    cross_sq = cross_x * cross_x + cross_y * cross_y + cross_z * cross_z
    length_sq = jnp.sum(along * along, axis=-2) + core_sq
    dist_begin = jnp.sqrt(jnp.sum(from_begin * from_begin, axis=-2) + core_sq)
    dist_end = jnp.sqrt(jnp.sum(from_end * from_end, axis=-2) + core_sq)
    projected = jnp.sum(
        along * (near / dist_begin[None, :, :, None, :] - from_end / dist_end[..., None, :]),
        axis=-2,
    )
    factor = (
        gammas
        * projected
        / (four_pi * jnp.sqrt(cross_sq * cross_sq + core_quad * length_sq * length_sq))
    )
    return jnp.stack(
        [
            jnp.sum(cross_x * factor, axis=(0, 1)),
            jnp.sum(cross_y * factor, axis=(0, 1)),
            jnp.sum(cross_z * factor, axis=(0, 1)),
        ],
        axis=1,
    )


def run_pairs(targets, payload, cotangent):
    number = targets.shape[0]
    age_count = targets.shape[-1]

    def one_batch(operands):
        velocity, pullback = jax.vjp(induced, operands[0], operands[1])
        grad_targets, grad_payload = pullback(operands[2])
        return (velocity, grad_targets, grad_payload)

    shaped = (
        targets.reshape(number // batch_rows, batch_rows, 3, age_count),
        payload.reshape(number // batch_rows, batch_rows, 12, age_count),
        cotangent.reshape(number // batch_rows, batch_rows, 3, age_count),
    )
    velocity, grad_targets, grad_payload = lax.map(one_batch, shaped)
    return (
        velocity.reshape(number, 3, age_count),
        grad_targets.reshape(number, 3, age_count),
        grad_payload.reshape(number, 12, age_count),
    )


def onehot_sum(indices, rows, values):
    selector = (jnp.arange(rows, dtype=jnp.int32)[:, None] == indices[None, :]).astype(jnp.float32)
    flat = values.reshape(values.shape[0], -1)
    summed = jnp.dot(
        selector, flat, precision=lax.Precision.HIGHEST, preferred_element_type=jnp.float32
    )
    return summed.reshape((rows,) + values.shape[1:])


def local_sparse(positions, strengths, core_radius, adjoint_seed, pair_target, pair_owner, pair_source):
    shape_here = positions.shape
    station_here = shape_here[3]
    age_here = shape_here[4]
    blocks_here = shape_here[1] * shape_here[2] * station_here
    group_size = lax.axis_size("turb") * lax.axis_size("age")
    pair_count = pair_target.shape[-1]
    capacity = 2 * pair_count // group_size
    target_ids = pair_target.reshape(pair_count)
    owner_ids = pair_owner.reshape(pair_count)
    source_ids = pair_source.reshape(pair_count)
    next_ages = shifted_2(positions[..., 0], "age", -1)
    next_stations = shifted_2(positions[:, :, :, 0, :], "span", -1)
    age_keep = (
        lax.axis_index("age") * age_here + jnp.arange(age_here, dtype=jnp.int32)
        < age_here * lax.axis_size("age") - 1
    ).astype(jnp.float32)
    station_keep = (
        lax.axis_index("span") * station_here + jnp.arange(station_here, dtype=jnp.int32)
        < station_here * lax.axis_size("span") - 1
    ).astype(jnp.float32)

    def build(nodes, after_age, after_station, circulation):
        trail_end = jnp.concatenate([nodes[..., 1:], after_age[..., None]], axis=-1)
        shed_end = jnp.concatenate([nodes[:, :, :, 1:, :], after_station[:, :, :, None, :]], axis=3)
        trail_gamma = circulation[0] * age_keep
        shed_gamma = circulation[1] * station_keep[:, None]
        stacked = jnp.concatenate(
            [nodes, trail_end, shed_end, trail_gamma[None], shed_gamma[None], core_radius[None]],
            axis=0,
        )
        return jnp.transpose(stacked.reshape(12, blocks_here, age_here), (1, 0, 2))

    payload, build_pullback = jax.vjp(build, positions, next_ages, next_stations, strengths)

    def to_rows(array):
        return jnp.transpose(array.reshape(array.shape[0], blocks_here, age_here), (1, 0, 2))

    def from_rows(array):
        return jnp.transpose(array, (1, 0, 2)).reshape(shape_here)

    target_blocks = to_rows(positions)
    seed_blocks = to_rows(adjoint_seed) * time_step
    owner_onehot = (owner_ids[:, None] == jnp.arange(group_size, dtype=jnp.int32)[None, :]).astype(
        jnp.int32
    )
    rank_within = jnp.sum((jnp.cumsum(owner_onehot, axis=0) - owner_onehot) * owner_onehot, axis=1)
    slot_index = owner_ids * capacity + rank_within
    request = (
        jnp.zeros((group_size * capacity,), jnp.int32)
        .at[slot_index]
        .set(source_ids)
        .reshape(group_size, capacity)
    )
    asked = lax.all_to_all(
        request, ("turb", "age"), split_axis=0, concat_axis=0, tiled=True
    ).reshape(group_size * capacity)
    pair_targets = target_blocks[target_ids]
    pair_seed = seed_blocks[target_ids]
    outgoing = (
        jnp.zeros((group_size * capacity, 6, age_here), jnp.float32)
        .at[slot_index]
        .set(jnp.concatenate([pair_targets, pair_seed], axis=1))
    )
    incoming = lax.all_to_all(
        outgoing.reshape(group_size, capacity, 6, age_here),
        ("turb", "age"),
        split_axis=0,
        concat_axis=0,
        tiled=True,
    )
    incoming = incoming.reshape(group_size * capacity, 6, age_here)
    slot_velocity, slot_grad, payload_terms = run_pairs(
        incoming[:, 0:3], payload[asked], incoming[:, 3:6]
    )
    results = jnp.concatenate([slot_velocity, slot_grad], axis=1).reshape(
        group_size, capacity, 6, age_here
    )
    answered = lax.all_to_all(
        results, ("turb", "age"), split_axis=0, concat_axis=0, tiled=True
    ).reshape(group_size * capacity, 6, age_here)[slot_index]
    pair_velocity = answered[:, 0:3]
    pair_grad = answered[:, 3:6]
    payload_grad = onehot_sum(asked, blocks_here, payload_terms)
    velocity = onehot_sum(target_ids, blocks_here, pair_velocity)
    target_grad = onehot_sum(target_ids, blocks_here, pair_grad)
    advected = positions + time_step * from_rows(velocity)
    advected = advected.at[0].add(time_step)
    grad_nodes, grad_after_age, grad_after_station, grad_strengths = build_pullback(payload_grad)
    from_prior_age = shifted_2(grad_after_age, "age", 1)
    from_prior_station = shifted_2(grad_after_station, "span", 1)
    grad_positions = adjoint_seed + grad_nodes + from_rows(target_grad)
    grad_positions = grad_positions.at[..., 0].add(from_prior_age)
    grad_positions = grad_positions.at[:, :, :, 0, :].add(from_prior_station)
    return (advected, grad_positions, grad_strengths)


TILE = 8
SRC_ROWS = 16
TGT_ROWS = 8


def cross(a, b):
    return (
        a[1] * b[2] - a[2] * b[1],
        a[2] * b[0] - a[0] * b[2],
        a[0] * b[1] - a[1] * b[0],
    )


def dot(a, b):
    return a[0] * b[0] + a[1] * b[1] + a[2] * b[2]


def segment(r0, r1, r2, inv1, cube1, gamma, core_sq, quad, quart, inside, w):
    c = cross(r0, r1)
    c_sq = dot(c, c)
    a = dot(r0, r1)
    b = dot(r0, r2)
    inv2 = lax.rsqrt(dot(r2, r2) + core_sq)
    proj = a * inv1 - b * inv2
    inv_d = lax.rsqrt(c_sq * c_sq + quart)
    inv_d = jnp.where(inside, inv_d, 0.0)
    q = dot(w, c)
    m = gamma * inv_d
    k = m * proj
    gp = m * q
    fd = (k * q) * (inv_d * inv_d)
    grad_gamma = proj * (q * inv_d)
    h = 2.0 * fd * c_sq
    gn2 = gp * b * (inv2 * inv2 * inv2)
    alpha = gp * (inv1 - inv2) - gn2
    beta = gn2 - gp * a * cube1
    delta = 2.0 * (gp * inv2 - fd * quad) + gn2
    gc = tuple(k * w[i] - h * c[i] for i in range(3))
    left = cross(gc, r0)
    right = cross(r1, gc)
    grad_r1 = tuple(left[i] + alpha * r0[i] + beta * r1[i] for i in range(3))
    grad_r0 = tuple(right[i] + alpha * r1[i] + delta * r0[i] for i in range(3))
    velocity = tuple(k * c[i] for i in range(3))
    return velocity, grad_r1, grad_r0, grad_gamma


def pair_tile(rows, ages):
    lane = lax.broadcasted_iota(jnp.int32, (TILE, ages), 1)
    begin = rows[0:3]
    core = rows[5]
    core_sq = core * core
    trail = [
        jnp.where(
            lane == ages - 1,
            pltpu.roll(rows[6 + i], ages - 1, 1),
            pltpu.roll(begin[i], ages - 1, 1),
        )
        for i in range(3)
    ]
    alongs = [[trail[i] - begin[i] for i in range(3)], [rows[9 + i] - begin[i] for i in range(3)]]
    gammas = [rows[3] * (1.0 / four_pi), rows[4] * (1.0 / four_pi)]
    core_quad = core_sq * core_sq
    lengths = [dot(r0, r0) + core_sq for r0 in alongs]
    quads = [core_quad * length for length in lengths]
    quarts = [quad * length for quad, length in zip(quads, lengths)]
    zero = jnp.zeros((TILE, ages), jnp.float32)
    sum_r1 = [zero] * 3
    sum_r0 = [[zero] * 3, [zero] * 3]
    sum_gamma = [zero, zero]
    out = [zero] * 6
    for offset in range(-REACH, REACH):
        shift = offset % ages
        moved = [pltpu.roll(x, shift, 1) if shift else x for x in rows[12:18]]
        target, w = moved[0:3], moved[3:6]
        if offset >= 0:
            inside = lane >= offset
        else:
            inside = lane < ages + offset
        r1 = [target[i] - begin[i] for i in range(3)]
        inv1 = lax.rsqrt(dot(r1, r1) + core_sq)
        cube1 = inv1 * inv1 * inv1
        vel = [None] * 3
        g1 = [None] * 3
        for kind in range(2):
            r0 = alongs[kind]
            r2 = [r1[i] - r0[i] for i in range(3)]
            v, d1, d0, dg = segment(
                r0, r1, r2, inv1, cube1, gammas[kind], core_sq,
                quads[kind], quarts[kind], inside, w,
            )
            vel = [v[i] if kind == 0 else vel[i] + v[i] for i in range(3)]
            g1 = [d1[i] if kind == 0 else g1[i] + d1[i] for i in range(3)]
            sum_r0[kind] = [sum_r0[kind][i] + d0[i] for i in range(3)]
            sum_gamma[kind] = sum_gamma[kind] + dg
        sum_r1 = [sum_r1[i] + g1[i] for i in range(3)]
        back = (-offset) % ages
        both = vel + g1
        out = [out[i] + (pltpu.roll(both[i], back, 1) if back else both[i]) for i in range(6)]
    grad_begin = [-(sum_r1[i] + sum_r0[0][i] + sum_r0[1][i]) for i in range(3)]
    grad_source = grad_begin + sum_r0[0] + sum_r0[1] + [g * (1.0 / four_pi) for g in sum_gamma]
    return grad_source, out


def pairs_kernel(
    group, blocks, stations, per_owner, grad_rows, target_ref, owner_ref, source_ref, table_ref,
    seed_ref, grad_ref, advected_ref, base_ref, rows_buf, src_buf, tgt_buf, acc, tgt_acc,
):
    pairs = target_ref.shape[0]
    me = lax.axis_index("turb") * lax.axis_size("age") + lax.axis_index("age")
    own_rows = me * per_owner
    ages = table_ref.shape[-1]
    halo = blocks // stations
    acc[...] = jnp.zeros_like(acc)
    tgt_acc[...] = jnp.zeros_like(tgt_acc)

    def tile(t, _):
        for j in range(TILE):
            p = t * TILE + j
            tgt = target_ref[p]
            owner = owner_ref[p]
            block = source_ref[p]
            src = owner * per_owner + block
            nxt = jnp.where(owner == group - 1, 0, owner + 1) * per_owner + block
            inner = lax.rem(block, stations) < stations - 1
            shed = jnp.where(inner, src + 1, owner * per_owner + 6 * blocks + lax.div(block, stations))
            shed_step = jnp.where(inner, blocks, halo)
            own = own_rows + tgt
            for r in range(6):
                rows_buf[pl.ds(r * TILE + j, 1), :] = table_ref[pl.ds(src + r * blocks, 1), :]
            for r in range(3):
                rows_buf[pl.ds((6 + r) * TILE + j, 1), :] = table_ref[pl.ds(nxt + r * blocks, 1), :]
                rows_buf[pl.ds((9 + r) * TILE + j, 1), :] = table_ref[pl.ds(shed + r * shed_step, 1), :]
                rows_buf[pl.ds((12 + r) * TILE + j, 1), :] = table_ref[pl.ds(own + r * blocks, 1), :]
                rows_buf[pl.ds((15 + r) * TILE + j, 1), :] = seed_ref[pl.ds(tgt + r * blocks, 1), :] * time_step
        rows = [rows_buf[pl.ds(r * TILE, TILE), :] for r in range(18)]
        grad_source, out = pair_tile(rows, ages)
        for r in range(11):
            src_buf[pl.ds(t * (TILE * SRC_ROWS) + r, TILE, stride=SRC_ROWS), :] = grad_source[r]
        for r in range(6):
            tgt_buf[pl.ds(t * (TILE * TGT_ROWS) + r, TILE, stride=TGT_ROWS), :] = out[r]
        return 0

    lax.fori_loop(0, pairs // TILE, tile, 0)

    def scatter(p, _):
        at = pl.ds(
            pl.multiple_of((owner_ref[p] * blocks + source_ref[p] + 1) * SRC_ROWS, SRC_ROWS), SRC_ROWS
        )
        acc[at, :] += src_buf[pl.ds(pl.multiple_of(p * SRC_ROWS, SRC_ROWS), SRC_ROWS), :]
        at = pl.ds(pl.multiple_of(target_ref[p] * TGT_ROWS, TGT_ROWS), TGT_ROWS)
        tgt_acc[at, :] += tgt_buf[pl.ds(pl.multiple_of(p * TGT_ROWS, TGT_ROWS), TGT_ROWS), :]
        return 0

    lax.fori_loop(0, pairs, scatter, 0, unroll=8)

    for c in range(3):
        for q in range(0, blocks, 8):
            at = pl.ds(c * blocks + q, 8)
            velocity = tgt_acc[pl.ds(q * TGT_ROWS + c, 8, stride=TGT_ROWS), :]
            here = table_ref[pl.ds(pl.multiple_of(own_rows + c * blocks + q, 8), 8), :]
            advected_ref[at, :] = here + time_step * (velocity + 1.0 if c == 0 else velocity)
            base_ref[at, :] = seed_ref[at, :] + tgt_acc[pl.ds(q * TGT_ROWS + 3 + c, 8, stride=TGT_ROWS), :]

    lane = lax.broadcasted_iota(jnp.int32, (TILE, ages), 1)
    sub = lax.broadcasted_iota(jnp.int32, (TILE, ages), 0)

    def fold(o, _):
        prev = lax.rem(o + group - 1, group)

        def rows_of(owner, q, r):
            return acc[pl.ds((owner * blocks + q + 1) * SRC_ROWS + r, 8, stride=SRC_ROWS), :]

        base = o * grad_rows
        for q in range(0, blocks, 8):
            for c in range(3):
                trail = jnp.where(lane == ages - 1, rows_of(prev, q, 3 + c), rows_of(o, q, 3 + c))
                shed = rows_of(o, q - 1, 6 + c)
                if q % stations == 0:
                    shed = jnp.where(sub == 0, 0.0, shed)
                grad_ref[pl.ds(base + c * blocks + q, 8), :] = (
                    rows_of(o, q, c) + pltpu.roll(trail, 1, 1) + shed
                )
            for c in range(2):
                grad_ref[pl.ds(base + (3 + c) * blocks + q, 8), :] = rows_of(o, q, 9 + c)
        for c in range(3):
            for h in range(halo):
                row = (o * blocks + h * stations + stations) * SRC_ROWS + 6 + c
                grad_ref[pl.ds(base + 5 * blocks + c * halo + h, 1), :] = acc[pl.ds(row, 1), :]
        grad_ref[pl.ds(base + 5 * blocks + 3 * halo, grad_rows - 5 * blocks - 3 * halo), :] = (
            jnp.zeros((grad_rows - 5 * blocks - 3 * halo, ages), jnp.float32)
        )
        return 0

    lax.fori_loop(0, group, fold, 0)


MESH = pl.DeviceIdType.MESH


def place():
    here = (lax.axis_index("turb"), lax.axis_index("age"), lax.axis_index("span"))
    spans = lax.axis_size("span")
    turb, age, span = here
    return (
        here,
        (1 - turb, age, span),
        (turb, age - 1, span),
        (turb, age + 1, span),
        (turb, age, lax.rem(span + spans - 1, spans)),
        (turb, age, lax.rem(span + 1, spans)),
    )


def greet(ages_count):
    here, other, below, above, prior, following = place()
    barrier = pltpu.get_barrier_semaphore()
    for device in (other, prior, following):
        pl.semaphore_signal(barrier, inc=1, device_id=device, device_id_type=MESH)

    @pl.when(here[1] > 0)
    def _():
        pl.semaphore_signal(barrier, inc=1, device_id=below, device_id_type=MESH)

    @pl.when(here[1] < ages_count - 1)
    def _():
        pl.semaphore_signal(barrier, inc=1, device_id=above, device_id_type=MESH)

    inner = (here[1] > 0).astype(jnp.int32) + (here[1] < ages_count - 1).astype(jnp.int32)
    pl.semaphore_wait(barrier, 3 + inner)


def keeps(stations, ages, shape):
    lane = lax.broadcasted_iota(jnp.int32, shape, 1)
    row = lax.broadcasted_iota(jnp.int32, shape, 0)
    last_age = lax.axis_index("age") == lax.axis_size("age") - 1
    last_station = lax.axis_index("span") == lax.axis_size("span") - 1
    trail = jnp.where(jnp.logical_and(last_age, lane == ages - 1), 0.0, 1.0)
    shed = jnp.where(jnp.logical_and(last_station, row % stations == stations - 1), 0.0, 1.0)
    return trail, shed


def gather_kernel(
    blocks, stations, per_owner, positions_ref, strengths_ref, core_ref, table_ref,
    strengths_buf, halo_buf, load_sems, halo_sems, send_sems, recv_sems,
):
    ages = table_ref.shape[-1]
    count = lax.axis_size("age")
    halo = blocks // stations
    here, other, below, above, prior, following = place()
    turb, age, span = here
    me = turb * count + age
    mate = (1 - turb) * count + age
    extra = per_owner - 6 * blocks
    parts = (
        (0, 3 * blocks),
        (3 * blocks, 2 * blocks),
        (5 * blocks, per_owner - 5 * blocks),
    )
    base = me * per_owner
    loads = [
        pltpu.make_async_copy(source, target, load_sems.at[k])
        for k, (source, target) in enumerate(
            (
                (positions_ref, table_ref.at[pl.ds(pl.multiple_of(base, 8), 3 * blocks)]),
                (strengths_ref, strengths_buf),
                (core_ref, table_ref.at[pl.ds(pl.multiple_of(base + 5 * blocks, 8), blocks)]),
            )
        )
    ]
    for load in loads:
        load.start()
    halo_buf[...] = jnp.zeros_like(halo_buf)
    trail, shed = keeps(stations, ages, (blocks, ages))
    greet(count)

    def rows(owner, part):
        return pl.ds(pl.multiple_of(owner * per_owner + parts[part][0], 8), parts[part][1])

    def copy(owner, part, way):
        at = rows(owner, part)
        return pltpu.make_async_remote_copy(
            src_ref=table_ref.at[at],
            dst_ref=table_ref.at[at],
            send_sem=send_sems.at[way, part, owner],
            recv_sem=recv_sems.at[part, owner],
            device_id=(other, below, above)[way],
            device_id_type=MESH,
        )

    def arrive(owner, part):
        copy(owner, part, 0).wait_recv()

    has_below = age > 0
    has_above = age < count - 1

    def share(owner, part):
        @pl.when(has_below)
        def _():
            copy(owner, part, 1).start()

        @pl.when(has_above)
        def _():
            copy(owner, part, 2).start()

    loads[0].wait()
    share(me, 0)
    copy(me, 0, 0).start()
    for k in range(3 * halo):
        halo_buf[pl.ds(k, 1), :] = table_ref[pl.ds(base + k * stations, 1), :]
    halo_copy = pltpu.make_async_remote_copy(
        src_ref=halo_buf,
        dst_ref=table_ref.at[pl.ds(pl.multiple_of(base + 6 * blocks, 8), extra)],
        send_sem=halo_sems.at[0],
        recv_sem=halo_sems.at[1],
        device_id=prior,
        device_id_type=MESH,
    )
    halo_copy.start()
    loads[1].wait()
    table_ref[pl.ds(pl.multiple_of(base + 3 * blocks, 8), blocks), :] = (
        strengths_buf[pl.ds(0, blocks), :] * trail
    )
    table_ref[pl.ds(pl.multiple_of(base + 4 * blocks, 8), blocks), :] = (
        strengths_buf[pl.ds(blocks, blocks), :] * shed
    )
    share(me, 1)
    copy(me, 1, 0).start()
    loads[2].wait()
    halo_copy.wait_recv()
    copy(me, 2, 0).start()
    share(me, 2)
    arrive(mate, 2)
    share(mate, 2)
    for step in range(1, count):
        for part in range(3):
            for way, sign in ((2, -1), (1, 1)):
                source = age + sign * step
                onward = has_above if way == 2 else has_below

                @pl.when(source >= 0 if sign < 0 else source < count)
                def _(source=source, way=way, onward=onward, part=part):
                    for column in (turb, 1 - turb)[: 2 if part == 2 else 1]:
                        owner = column * count + source
                        arrive(owner, part)

                        @pl.when(onward)
                        def _(owner=owner):
                            copy(owner, part, way).start()

                        if part < 2:
                            copy(owner, part, 0).start()

    for source in range(count):
        for part in range(2):
            arrive((1 - turb) * count + source, part)
    halo_copy.wait_send()
    copy(me, 2, 0).wait_send()
    for source in range(count):
        sent = [(turb * count + source, part) for part in range(3)]
        sent.append(((1 - turb) * count + source, 2))
        for part in range(2):
            copy(sent[part][0], part, 0).wait_send()

        @pl.when(jnp.logical_and(source >= age, has_below))
        def _(sent=sent):
            for owner, part in sent:
                copy(owner, part, 1).wait_send()

        @pl.when(jnp.logical_and(source <= age, has_above))
        def _(sent=sent):
            for owner, part in sent:
                copy(owner, part, 2).wait_send()


def reduce_kernel(
    blocks, stations, grad_rows, early, grads_ref, base_ref, positions_grad_ref, strengths_grad_ref,
    work, from_mate, from_below, from_above, late_in, halo_out, halo_in,
    mate_sems, chain_send, chain_recv, late_sems, halo_sems,
):
    ages = grads_ref.shape[-1]
    count = lax.axis_size("age")
    halo = blocks // stations
    here, other, below, above, prior, following = place()
    turb, age, span = here
    late = grad_rows - early
    half = (early + 2 * late) // 16 * 8
    cut = half - 2 * late
    pieces = ((0, cut), (cut, early - cut))
    spans = ((0, half), (half, early + 2 * late - half))
    has_below = age > 0
    has_above = age < count - 1

    def part(column, dest, start, number):
        owner = column * count + dest
        return pl.ds(pl.multiple_of(owner * grad_rows + start, 8), number)

    def mate_copy(dest, piece):
        return pltpu.make_async_remote_copy(
            src_ref=grads_ref.at[part(1 - turb, dest, *pieces[piece])],
            dst_ref=from_mate.at[dest, pl.ds(*pieces[piece])],
            send_sem=mate_sems.at[0, dest, piece],
            recv_sem=mate_sems.at[1, dest, piece],
            device_id=other,
            device_id_type=MESH,
        )

    def chain_copy(dest, piece, upward):
        at = pl.ds(*spans[piece])
        return pltpu.make_async_remote_copy(
            src_ref=work.at[dest, at],
            dst_ref=(from_below if upward else from_above).at[dest, at],
            send_sem=chain_send.at[dest, piece],
            recv_sem=chain_recv.at[0 if upward else 1, dest, piece],
            device_id=above if upward else below,
            device_id_type=MESH,
        )

    order = [jnp.int32(0)] * count
    rank = jnp.int32(0)
    for distance in range(count - 1, -1, -1):
        for sign in (1, -1) if distance else (1,):
            dest = age + sign * distance
            valid = jnp.logical_and(dest >= 0, dest < count)
            order = [
                jnp.where(jnp.logical_and(valid, rank == k), dest, order[k]) for k in range(count)
            ]
            rank = rank + valid.astype(jnp.int32)
    steps = [(order[k], piece) for k in range(count) for piece in range(2)]

    greet(count)
    mate_copy(*steps[0]).start()

    def take(number):
        dest, piece = steps[number]
        mate_copy(dest, piece).wait_recv()
        if number + 1 < len(steps):
            mate_copy(*steps[number + 1]).start()
        start, size = pieces[piece]
        if piece == 0:
            work[dest, pl.ds(0, late), :] = grads_ref[part(turb, dest, early, late), :]
            work[dest, pl.ds(late, late), :] = grads_ref[part(1 - turb, dest, early, late), :]
        work[dest, pl.ds(2 * late + start, size), :] = (
            grads_ref[part(turb, dest, start, size), :] + from_mate[dest, pl.ds(start, size), :]
        )
        at = pl.ds(*spans[piece])

        @pl.when(jnp.logical_and(dest >= age, has_below))
        def _():
            chain_copy(dest, piece, True).wait_recv()
            work[dest, at, :] = work[dest, at, :] + from_below[dest, at, :]

        @pl.when(jnp.logical_and(dest <= age, has_above))
        def _():
            chain_copy(dest, piece, False).wait_recv()
            work[dest, at, :] = work[dest, at, :] + from_above[dest, at, :]

        pl.when(dest > age)(lambda: chain_copy(dest, piece, True).start())
        pl.when(dest < age)(lambda: chain_copy(dest, piece, False).start())

    for number in range(len(steps) - 1):
        take(number)
    late_copy = pltpu.make_async_remote_copy(
        src_ref=work.at[age, pl.ds(late, late)],
        dst_ref=late_in,
        send_sem=late_sems.at[0],
        recv_sem=late_sems.at[1],
        device_id=other,
        device_id_type=MESH,
    )
    late_copy.start()
    late_copy.wait_recv()
    work[age, pl.ds(0, late), :] = work[age, pl.ds(0, late), :] + late_in[...]
    halo_out[...] = work[age, pl.ds(5 * blocks - early, grad_rows - 5 * blocks), :]
    halo_copy = pltpu.make_async_remote_copy(
        src_ref=halo_out,
        dst_ref=halo_in,
        send_sem=halo_sems.at[0],
        recv_sem=halo_sems.at[1],
        device_id=following,
        device_id_type=MESH,
    )
    halo_copy.start()
    trail, shed = keeps(stations, ages, (2 * blocks, ages))
    row = lax.broadcasted_iota(jnp.int32, (2 * blocks, ages), 0)
    keep = jnp.where(row < blocks, trail, shed)
    first = early - 3 * blocks
    strengths_grad_ref[pl.ds(first, 2 * blocks - first), :] = (
        work[age, pl.ds(0, 2 * blocks - first), :] * keep[first:]
    )
    take(len(steps) - 1)
    strengths_grad_ref[pl.ds(0, first), :] = (
        work[age, pl.ds(2 * late + 3 * blocks, first), :] * keep[:first]
    )
    positions_grad_ref[...] = base_ref[...] + work[age, pl.ds(2 * late, 3 * blocks), :]
    halo_copy.wait_recv()
    for k in range(3 * halo):
        at = pl.ds(k * stations, 1)
        positions_grad_ref[at, :] = positions_grad_ref[at, :] + halo_in[pl.ds(k, 1), :]
    late_copy.wait_send()
    halo_copy.wait_send()
    for dest in range(count):
        for piece in range(2):
            mate_copy(dest, piece).wait_send()
            pl.when(dest > age)(lambda d=dest, p=piece: chain_copy(d, p, True).wait_send())
            pl.when(dest < age)(lambda d=dest, p=piece: chain_copy(d, p, False).wait_send())


def local_dense(positions, strengths, core_radius, adjoint_seed, pair_target, pair_owner, pair_source):
    shape_here = positions.shape
    stations = shape_here[3]
    ages = shape_here[4]
    blocks = shape_here[1] * shape_here[2] * stations
    halo = blocks // stations
    count = lax.axis_size("age")
    group = lax.axis_size("turb") * count
    pairs = pair_target.shape[-1]
    per_owner = -(-(6 * blocks + 3 * halo) // 8) * 8
    grad_rows = -(-(5 * blocks + 3 * halo) // 8) * 8
    early = grad_rows * 5 // 6 // 8 * 8
    late = grad_rows - early
    vmem = pl.BlockSpec(memory_space=pltpu.VMEM)
    limit = 40 * 1024 * 1024
    dma = pltpu.SemaphoreType.DMA
    rows = positions.reshape(3 * blocks, ages)
    table = pl.pallas_call(
        functools.partial(gather_kernel, blocks, stations, per_owner),
        out_shape=jax.ShapeDtypeStruct((group * per_owner, ages), jnp.float32),
        in_specs=[pl.BlockSpec(memory_space=pl.ANY)] * 3,
        out_specs=vmem,
        scratch_shapes=[
            pltpu.VMEM((2 * blocks, ages), jnp.float32),
            pltpu.VMEM((per_owner - 6 * blocks, ages), jnp.float32),
            dma((3,)),
            dma((2,)),
            dma((3, 3, group)),
            dma((3, group)),
        ],
        compiler_params=pltpu.CompilerParams(
            collective_id=0, has_side_effects=True, vmem_limit_bytes=limit
        ),
    )(rows, strengths.reshape(2 * blocks, ages), core_radius.reshape(blocks, ages))
    seeds = adjoint_seed.reshape(3 * blocks, ages)
    smem = pl.BlockSpec(memory_space=pltpu.SMEM)
    rows_out = jax.ShapeDtypeStruct((3 * blocks, ages), jnp.float32)
    grads, advected, grad_base = pl.pallas_call(
        functools.partial(pairs_kernel, group, blocks, stations, per_owner, grad_rows),
        out_shape=(
            jax.ShapeDtypeStruct((group * grad_rows, ages), jnp.float32),
            rows_out,
            rows_out,
        ),
        in_specs=[smem, smem, smem, vmem, vmem],
        out_specs=(vmem, vmem, vmem),
        scratch_shapes=[
            pltpu.VMEM((18 * TILE, ages), jnp.float32),
            pltpu.VMEM((pairs * SRC_ROWS, ages), jnp.float32),
            pltpu.VMEM((pairs * TGT_ROWS, ages), jnp.float32),
            pltpu.VMEM(((group * blocks + 1) * SRC_ROWS, ages), jnp.float32),
            pltpu.VMEM((blocks * TGT_ROWS, ages), jnp.float32),
        ],
        compiler_params=pltpu.CompilerParams(vmem_limit_bytes=limit),
    )(
        pair_target.reshape(pairs),
        pair_owner.reshape(pairs),
        pair_source.reshape(pairs),
        table,
        seeds,
    )
    extra = grad_rows - 5 * blocks
    grad_positions, grad_strengths = pl.pallas_call(
        functools.partial(reduce_kernel, blocks, stations, grad_rows, early),
        out_shape=(rows_out, jax.ShapeDtypeStruct((2 * blocks, ages), jnp.float32)),
        in_specs=[vmem] * 2,
        out_specs=(vmem, vmem),
        scratch_shapes=[
            pltpu.VMEM((count, early + 2 * late, ages), jnp.float32),
            pltpu.VMEM((count, early, ages), jnp.float32),
            pltpu.VMEM((count, early + 2 * late, ages), jnp.float32),
            pltpu.VMEM((count, early + 2 * late, ages), jnp.float32),
            pltpu.VMEM((late, ages), jnp.float32),
            pltpu.VMEM((extra, ages), jnp.float32),
            pltpu.VMEM((extra, ages), jnp.float32),
            dma((2, count, 2)),
            dma((count, 2)),
            dma((2, count, 2)),
            dma((2,)),
            dma((2,)),
        ],
        compiler_params=pltpu.CompilerParams(
            collective_id=1, has_side_effects=True, vmem_limit_bytes=limit
        ),
    )(grads, grad_base)
    return (
        advected.reshape(shape_here),
        grad_positions.reshape(shape_here),
        grad_strengths.reshape(strengths.shape),
    )


def local(positions, strengths, core_radius, adjoint_seed, pair_target, pair_owner, pair_source):
    blocks = positions.shape[1] * positions.shape[2] * positions.shape[3]
    group = lax.axis_size("turb") * lax.axis_size("age")
    fits = lax.axis_size("turb") == 2 and lax.axis_size("span") > 2 and lax.axis_size("age") > 1
    dense = fits and group * blocks <= 8 * pair_target.shape[-1]
    chosen = local_dense if dense else local_sparse
    return chosen(
        positions, strengths, core_radius, adjoint_seed, pair_target, pair_owner, pair_source
    )


def solution(mesh):
    placed = (
        P(None, "turb", None, "span", "age"),
        P(None, "turb", None, "span", "age"),
        P("turb", None, "span", "age"),
        P(None, "turb", None, "span", "age"),
        P("turb", "age", "span", None),
        P("turb", "age", "span", None),
        P("turb", "age", "span", None),
    )
    return jax.shard_map(
        local,
        mesh=mesh,
        in_specs=placed,
        out_specs=(
            P(None, "turb", None, "span", "age"),
            P(None, "turb", None, "span", "age"),
            P(None, "turb", None, "span", "age"),
        ),
        check_vma=False,
    )
```

```python
import functools
import math

import jax
import jax.numpy as jnp
from jax import lax
from jax.experimental import pallas as pl
from jax.experimental.pallas import tpu as pltpu
from jax.sharding import PartitionSpec as P

REACH = 8


time_step = 0.5
four_pi = 4.0 * math.pi
batch_rows = 16


def shifted_2(value, axis, steps):
    count = lax.axis_size(axis)
    leading, last = (max(0, -steps), min(count, count - steps))
    return lax.ppermute(value, axis, [(source, source + steps) for source in range(leading, last)])


def windows(payload):
    age_count = payload.shape[-1]
    padded = jnp.pad(payload, ((0, 0), (0, 0), (REACH, REACH)))
    stacked = jnp.stack(
        [
            padded[:, :, REACH + offset : REACH + offset + age_count]
            for offset in range(-REACH, REACH)
        ]
    )
    shifted = (
        jnp.arange(-REACH, REACH, dtype=jnp.int32)[:, None]
        + jnp.arange(age_count, dtype=jnp.int32)[None, :]
    )
    inside = ((shifted >= 0) & (shifted < age_count)).astype(payload.dtype)
    return (stacked, inside)


def induced(targets, payload):
    stacked, inside = windows(payload)
    begins = stacked[:, :, 0:3]
    end_points = jnp.stack([stacked[:, :, 3:6], stacked[:, :, 6:9]])
    gammas = jnp.stack([stacked[:, :, 9], stacked[:, :, 10]]) * inside[None, :, None, :]
    core = jnp.where(inside[:, None, :] > 0, stacked[:, :, 11], 1.0)
    core_sq = core * core
    core_quad = core_sq * core_sq
    from_begin = targets[None] - begins
    from_end = targets[None, None] - end_points
    along = end_points - begins[None]
    near = from_begin[None]
    cross_x = near[..., 1, :] * from_end[..., 2, :] - near[..., 2, :] * from_end[..., 1, :]
    cross_y = near[..., 2, :] * from_end[..., 0, :] - near[..., 0, :] * from_end[..., 2, :]
    cross_z = near[..., 0, :] * from_end[..., 1, :] - near[..., 1, :] * from_end[..., 0, :]
    cross_sq = cross_x * cross_x + cross_y * cross_y + cross_z * cross_z
    length_sq = jnp.sum(along * along, axis=-2) + core_sq
    dist_begin = jnp.sqrt(jnp.sum(from_begin * from_begin, axis=-2) + core_sq)
    dist_end = jnp.sqrt(jnp.sum(from_end * from_end, axis=-2) + core_sq)
    projected = jnp.sum(
        along * (near / dist_begin[None, :, :, None, :] - from_end / dist_end[..., None, :]),
        axis=-2,
    )
    factor = (
        gammas
        * projected
        / (four_pi * jnp.sqrt(cross_sq * cross_sq + core_quad * length_sq * length_sq))
    )
    return jnp.stack(
        [
            jnp.sum(cross_x * factor, axis=(0, 1)),
            jnp.sum(cross_y * factor, axis=(0, 1)),
            jnp.sum(cross_z * factor, axis=(0, 1)),
        ],
        axis=1,
    )


def run_pairs(targets, payload, cotangent):
    number = targets.shape[0]
    age_count = targets.shape[-1]

    def one_batch(operands):
        velocity, pullback = jax.vjp(induced, operands[0], operands[1])
        grad_targets, grad_payload = pullback(operands[2])
        return (velocity, grad_targets, grad_payload)

    shaped = (
        targets.reshape(number // batch_rows, batch_rows, 3, age_count),
        payload.reshape(number // batch_rows, batch_rows, 12, age_count),
        cotangent.reshape(number // batch_rows, batch_rows, 3, age_count),
    )
    velocity, grad_targets, grad_payload = lax.map(one_batch, shaped)
    return (
        velocity.reshape(number, 3, age_count),
        grad_targets.reshape(number, 3, age_count),
        grad_payload.reshape(number, 12, age_count),
    )


def onehot_sum(indices, rows, values):
    selector = (jnp.arange(rows, dtype=jnp.int32)[:, None] == indices[None, :]).astype(jnp.float32)
    flat = values.reshape(values.shape[0], -1)
    summed = jnp.dot(
        selector, flat, precision=lax.Precision.HIGHEST, preferred_element_type=jnp.float32
    )
    return summed.reshape((rows,) + values.shape[1:])


def local_sparse(positions, strengths, core_radius, adjoint_seed, pair_target, pair_owner, pair_source):
    shape_here = positions.shape
    station_here = shape_here[3]
    age_here = shape_here[4]
    blocks_here = shape_here[1] * shape_here[2] * station_here
    group_size = lax.axis_size("turb") * lax.axis_size("age")
    pair_count = pair_target.shape[-1]
    capacity = 2 * pair_count // group_size
    target_ids = pair_target.reshape(pair_count)
    owner_ids = pair_owner.reshape(pair_count)
    source_ids = pair_source.reshape(pair_count)
    next_ages = shifted_2(positions[..., 0], "age", -1)
    next_stations = shifted_2(positions[:, :, :, 0, :], "span", -1)
    age_keep = (
        lax.axis_index("age") * age_here + jnp.arange(age_here, dtype=jnp.int32)
        < age_here * lax.axis_size("age") - 1
    ).astype(jnp.float32)
    station_keep = (
        lax.axis_index("span") * station_here + jnp.arange(station_here, dtype=jnp.int32)
        < station_here * lax.axis_size("span") - 1
    ).astype(jnp.float32)

    def build(nodes, after_age, after_station, circulation):
        trail_end = jnp.concatenate([nodes[..., 1:], after_age[..., None]], axis=-1)
        shed_end = jnp.concatenate([nodes[:, :, :, 1:, :], after_station[:, :, :, None, :]], axis=3)
        trail_gamma = circulation[0] * age_keep
        shed_gamma = circulation[1] * station_keep[:, None]
        stacked = jnp.concatenate(
            [nodes, trail_end, shed_end, trail_gamma[None], shed_gamma[None], core_radius[None]],
            axis=0,
        )
        return jnp.transpose(stacked.reshape(12, blocks_here, age_here), (1, 0, 2))

    payload, build_pullback = jax.vjp(build, positions, next_ages, next_stations, strengths)

    def to_rows(array):
        return jnp.transpose(array.reshape(array.shape[0], blocks_here, age_here), (1, 0, 2))

    def from_rows(array):
        return jnp.transpose(array, (1, 0, 2)).reshape(shape_here)

    target_blocks = to_rows(positions)
    seed_blocks = to_rows(adjoint_seed) * time_step
    owner_onehot = (owner_ids[:, None] == jnp.arange(group_size, dtype=jnp.int32)[None, :]).astype(
        jnp.int32
    )
    rank_within = jnp.sum((jnp.cumsum(owner_onehot, axis=0) - owner_onehot) * owner_onehot, axis=1)
    slot_index = owner_ids * capacity + rank_within
    request = (
        jnp.zeros((group_size * capacity,), jnp.int32)
        .at[slot_index]
        .set(source_ids)
        .reshape(group_size, capacity)
    )
    asked = lax.all_to_all(
        request, ("turb", "age"), split_axis=0, concat_axis=0, tiled=True
    ).reshape(group_size * capacity)
    pair_targets = target_blocks[target_ids]
    pair_seed = seed_blocks[target_ids]
    outgoing = (
        jnp.zeros((group_size * capacity, 6, age_here), jnp.float32)
        .at[slot_index]
        .set(jnp.concatenate([pair_targets, pair_seed], axis=1))
    )
    incoming = lax.all_to_all(
        outgoing.reshape(group_size, capacity, 6, age_here),
        ("turb", "age"),
        split_axis=0,
        concat_axis=0,
        tiled=True,
    )
    incoming = incoming.reshape(group_size * capacity, 6, age_here)
    slot_velocity, slot_grad, payload_terms = run_pairs(
        incoming[:, 0:3], payload[asked], incoming[:, 3:6]
    )
    results = jnp.concatenate([slot_velocity, slot_grad], axis=1).reshape(
        group_size, capacity, 6, age_here
    )
    answered = lax.all_to_all(
        results, ("turb", "age"), split_axis=0, concat_axis=0, tiled=True
    ).reshape(group_size * capacity, 6, age_here)[slot_index]
    pair_velocity = answered[:, 0:3]
    pair_grad = answered[:, 3:6]
    payload_grad = onehot_sum(asked, blocks_here, payload_terms)
    velocity = onehot_sum(target_ids, blocks_here, pair_velocity)
    target_grad = onehot_sum(target_ids, blocks_here, pair_grad)
    advected = positions + time_step * from_rows(velocity)
    advected = advected.at[0].add(time_step)
    grad_nodes, grad_after_age, grad_after_station, grad_strengths = build_pullback(payload_grad)
    from_prior_age = shifted_2(grad_after_age, "age", 1)
    from_prior_station = shifted_2(grad_after_station, "span", 1)
    grad_positions = adjoint_seed + grad_nodes + from_rows(target_grad)
    grad_positions = grad_positions.at[..., 0].add(from_prior_age)
    grad_positions = grad_positions.at[:, :, :, 0, :].add(from_prior_station)
    return (advected, grad_positions, grad_strengths)


TILE = 8
SRC_ROWS = 16
TGT_ROWS = 8


def cross(a, b):
    return (
        a[1] * b[2] - a[2] * b[1],
        a[2] * b[0] - a[0] * b[2],
        a[0] * b[1] - a[1] * b[0],
    )


def dot(a, b):
    return a[0] * b[0] + a[1] * b[1] + a[2] * b[2]


def segment(r0, r1, r2, inv1, cube1, gamma, core_sq, quad, quart, inside, w):
    c = cross(r0, r1)
    c_sq = dot(c, c)
    a = dot(r0, r1)
    b = dot(r0, r2)
    inv2 = lax.rsqrt(dot(r2, r2) + core_sq)
    proj = a * inv1 - b * inv2
    inv_d = lax.rsqrt(c_sq * c_sq + quart)
    inv_d = jnp.where(inside, inv_d, 0.0)
    q = dot(w, c)
    m = gamma * inv_d
    k = m * proj
    gp = m * q
    fd = (k * q) * (inv_d * inv_d)
    grad_gamma = proj * (q * inv_d)
    h = 2.0 * fd * c_sq
    gn2 = gp * b * (inv2 * inv2 * inv2)
    alpha = gp * (inv1 - inv2) - gn2
    beta = gn2 - gp * a * cube1
    delta = 2.0 * (gp * inv2 - fd * quad) + gn2
    gc = tuple(k * w[i] - h * c[i] for i in range(3))
    left = cross(gc, r0)
    right = cross(r1, gc)
    grad_r1 = tuple(left[i] + alpha * r0[i] + beta * r1[i] for i in range(3))
    grad_r0 = tuple(right[i] + alpha * r1[i] + delta * r0[i] for i in range(3))
    velocity = tuple(k * c[i] for i in range(3))
    return velocity, grad_r1, grad_r0, grad_gamma


def pair_tile(rows, ages):
    lane = lax.broadcasted_iota(jnp.int32, (TILE, ages), 1)
    begin = rows[0:3]
    core = rows[5]
    core_sq = core * core
    trail = [
        jnp.where(
            lane == ages - 1,
            pltpu.roll(rows[6 + i], ages - 1, 1),
            pltpu.roll(begin[i], ages - 1, 1),
        )
        for i in range(3)
    ]
    alongs = [[trail[i] - begin[i] for i in range(3)], [rows[9 + i] - begin[i] for i in range(3)]]
    gammas = [rows[3] * (1.0 / four_pi), rows[4] * (1.0 / four_pi)]
    core_quad = core_sq * core_sq
    lengths = [dot(r0, r0) + core_sq for r0 in alongs]
    quads = [core_quad * length for length in lengths]
    quarts = [quad * length for quad, length in zip(quads, lengths)]
    zero = jnp.zeros((TILE, ages), jnp.float32)
    sum_r1 = [zero] * 3
    sum_r0 = [[zero] * 3, [zero] * 3]
    sum_gamma = [zero, zero]
    out = [zero] * 6
    for offset in range(-REACH, REACH):
        shift = offset % ages
        moved = [pltpu.roll(x, shift, 1) if shift else x for x in rows[12:18]]
        target, w = moved[0:3], moved[3:6]
        if offset >= 0:
            inside = lane >= offset
        else:
            inside = lane < ages + offset
        r1 = [target[i] - begin[i] for i in range(3)]
        inv1 = lax.rsqrt(dot(r1, r1) + core_sq)
        cube1 = inv1 * inv1 * inv1
        vel = [None] * 3
        g1 = [None] * 3
        for kind in range(2):
            r0 = alongs[kind]
            r2 = [r1[i] - r0[i] for i in range(3)]
            v, d1, d0, dg = segment(
                r0, r1, r2, inv1, cube1, gammas[kind], core_sq,
                quads[kind], quarts[kind], inside, w,
            )
            vel = [v[i] if kind == 0 else vel[i] + v[i] for i in range(3)]
            g1 = [d1[i] if kind == 0 else g1[i] + d1[i] for i in range(3)]
            sum_r0[kind] = [sum_r0[kind][i] + d0[i] for i in range(3)]
            sum_gamma[kind] = sum_gamma[kind] + dg
        sum_r1 = [sum_r1[i] + g1[i] for i in range(3)]
        back = (-offset) % ages
        both = vel + g1
        out = [out[i] + (pltpu.roll(both[i], back, 1) if back else both[i]) for i in range(6)]
    grad_begin = [-(sum_r1[i] + sum_r0[0][i] + sum_r0[1][i]) for i in range(3)]
    grad_source = grad_begin + sum_r0[0] + sum_r0[1] + [g * (1.0 / four_pi) for g in sum_gamma]
    return grad_source, out


def pairs_kernel(
    group, blocks, stations, per_owner, grad_rows, target_ref, owner_ref, source_ref, table_ref,
    seed_ref, grad_ref, advected_ref, base_ref, rows_buf, src_buf, tgt_buf, acc, tgt_acc,
):
    pairs = target_ref.shape[0]
    me = lax.axis_index("turb") * lax.axis_size("age") + lax.axis_index("age")
    own_rows = me * per_owner
    ages = table_ref.shape[-1]
    halo = blocks // stations
    acc[...] = jnp.zeros_like(acc)
    tgt_acc[...] = jnp.zeros_like(tgt_acc)

    def tile(t, _):
        for j in range(TILE):
            p = t * TILE + j
            tgt = target_ref[p]
            owner = owner_ref[p]
            block = source_ref[p]
            src = owner * per_owner + block
            nxt = jnp.where(owner == group - 1, 0, owner + 1) * per_owner + block
            inner = lax.rem(block, stations) < stations - 1
            shed = jnp.where(inner, src + 1, owner * per_owner + 6 * blocks + lax.div(block, stations))
            shed_step = jnp.where(inner, blocks, halo)
            own = own_rows + tgt
            for r in range(6):
                rows_buf[pl.ds(r * TILE + j, 1), :] = table_ref[pl.ds(src + r * blocks, 1), :]
            for r in range(3):
                rows_buf[pl.ds((6 + r) * TILE + j, 1), :] = table_ref[pl.ds(nxt + r * blocks, 1), :]
                rows_buf[pl.ds((9 + r) * TILE + j, 1), :] = table_ref[pl.ds(shed + r * shed_step, 1), :]
                rows_buf[pl.ds((12 + r) * TILE + j, 1), :] = table_ref[pl.ds(own + r * blocks, 1), :]
                rows_buf[pl.ds((15 + r) * TILE + j, 1), :] = seed_ref[pl.ds(tgt + r * blocks, 1), :] * time_step
        rows = [rows_buf[pl.ds(r * TILE, TILE), :] for r in range(18)]
        grad_source, out = pair_tile(rows, ages)
        for r in range(11):
            src_buf[pl.ds(t * (TILE * SRC_ROWS) + r, TILE, stride=SRC_ROWS), :] = grad_source[r]
        for r in range(6):
            tgt_buf[pl.ds(t * (TILE * TGT_ROWS) + r, TILE, stride=TGT_ROWS), :] = out[r]
        return 0

    lax.fori_loop(0, pairs // TILE, tile, 0)

    def scatter(p, _):
        at = pl.ds(
            pl.multiple_of((owner_ref[p] * blocks + source_ref[p] + 1) * SRC_ROWS, SRC_ROWS), SRC_ROWS
        )
        acc[at, :] += src_buf[pl.ds(pl.multiple_of(p * SRC_ROWS, SRC_ROWS), SRC_ROWS), :]
        at = pl.ds(pl.multiple_of(target_ref[p] * TGT_ROWS, TGT_ROWS), TGT_ROWS)
        tgt_acc[at, :] += tgt_buf[pl.ds(pl.multiple_of(p * TGT_ROWS, TGT_ROWS), TGT_ROWS), :]
        return 0

    lax.fori_loop(0, pairs, scatter, 0, unroll=8)

    for c in range(3):
        for q in range(0, blocks, 8):
            at = pl.ds(c * blocks + q, 8)
            velocity = tgt_acc[pl.ds(q * TGT_ROWS + c, 8, stride=TGT_ROWS), :]
            here = table_ref[pl.ds(pl.multiple_of(own_rows + c * blocks + q, 8), 8), :]
            advected_ref[at, :] = here + time_step * (velocity + 1.0 if c == 0 else velocity)
            base_ref[at, :] = seed_ref[at, :] + tgt_acc[pl.ds(q * TGT_ROWS + 3 + c, 8, stride=TGT_ROWS), :]

    lane = lax.broadcasted_iota(jnp.int32, (TILE, ages), 1)
    sub = lax.broadcasted_iota(jnp.int32, (TILE, ages), 0)

    def fold(o, _):
        prev = lax.rem(o + group - 1, group)

        def rows_of(owner, q, r):
            return acc[pl.ds((owner * blocks + q + 1) * SRC_ROWS + r, 8, stride=SRC_ROWS), :]

        base = o * grad_rows
        for q in range(0, blocks, 8):
            for c in range(3):
                trail = jnp.where(lane == ages - 1, rows_of(prev, q, 3 + c), rows_of(o, q, 3 + c))
                shed = rows_of(o, q - 1, 6 + c)
                if q % stations == 0:
                    shed = jnp.where(sub == 0, 0.0, shed)
                grad_ref[pl.ds(base + c * blocks + q, 8), :] = (
                    rows_of(o, q, c) + pltpu.roll(trail, 1, 1) + shed
                )
            for c in range(2):
                grad_ref[pl.ds(base + (3 + c) * blocks + q, 8), :] = rows_of(o, q, 9 + c)
        for c in range(3):
            for h in range(halo):
                row = (o * blocks + h * stations + stations) * SRC_ROWS + 6 + c
                grad_ref[pl.ds(base + 5 * blocks + c * halo + h, 1), :] = acc[pl.ds(row, 1), :]
        grad_ref[pl.ds(base + 5 * blocks + 3 * halo, grad_rows - 5 * blocks - 3 * halo), :] = (
            jnp.zeros((grad_rows - 5 * blocks - 3 * halo, ages), jnp.float32)
        )
        return 0

    lax.fori_loop(0, group, fold, 0)


MESH = pl.DeviceIdType.MESH


def place():
    here = (lax.axis_index("turb"), lax.axis_index("age"), lax.axis_index("span"))
    spans = lax.axis_size("span")
    turb, age, span = here
    return (
        here,
        (1 - turb, age, span),
        (turb, age - 1, span),
        (turb, age + 1, span),
        (turb, age, lax.rem(span + spans - 1, spans)),
        (turb, age, lax.rem(span + 1, spans)),
    )


def greet(ages_count):
    here, other, below, above, prior, following = place()
    barrier = pltpu.get_barrier_semaphore()
    for device in (other, prior, following):
        pl.semaphore_signal(barrier, inc=1, device_id=device, device_id_type=MESH)

    @pl.when(here[1] > 0)
    def _():
        pl.semaphore_signal(barrier, inc=1, device_id=below, device_id_type=MESH)

    @pl.when(here[1] < ages_count - 1)
    def _():
        pl.semaphore_signal(barrier, inc=1, device_id=above, device_id_type=MESH)

    inner = (here[1] > 0).astype(jnp.int32) + (here[1] < ages_count - 1).astype(jnp.int32)
    pl.semaphore_wait(barrier, 3 + inner)


def keeps(stations, ages, shape):
    lane = lax.broadcasted_iota(jnp.int32, shape, 1)
    row = lax.broadcasted_iota(jnp.int32, shape, 0)
    last_age = lax.axis_index("age") == lax.axis_size("age") - 1
    last_station = lax.axis_index("span") == lax.axis_size("span") - 1
    trail = jnp.where(jnp.logical_and(last_age, lane == ages - 1), 0.0, 1.0)
    shed = jnp.where(jnp.logical_and(last_station, row % stations == stations - 1), 0.0, 1.0)
    return trail, shed


def gather_kernel(
    blocks, stations, per_owner, positions_ref, strengths_ref, core_ref, table_ref,
    strengths_buf, halo_buf, load_sems, halo_sems, send_sems, recv_sems,
):
    ages = table_ref.shape[-1]
    count = lax.axis_size("age")
    halo = blocks // stations
    here, other, below, above, prior, following = place()
    turb, age, span = here
    me = turb * count + age
    mate = (1 - turb) * count + age
    extra = per_owner - 6 * blocks
    parts = (
        (0, 3 * blocks),
        (3 * blocks, 2 * blocks),
        (5 * blocks, per_owner - 5 * blocks),
    )
    base = me * per_owner
    loads = [
        pltpu.make_async_copy(source, target, load_sems.at[k])
        for k, (source, target) in enumerate(
            (
                (positions_ref, table_ref.at[pl.ds(pl.multiple_of(base, 8), 3 * blocks)]),
                (strengths_ref, strengths_buf),
                (core_ref, table_ref.at[pl.ds(pl.multiple_of(base + 5 * blocks, 8), blocks)]),
            )
        )
    ]
    for load in loads:
        load.start()
    halo_buf[...] = jnp.zeros_like(halo_buf)
    trail, shed = keeps(stations, ages, (blocks, ages))
    greet(count)

    def rows(owner, part):
        return pl.ds(pl.multiple_of(owner * per_owner + parts[part][0], 8), parts[part][1])

    def copy(owner, part, way):
        at = rows(owner, part)
        return pltpu.make_async_remote_copy(
            src_ref=table_ref.at[at],
            dst_ref=table_ref.at[at],
            send_sem=send_sems.at[way, part, owner],
            recv_sem=recv_sems.at[part, owner],
            device_id=(other, below, above)[way],
            device_id_type=MESH,
        )

    def arrive(owner, part):
        copy(owner, part, 0).wait_recv()

    has_below = age > 0
    has_above = age < count - 1

    def share(owner, part):
        @pl.when(has_below)
        def _():
            copy(owner, part, 1).start()

        @pl.when(has_above)
        def _():
            copy(owner, part, 2).start()

    loads[0].wait()
    share(me, 0)
    copy(me, 0, 0).start()
    for k in range(3 * halo):
        halo_buf[pl.ds(k, 1), :] = table_ref[pl.ds(base + k * stations, 1), :]
    halo_copy = pltpu.make_async_remote_copy(
        src_ref=halo_buf,
        dst_ref=table_ref.at[pl.ds(pl.multiple_of(base + 6 * blocks, 8), extra)],
        send_sem=halo_sems.at[0],
        recv_sem=halo_sems.at[1],
        device_id=prior,
        device_id_type=MESH,
    )
    halo_copy.start()
    loads[1].wait()
    table_ref[pl.ds(pl.multiple_of(base + 3 * blocks, 8), blocks), :] = (
        strengths_buf[pl.ds(0, blocks), :] * trail
    )
    table_ref[pl.ds(pl.multiple_of(base + 4 * blocks, 8), blocks), :] = (
        strengths_buf[pl.ds(blocks, blocks), :] * shed
    )
    share(me, 1)
    copy(me, 1, 0).start()
    loads[2].wait()
    halo_copy.wait_recv()
    copy(me, 2, 0).start()
    share(me, 2)
    arrive(mate, 2)
    share(mate, 2)
    for step in range(1, count):
        for part in range(3):
            for way, sign in ((2, -1), (1, 1)):
                source = age + sign * step
                onward = has_above if way == 2 else has_below

                @pl.when(source >= 0 if sign < 0 else source < count)
                def _(source=source, way=way, onward=onward, part=part):
                    for column in (turb, 1 - turb)[: 2 if part == 2 else 1]:
                        owner = column * count + source
                        arrive(owner, part)

                        @pl.when(onward)
                        def _(owner=owner):
                            copy(owner, part, way).start()

                        if part < 2:
                            copy(owner, part, 0).start()

    for source in range(count):
        for part in range(2):
            arrive((1 - turb) * count + source, part)
    halo_copy.wait_send()
    copy(me, 2, 0).wait_send()
    for source in range(count):
        sent = [(turb * count + source, part) for part in range(3)]
        sent.append(((1 - turb) * count + source, 2))
        for part in range(2):
            copy(sent[part][0], part, 0).wait_send()

        @pl.when(jnp.logical_and(source >= age, has_below))
        def _(sent=sent):
            for owner, part in sent:
                copy(owner, part, 1).wait_send()

        @pl.when(jnp.logical_and(source <= age, has_above))
        def _(sent=sent):
            for owner, part in sent:
                copy(owner, part, 2).wait_send()


def reduce_kernel(
    blocks, stations, grad_rows, early, grads_ref, base_ref, positions_grad_ref, strengths_grad_ref,
    work, from_mate, from_below, from_above, late_in, halo_out, halo_in,
    mate_sems, chain_send, chain_recv, late_sems, halo_sems,
):
    ages = grads_ref.shape[-1]
    count = lax.axis_size("age")
    halo = blocks // stations
    here, other, below, above, prior, following = place()
    turb, age, span = here
    late = grad_rows - early
    half = (early + 2 * late) // 16 * 8
    cut = half - 2 * late
    pieces = ((0, cut), (cut, early - cut))
    spans = ((0, half), (half, early + 2 * late - half))
    has_below = age > 0
    has_above = age < count - 1

    def part(column, dest, start, number):
        owner = column * count + dest
        return pl.ds(pl.multiple_of(owner * grad_rows + start, 8), number)

    def mate_copy(dest, piece):
        return pltpu.make_async_remote_copy(
            src_ref=grads_ref.at[part(1 - turb, dest, *pieces[piece])],
            dst_ref=from_mate.at[dest, pl.ds(*pieces[piece])],
            send_sem=mate_sems.at[0, dest, piece],
            recv_sem=mate_sems.at[1, dest, piece],
            device_id=other,
            device_id_type=MESH,
        )

    def chain_copy(dest, piece, upward):
        at = pl.ds(*spans[piece])
        return pltpu.make_async_remote_copy(
            src_ref=work.at[dest, at],
            dst_ref=(from_below if upward else from_above).at[dest, at],
            send_sem=chain_send.at[dest, piece],
            recv_sem=chain_recv.at[0 if upward else 1, dest, piece],
            device_id=above if upward else below,
            device_id_type=MESH,
        )

    order = [jnp.int32(0)] * count
    rank = jnp.int32(0)
    for distance in range(count - 1, -1, -1):
        for sign in (1, -1) if distance else (1,):
            dest = age + sign * distance
            valid = jnp.logical_and(dest >= 0, dest < count)
            order = [
                jnp.where(jnp.logical_and(valid, rank == k), dest, order[k]) for k in range(count)
            ]
            rank = rank + valid.astype(jnp.int32)
    steps = [(order[k], piece) for k in range(count) for piece in range(2)]

    greet(count)
    mate_copy(*steps[0]).start()
    mate_copy(*steps[1]).start()

    def take(number):
        dest, piece = steps[number]
        mate_copy(dest, piece).wait_recv()
        if number + 2 < len(steps):
            mate_copy(*steps[number + 2]).start()
        start, size = pieces[piece]
        if piece == 0:
            work[dest, pl.ds(0, late), :] = grads_ref[part(turb, dest, early, late), :]
            work[dest, pl.ds(late, late), :] = grads_ref[part(1 - turb, dest, early, late), :]
        work[dest, pl.ds(2 * late + start, size), :] = (
            grads_ref[part(turb, dest, start, size), :] + from_mate[dest, pl.ds(start, size), :]
        )
        at = pl.ds(*spans[piece])

        @pl.when(jnp.logical_and(dest >= age, has_below))
        def _():
            chain_copy(dest, piece, True).wait_recv()
            work[dest, at, :] = work[dest, at, :] + from_below[dest, at, :]

        @pl.when(jnp.logical_and(dest <= age, has_above))
        def _():
            chain_copy(dest, piece, False).wait_recv()
            work[dest, at, :] = work[dest, at, :] + from_above[dest, at, :]

        pl.when(dest > age)(lambda: chain_copy(dest, piece, True).start())
        pl.when(dest < age)(lambda: chain_copy(dest, piece, False).start())

    for number in range(len(steps) - 1):
        take(number)
    late_copy = pltpu.make_async_remote_copy(
        src_ref=work.at[age, pl.ds(late, late)],
        dst_ref=late_in,
        send_sem=late_sems.at[0],
        recv_sem=late_sems.at[1],
        device_id=other,
        device_id_type=MESH,
    )
    late_copy.start()
    late_copy.wait_recv()
    work[age, pl.ds(0, late), :] = work[age, pl.ds(0, late), :] + late_in[...]
    halo_out[...] = work[age, pl.ds(5 * blocks - early, grad_rows - 5 * blocks), :]
    halo_copy = pltpu.make_async_remote_copy(
        src_ref=halo_out,
        dst_ref=halo_in,
        send_sem=halo_sems.at[0],
        recv_sem=halo_sems.at[1],
        device_id=following,
        device_id_type=MESH,
    )
    halo_copy.start()
    trail, shed = keeps(stations, ages, (2 * blocks, ages))
    row = lax.broadcasted_iota(jnp.int32, (2 * blocks, ages), 0)
    keep = jnp.where(row < blocks, trail, shed)
    first = early - 3 * blocks
    strengths_grad_ref[pl.ds(first, 2 * blocks - first), :] = (
        work[age, pl.ds(0, 2 * blocks - first), :] * keep[first:]
    )
    take(len(steps) - 1)
    strengths_grad_ref[pl.ds(0, first), :] = (
        work[age, pl.ds(2 * late + 3 * blocks, first), :] * keep[:first]
    )
    positions_grad_ref[...] = base_ref[...] + work[age, pl.ds(2 * late, 3 * blocks), :]
    halo_copy.wait_recv()
    for k in range(3 * halo):
        at = pl.ds(k * stations, 1)
        positions_grad_ref[at, :] = positions_grad_ref[at, :] + halo_in[pl.ds(k, 1), :]
    late_copy.wait_send()
    halo_copy.wait_send()
    for dest in range(count):
        for piece in range(2):
            mate_copy(dest, piece).wait_send()
            pl.when(dest > age)(lambda d=dest, p=piece: chain_copy(d, p, True).wait_send())
            pl.when(dest < age)(lambda d=dest, p=piece: chain_copy(d, p, False).wait_send())


def local_dense(positions, strengths, core_radius, adjoint_seed, pair_target, pair_owner, pair_source):
    shape_here = positions.shape
    stations = shape_here[3]
    ages = shape_here[4]
    blocks = shape_here[1] * shape_here[2] * stations
    halo = blocks // stations
    count = lax.axis_size("age")
    group = lax.axis_size("turb") * count
    pairs = pair_target.shape[-1]
    per_owner = -(-(6 * blocks + 3 * halo) // 8) * 8
    grad_rows = -(-(5 * blocks + 3 * halo) // 8) * 8
    early = grad_rows * 5 // 6 // 8 * 8
    late = grad_rows - early
    vmem = pl.BlockSpec(memory_space=pltpu.VMEM)
    limit = 40 * 1024 * 1024
    dma = pltpu.SemaphoreType.DMA
    rows = positions.reshape(3 * blocks, ages)
    table = pl.pallas_call(
        functools.partial(gather_kernel, blocks, stations, per_owner),
        out_shape=jax.ShapeDtypeStruct((group * per_owner, ages), jnp.float32),
        in_specs=[pl.BlockSpec(memory_space=pl.ANY)] * 3,
        out_specs=vmem,
        scratch_shapes=[
            pltpu.VMEM((2 * blocks, ages), jnp.float32),
            pltpu.VMEM((per_owner - 6 * blocks, ages), jnp.float32),
            dma((3,)),
            dma((2,)),
            dma((3, 3, group)),
            dma((3, group)),
        ],
        compiler_params=pltpu.CompilerParams(
            collective_id=0, has_side_effects=True, vmem_limit_bytes=limit
        ),
    )(rows, strengths.reshape(2 * blocks, ages), core_radius.reshape(blocks, ages))
    seeds = adjoint_seed.reshape(3 * blocks, ages)
    smem = pl.BlockSpec(memory_space=pltpu.SMEM)
    rows_out = jax.ShapeDtypeStruct((3 * blocks, ages), jnp.float32)
    grads, advected, grad_base = pl.pallas_call(
        functools.partial(pairs_kernel, group, blocks, stations, per_owner, grad_rows),
        out_shape=(
            jax.ShapeDtypeStruct((group * grad_rows, ages), jnp.float32),
            rows_out,
            rows_out,
        ),
        in_specs=[smem, smem, smem, vmem, vmem],
        out_specs=(vmem, vmem, vmem),
        scratch_shapes=[
            pltpu.VMEM((18 * TILE, ages), jnp.float32),
            pltpu.VMEM((pairs * SRC_ROWS, ages), jnp.float32),
            pltpu.VMEM((pairs * TGT_ROWS, ages), jnp.float32),
            pltpu.VMEM(((group * blocks + 1) * SRC_ROWS, ages), jnp.float32),
            pltpu.VMEM((blocks * TGT_ROWS, ages), jnp.float32),
        ],
        compiler_params=pltpu.CompilerParams(vmem_limit_bytes=limit),
    )(
        pair_target.reshape(pairs),
        pair_owner.reshape(pairs),
        pair_source.reshape(pairs),
        table,
        seeds,
    )
    extra = grad_rows - 5 * blocks
    grad_positions, grad_strengths = pl.pallas_call(
        functools.partial(reduce_kernel, blocks, stations, grad_rows, early),
        out_shape=(rows_out, jax.ShapeDtypeStruct((2 * blocks, ages), jnp.float32)),
        in_specs=[vmem] * 2,
        out_specs=(vmem, vmem),
        scratch_shapes=[
            pltpu.VMEM((count, early + 2 * late, ages), jnp.float32),
            pltpu.VMEM((count, early, ages), jnp.float32),
            pltpu.VMEM((count, early + 2 * late, ages), jnp.float32),
            pltpu.VMEM((count, early + 2 * late, ages), jnp.float32),
            pltpu.VMEM((late, ages), jnp.float32),
            pltpu.VMEM((extra, ages), jnp.float32),
            pltpu.VMEM((extra, ages), jnp.float32),
            dma((2, count, 2)),
            dma((count, 2)),
            dma((2, count, 2)),
            dma((2,)),
            dma((2,)),
        ],
        compiler_params=pltpu.CompilerParams(
            collective_id=1, has_side_effects=True, vmem_limit_bytes=limit
        ),
    )(grads, grad_base)
    return (
        advected.reshape(shape_here),
        grad_positions.reshape(shape_here),
        grad_strengths.reshape(strengths.shape),
    )


def local(positions, strengths, core_radius, adjoint_seed, pair_target, pair_owner, pair_source):
    blocks = positions.shape[1] * positions.shape[2] * positions.shape[3]
    group = lax.axis_size("turb") * lax.axis_size("age")
    fits = lax.axis_size("turb") == 2 and lax.axis_size("span") > 2 and lax.axis_size("age") > 1
    dense = fits and group * blocks <= 8 * pair_target.shape[-1]
    chosen = local_dense if dense else local_sparse
    return chosen(
        positions, strengths, core_radius, adjoint_seed, pair_target, pair_owner, pair_source
    )


def solution(mesh):
    placed = (
        P(None, "turb", None, "span", "age"),
        P(None, "turb", None, "span", "age"),
        P("turb", None, "span", "age"),
        P(None, "turb", None, "span", "age"),
        P("turb", "age", "span", None),
        P("turb", "age", "span", None),
        P("turb", "age", "span", None),
    )
    return jax.shard_map(
        local,
        mesh=mesh,
        in_specs=placed,
        out_specs=(
            P(None, "turb", None, "span", "age"),
            P(None, "turb", None, "span", "age"),
            P(None, "turb", None, "span", "age"),
        ),
        check_vma=False,
    )
```

```python
import functools
import math

import jax
import jax.numpy as jnp
from jax import lax
from jax.experimental import pallas as pl
from jax.experimental.pallas import tpu as pltpu
from jax.sharding import PartitionSpec as P

REACH = 8


time_step = 0.5
four_pi = 4.0 * math.pi
batch_rows = 16


def shifted_2(value, axis, steps):
    count = lax.axis_size(axis)
    leading, last = (max(0, -steps), min(count, count - steps))
    return lax.ppermute(value, axis, [(source, source + steps) for source in range(leading, last)])


def windows(payload):
    age_count = payload.shape[-1]
    padded = jnp.pad(payload, ((0, 0), (0, 0), (REACH, REACH)))
    stacked = jnp.stack(
        [
            padded[:, :, REACH + offset : REACH + offset + age_count]
            for offset in range(-REACH, REACH)
        ]
    )
    shifted = (
        jnp.arange(-REACH, REACH, dtype=jnp.int32)[:, None]
        + jnp.arange(age_count, dtype=jnp.int32)[None, :]
    )
    inside = ((shifted >= 0) & (shifted < age_count)).astype(payload.dtype)
    return (stacked, inside)


def induced(targets, payload):
    stacked, inside = windows(payload)
    begins = stacked[:, :, 0:3]
    end_points = jnp.stack([stacked[:, :, 3:6], stacked[:, :, 6:9]])
    gammas = jnp.stack([stacked[:, :, 9], stacked[:, :, 10]]) * inside[None, :, None, :]
    core = jnp.where(inside[:, None, :] > 0, stacked[:, :, 11], 1.0)
    core_sq = core * core
    core_quad = core_sq * core_sq
    from_begin = targets[None] - begins
    from_end = targets[None, None] - end_points
    along = end_points - begins[None]
    near = from_begin[None]
    cross_x = near[..., 1, :] * from_end[..., 2, :] - near[..., 2, :] * from_end[..., 1, :]
    cross_y = near[..., 2, :] * from_end[..., 0, :] - near[..., 0, :] * from_end[..., 2, :]
    cross_z = near[..., 0, :] * from_end[..., 1, :] - near[..., 1, :] * from_end[..., 0, :]
    cross_sq = cross_x * cross_x + cross_y * cross_y + cross_z * cross_z
    length_sq = jnp.sum(along * along, axis=-2) + core_sq
    dist_begin = jnp.sqrt(jnp.sum(from_begin * from_begin, axis=-2) + core_sq)
    dist_end = jnp.sqrt(jnp.sum(from_end * from_end, axis=-2) + core_sq)
    projected = jnp.sum(
        along * (near / dist_begin[None, :, :, None, :] - from_end / dist_end[..., None, :]),
        axis=-2,
    )
    factor = (
        gammas
        * projected
        / (four_pi * jnp.sqrt(cross_sq * cross_sq + core_quad * length_sq * length_sq))
    )
    return jnp.stack(
        [
            jnp.sum(cross_x * factor, axis=(0, 1)),
            jnp.sum(cross_y * factor, axis=(0, 1)),
            jnp.sum(cross_z * factor, axis=(0, 1)),
        ],
        axis=1,
    )


def run_pairs(targets, payload, cotangent):
    number = targets.shape[0]
    age_count = targets.shape[-1]

    def one_batch(operands):
        velocity, pullback = jax.vjp(induced, operands[0], operands[1])
        grad_targets, grad_payload = pullback(operands[2])
        return (velocity, grad_targets, grad_payload)

    shaped = (
        targets.reshape(number // batch_rows, batch_rows, 3, age_count),
        payload.reshape(number // batch_rows, batch_rows, 12, age_count),
        cotangent.reshape(number // batch_rows, batch_rows, 3, age_count),
    )
    velocity, grad_targets, grad_payload = lax.map(one_batch, shaped)
    return (
        velocity.reshape(number, 3, age_count),
        grad_targets.reshape(number, 3, age_count),
        grad_payload.reshape(number, 12, age_count),
    )


def onehot_sum(indices, rows, values):
    selector = (jnp.arange(rows, dtype=jnp.int32)[:, None] == indices[None, :]).astype(jnp.float32)
    flat = values.reshape(values.shape[0], -1)
    summed = jnp.dot(
        selector, flat, precision=lax.Precision.HIGHEST, preferred_element_type=jnp.float32
    )
    return summed.reshape((rows,) + values.shape[1:])


def local_sparse(positions, strengths, core_radius, adjoint_seed, pair_target, pair_owner, pair_source):
    shape_here = positions.shape
    station_here = shape_here[3]
    age_here = shape_here[4]
    blocks_here = shape_here[1] * shape_here[2] * station_here
    group_size = lax.axis_size("turb") * lax.axis_size("age")
    pair_count = pair_target.shape[-1]
    capacity = 2 * pair_count // group_size
    target_ids = pair_target.reshape(pair_count)
    owner_ids = pair_owner.reshape(pair_count)
    source_ids = pair_source.reshape(pair_count)
    next_ages = shifted_2(positions[..., 0], "age", -1)
    next_stations = shifted_2(positions[:, :, :, 0, :], "span", -1)
    age_keep = (
        lax.axis_index("age") * age_here + jnp.arange(age_here, dtype=jnp.int32)
        < age_here * lax.axis_size("age") - 1
    ).astype(jnp.float32)
    station_keep = (
        lax.axis_index("span") * station_here + jnp.arange(station_here, dtype=jnp.int32)
        < station_here * lax.axis_size("span") - 1
    ).astype(jnp.float32)

    def build(nodes, after_age, after_station, circulation):
        trail_end = jnp.concatenate([nodes[..., 1:], after_age[..., None]], axis=-1)
        shed_end = jnp.concatenate([nodes[:, :, :, 1:, :], after_station[:, :, :, None, :]], axis=3)
        trail_gamma = circulation[0] * age_keep
        shed_gamma = circulation[1] * station_keep[:, None]
        stacked = jnp.concatenate(
            [nodes, trail_end, shed_end, trail_gamma[None], shed_gamma[None], core_radius[None]],
            axis=0,
        )
        return jnp.transpose(stacked.reshape(12, blocks_here, age_here), (1, 0, 2))

    payload, build_pullback = jax.vjp(build, positions, next_ages, next_stations, strengths)

    def to_rows(array):
        return jnp.transpose(array.reshape(array.shape[0], blocks_here, age_here), (1, 0, 2))

    def from_rows(array):
        return jnp.transpose(array, (1, 0, 2)).reshape(shape_here)

    target_blocks = to_rows(positions)
    seed_blocks = to_rows(adjoint_seed) * time_step
    owner_onehot = (owner_ids[:, None] == jnp.arange(group_size, dtype=jnp.int32)[None, :]).astype(
        jnp.int32
    )
    rank_within = jnp.sum((jnp.cumsum(owner_onehot, axis=0) - owner_onehot) * owner_onehot, axis=1)
    slot_index = owner_ids * capacity + rank_within
    request = (
        jnp.zeros((group_size * capacity,), jnp.int32)
        .at[slot_index]
        .set(source_ids)
        .reshape(group_size, capacity)
    )
    asked = lax.all_to_all(
        request, ("turb", "age"), split_axis=0, concat_axis=0, tiled=True
    ).reshape(group_size * capacity)
    pair_targets = target_blocks[target_ids]
    pair_seed = seed_blocks[target_ids]
    outgoing = (
        jnp.zeros((group_size * capacity, 6, age_here), jnp.float32)
        .at[slot_index]
        .set(jnp.concatenate([pair_targets, pair_seed], axis=1))
    )
    incoming = lax.all_to_all(
        outgoing.reshape(group_size, capacity, 6, age_here),
        ("turb", "age"),
        split_axis=0,
        concat_axis=0,
        tiled=True,
    )
    incoming = incoming.reshape(group_size * capacity, 6, age_here)
    slot_velocity, slot_grad, payload_terms = run_pairs(
        incoming[:, 0:3], payload[asked], incoming[:, 3:6]
    )
    results = jnp.concatenate([slot_velocity, slot_grad], axis=1).reshape(
        group_size, capacity, 6, age_here
    )
    answered = lax.all_to_all(
        results, ("turb", "age"), split_axis=0, concat_axis=0, tiled=True
    ).reshape(group_size * capacity, 6, age_here)[slot_index]
    pair_velocity = answered[:, 0:3]
    pair_grad = answered[:, 3:6]
    payload_grad = onehot_sum(asked, blocks_here, payload_terms)
    velocity = onehot_sum(target_ids, blocks_here, pair_velocity)
    target_grad = onehot_sum(target_ids, blocks_here, pair_grad)
    advected = positions + time_step * from_rows(velocity)
    advected = advected.at[0].add(time_step)
    grad_nodes, grad_after_age, grad_after_station, grad_strengths = build_pullback(payload_grad)
    from_prior_age = shifted_2(grad_after_age, "age", 1)
    from_prior_station = shifted_2(grad_after_station, "span", 1)
    grad_positions = adjoint_seed + grad_nodes + from_rows(target_grad)
    grad_positions = grad_positions.at[..., 0].add(from_prior_age)
    grad_positions = grad_positions.at[:, :, :, 0, :].add(from_prior_station)
    return (advected, grad_positions, grad_strengths)


TILE = 8


def cross(a, b):
    return (
        a[1] * b[2] - a[2] * b[1],
        a[2] * b[0] - a[0] * b[2],
        a[0] * b[1] - a[1] * b[0],
    )


def dot(a, b):
    return a[0] * b[0] + a[1] * b[1] + a[2] * b[2]


def segment(r0, r1, r2, inv1, cube1, gamma, core_sq, quad, quart, inside, w):
    c = cross(r0, r1)
    c_sq = dot(c, c)
    a = dot(r0, r1)
    b = dot(r0, r2)
    inv2 = lax.rsqrt(dot(r2, r2) + core_sq)
    proj = a * inv1 - b * inv2
    inv_d = lax.rsqrt(c_sq * c_sq + quart)
    inv_d = jnp.where(inside, inv_d, 0.0)
    q = dot(w, c)
    m = gamma * inv_d
    k = m * proj
    gp = m * q
    fd = (k * q) * (inv_d * inv_d)
    grad_gamma = proj * (q * inv_d)
    h = 2.0 * fd * c_sq
    gn2 = gp * b * (inv2 * inv2 * inv2)
    alpha = gp * (inv1 - inv2) - gn2
    beta = gn2 - gp * a * cube1
    delta = 2.0 * (gp * inv2 - fd * quad) + gn2
    gc = tuple(k * w[i] - h * c[i] for i in range(3))
    left = cross(gc, r0)
    right = cross(r1, gc)
    grad_r1 = tuple(left[i] + alpha * r0[i] + beta * r1[i] for i in range(3))
    grad_r0 = tuple(right[i] + alpha * r1[i] + delta * r0[i] for i in range(3))
    velocity = tuple(k * c[i] for i in range(3))
    return velocity, grad_r1, grad_r0, grad_gamma


def pair_tile(rows, ages):
    lane = lax.broadcasted_iota(jnp.int32, (TILE, ages), 1)
    begin = rows[0:3]
    core = rows[5]
    core_sq = core * core
    trail = [
        jnp.where(
            lane == ages - 1,
            pltpu.roll(rows[6 + i], ages - 1, 1),
            pltpu.roll(begin[i], ages - 1, 1),
        )
        for i in range(3)
    ]
    alongs = [[trail[i] - begin[i] for i in range(3)], [rows[9 + i] - begin[i] for i in range(3)]]
    gammas = [rows[3] * (1.0 / four_pi), rows[4] * (1.0 / four_pi)]
    core_quad = core_sq * core_sq
    lengths = [dot(r0, r0) + core_sq for r0 in alongs]
    quads = [core_quad * length for length in lengths]
    quarts = [quad * length for quad, length in zip(quads, lengths)]
    zero = jnp.zeros((TILE, ages), jnp.float32)
    sum_r1 = [zero] * 3
    sum_r0 = [[zero] * 3, [zero] * 3]
    sum_gamma = [zero, zero]
    out = [zero] * 6
    for offset in range(-REACH, REACH):
        shift = offset % ages
        moved = [pltpu.roll(x, shift, 1) if shift else x for x in rows[12:18]]
        target, w = moved[0:3], moved[3:6]
        if offset >= 0:
            inside = lane >= offset
        else:
            inside = lane < ages + offset
        r1 = [target[i] - begin[i] for i in range(3)]
        inv1 = lax.rsqrt(dot(r1, r1) + core_sq)
        cube1 = inv1 * inv1 * inv1
        vel = [None] * 3
        g1 = [None] * 3
        for kind in range(2):
            r0 = alongs[kind]
            r2 = [r1[i] - r0[i] for i in range(3)]
            v, d1, d0, dg = segment(
                r0, r1, r2, inv1, cube1, gammas[kind], core_sq,
                quads[kind], quarts[kind], inside, w,
            )
            vel = [v[i] if kind == 0 else vel[i] + v[i] for i in range(3)]
            g1 = [d1[i] if kind == 0 else g1[i] + d1[i] for i in range(3)]
            sum_r0[kind] = [sum_r0[kind][i] + d0[i] for i in range(3)]
            sum_gamma[kind] = sum_gamma[kind] + dg
        sum_r1 = [sum_r1[i] + g1[i] for i in range(3)]
        back = (-offset) % ages
        both = vel + g1
        out = [out[i] + (pltpu.roll(both[i], back, 1) if back else both[i]) for i in range(6)]
    carry = zero
    grad_begin = []
    for i in range(3):
        moved = pltpu.roll(sum_r0[0][i], 1, 1)
        carry = jnp.where(lane == i, pltpu.roll(moved, i, 1) if i else moved, carry)
        moved = jnp.where(lane == 0, 0.0, moved)
        grad_begin.append(moved - (sum_r1[i] + sum_r0[0][i] + sum_r0[1][i]))
    gammas = [g * (1.0 / four_pi) for g in sum_gamma]
    return grad_begin + gammas + sum_r0[1] + [carry] + out


MESH = pl.DeviceIdType.MESH


def place():
    here = (lax.axis_index("turb"), lax.axis_index("age"), lax.axis_index("span"))
    spans = lax.axis_size("span")
    turb, age, span = here
    return (
        here,
        (1 - turb, age, span),
        (turb, age - 1, span),
        (turb, age + 1, span),
        (turb, age, lax.rem(span + spans - 1, spans)),
        (turb, age, lax.rem(span + 1, spans)),
    )


def greet(ages_count):
    here, other, below, above, prior, following = place()
    barrier = pltpu.get_barrier_semaphore()
    for device in (other, prior, following):
        pl.semaphore_signal(barrier, inc=1, device_id=device, device_id_type=MESH)

    @pl.when(here[1] > 0)
    def _():
        pl.semaphore_signal(barrier, inc=1, device_id=below, device_id_type=MESH)

    @pl.when(here[1] < ages_count - 1)
    def _():
        pl.semaphore_signal(barrier, inc=1, device_id=above, device_id_type=MESH)

    inner = (here[1] > 0).astype(jnp.int32) + (here[1] < ages_count - 1).astype(jnp.int32)
    pl.semaphore_wait(barrier, 3 + inner)


def keeps(stations, ages, shape):
    lane = lax.broadcasted_iota(jnp.int32, shape, 1)
    row = lax.broadcasted_iota(jnp.int32, shape, 0)
    last_age = lax.axis_index("age") == lax.axis_size("age") - 1
    last_station = lax.axis_index("span") == lax.axis_size("span") - 1
    trail = jnp.where(jnp.logical_and(last_age, lane == ages - 1), 0.0, 1.0)
    shed = jnp.where(jnp.logical_and(last_station, row % stations == stations - 1), 0.0, 1.0)
    return trail, shed


def gather_all(
    blocks, stations, per_owner, positions_ref, strengths_ref, core_ref, seed_ref, table_ref,
    strengths_buf, halo_buf, seed_buf, load_sems, halo_sems, send_sems, recv_sems,
):
    ages = table_ref.shape[-1]
    count = lax.axis_size("age")
    halo = blocks // stations
    here, other, below, above, prior, following = place()
    turb, age, span = here
    me = turb * count + age
    mate = (1 - turb) * count + age
    extra = per_owner - 6 * blocks
    parts = (
        (0, 3 * blocks),
        (3 * blocks, 2 * blocks),
        (5 * blocks, per_owner - 5 * blocks),
    )
    base = me * per_owner
    loads = [
        pltpu.make_async_copy(source, target, load_sems.at[k])
        for k, (source, target) in enumerate(
            (
                (positions_ref, table_ref.at[pl.ds(pl.multiple_of(base, 8), 3 * blocks)]),
                (strengths_ref, strengths_buf),
                (core_ref, table_ref.at[pl.ds(pl.multiple_of(base + 5 * blocks, 8), blocks)]),
                (seed_ref, seed_buf),
            )
        )
    ]
    for load in loads:
        load.start()
    halo_buf[...] = jnp.zeros_like(halo_buf)
    trail, shed = keeps(stations, ages, (blocks, ages))
    greet(count)

    def rows(owner, part):
        return pl.ds(pl.multiple_of(owner * per_owner + parts[part][0], 8), parts[part][1])

    def copy(owner, part, way):
        at = rows(owner, part)
        return pltpu.make_async_remote_copy(
            src_ref=table_ref.at[at],
            dst_ref=table_ref.at[at],
            send_sem=send_sems.at[way, part, owner],
            recv_sem=recv_sems.at[part, owner],
            device_id=(other, below, above)[way],
            device_id_type=MESH,
        )

    def arrive(owner, part):
        copy(owner, part, 0).wait_recv()

    has_below = age > 0
    has_above = age < count - 1

    def share(owner, part):
        @pl.when(has_below)
        def _():
            copy(owner, part, 1).start()

        @pl.when(has_above)
        def _():
            copy(owner, part, 2).start()

    loads[0].wait()
    share(me, 0)
    copy(me, 0, 0).start()
    for k in range(3 * halo):
        halo_buf[pl.ds(k, 1), :] = table_ref[pl.ds(base + k * stations, 1), :]
    halo_copy = pltpu.make_async_remote_copy(
        src_ref=halo_buf,
        dst_ref=table_ref.at[pl.ds(pl.multiple_of(base + 6 * blocks, 8), extra)],
        send_sem=halo_sems.at[0],
        recv_sem=halo_sems.at[1],
        device_id=prior,
        device_id_type=MESH,
    )
    halo_copy.start()
    loads[1].wait()
    table_ref[pl.ds(pl.multiple_of(base + 3 * blocks, 8), blocks), :] = (
        strengths_buf[pl.ds(0, blocks), :] * trail
    )
    table_ref[pl.ds(pl.multiple_of(base + 4 * blocks, 8), blocks), :] = (
        strengths_buf[pl.ds(blocks, blocks), :] * shed
    )
    share(me, 1)
    copy(me, 1, 0).start()
    loads[2].wait()
    loads[3].wait()
    halo_copy.wait_recv()
    copy(me, 2, 0).start()
    share(me, 2)
    arrive(mate, 2)
    share(mate, 2)
    for step in range(1, count):
        for part in range(3):
            for way, sign in ((2, -1), (1, 1)):
                source = age + sign * step
                onward = has_above if way == 2 else has_below

                @pl.when(source >= 0 if sign < 0 else source < count)
                def _(source=source, way=way, onward=onward, part=part):
                    for column in (turb, 1 - turb)[: 2 if part == 2 else 1]:
                        owner = column * count + source
                        arrive(owner, part)

                        @pl.when(onward)
                        def _(owner=owner):
                            copy(owner, part, way).start()

                        if part < 2:
                            copy(owner, part, 0).start()

    for source in range(count):
        for part in range(2):
            arrive((1 - turb) * count + source, part)
    halo_copy.wait_send()
    copy(me, 2, 0).wait_send()
    for source in range(count):
        sent = [(turb * count + source, part) for part in range(3)]
        sent.append(((1 - turb) * count + source, 2))
        for part in range(2):
            copy(sent[part][0], part, 0).wait_send()

        @pl.when(jnp.logical_and(source >= age, has_below))
        def _(sent=sent):
            for owner, part in sent:
                copy(owner, part, 1).wait_send()

        @pl.when(jnp.logical_and(source <= age, has_above))
        def _(sent=sent):
            for owner, part in sent:
                copy(owner, part, 2).wait_send()


def exact_dot(selector, terms):
    parts = [jnp.dot(selector, term, preferred_element_type=jnp.float32) for term in terms]
    return (parts[2] + parts[1]) + parts[0]


def split_terms(value):
    high = value.astype(jnp.bfloat16)
    rest = value - high.astype(jnp.float32)
    middle = rest.astype(jnp.bfloat16)
    low = (rest - middle.astype(jnp.float32)).astype(jnp.bfloat16)
    return high, middle, low


def step_kernel(
    blocks, stations, per_owner, grad_rows, early, target_ref, owner_ref, source_ref,
    target_row, owner_row, source_row, positions_ref, strengths_ref, core_ref, seed_ref,
    advected_ref, positions_grad_ref, strengths_grad_ref,
    table_ref, strengths_buf, halo_buf, seed_buf, rows_buf, values, terms, grads_ref, base_ref,
    work, from_mate, from_below, from_above, late_in, halo_out, halo_in,
    load_sems, start_sems, send_sems, recv_sems,
    mate_sems, chain_send, chain_recv, late_sems, halo_sems,
):
    ages = grads_ref.shape[-1]
    count = lax.axis_size("age")
    halo = blocks // stations
    here, other, below, above, prior, following = place()
    turb, age, span = here
    late = grad_rows - early
    half = (early + 2 * late) // 16 * 8
    cut = half - 2 * late
    pieces = ((0, cut), (cut, early - cut))
    group = 2 * count
    pairs = target_ref.shape[0]
    me = turb * count + age
    own_rows = me * per_owner

    gather_all(
        blocks, stations, per_owner, positions_ref, strengths_ref, core_ref, seed_ref, table_ref,
        strengths_buf, halo_buf, seed_buf, load_sems, start_sems, send_sems, recv_sems,
    )

    def tile(t, _):
        for j in range(TILE):
            p = t * TILE + j
            tgt = target_ref[p]
            owner = owner_ref[p]
            block = source_ref[p]
            src = owner * per_owner + block
            nxt = jnp.where(owner == group - 1, 0, owner + 1) * per_owner + block
            inner = lax.rem(block, stations) < stations - 1
            shed = jnp.where(inner, src + 1, owner * per_owner + 6 * blocks + lax.div(block, stations))
            shed_step = jnp.where(inner, blocks, halo)
            own = own_rows + tgt
            for r in range(6):
                rows_buf[pl.ds(r * TILE + j, 1), :] = table_ref[pl.ds(src + r * blocks, 1), :]
            for r in range(3):
                rows_buf[pl.ds((6 + r) * TILE + j, 1), :] = table_ref[pl.ds(nxt + r * blocks, 1), :]
                rows_buf[pl.ds((9 + r) * TILE + j, 1), :] = table_ref[pl.ds(shed + r * shed_step, 1), :]
                rows_buf[pl.ds((12 + r) * TILE + j, 1), :] = table_ref[pl.ds(own + r * blocks, 1), :]
                rows_buf[pl.ds((15 + r) * TILE + j, 1), :] = (
                    seed_buf[pl.ds(tgt + r * blocks, 1), :] * time_step
                )
        rows = [rows_buf[pl.ds(r * TILE, TILE), :] for r in range(18)]
        for r, value in enumerate(pair_tile(rows, ages)):
            values[pl.ds(pl.multiple_of(t * TILE, TILE), TILE), pl.ds(r * ages, ages)] = value
        return 0

    lax.fori_loop(0, pairs // TILE, tile, 0)
    for k, term in enumerate(split_terms(values[...])):
        terms[k] = term

    def select(rows, chosen, which):
        row = lax.broadcasted_iota(jnp.int32, (rows, pairs), 0)
        hit = jnp.logical_and(row == chosen, which)
        return jnp.where(hit, 1.0, 0.0).astype(jnp.bfloat16)

    def columns(first, number):
        return [terms[k, :, pl.ds(first * ages, number * ages)] for k in range(3)]

    owners = owner_row[...]
    sources = source_row[...]
    followers = jnp.where(owners == group - 1, 0, owners + 1)
    inner_row = sources % stations < stations - 1
    lane_first = lax.broadcasted_iota(jnp.int32, (blocks, ages), 1) == 0
    extra = grad_rows - 5 * blocks

    def scatter(column, dest):
        owner = column * count + dest
        from_here = owners == owner
        main = exact_dot(select(blocks, sources, from_here), columns(0, 5))
        inner_shed = exact_dot(
            select(blocks, sources + 1, jnp.logical_and(from_here, inner_row)), columns(5, 3)
        )
        outer_shed = exact_dot(
            select(
                -(-halo // 8) * 8,
                sources // stations,
                jnp.logical_and(from_here, jnp.logical_not(inner_row)),
            ),
            columns(5, 3),
        )
        carry = exact_dot(select(blocks, sources, followers == owner), columns(8, 1))
        for r in range(5):
            value = main[:, r * ages : (r + 1) * ages]
            if r < 3:
                lane0 = pltpu.roll(carry, ages - r, 1) if r else carry
                value = value + inner_shed[:, r * ages : (r + 1) * ages]
                value = value + jnp.where(lane_first, lane0, 0.0)
            grads_ref[part(column, dest, r * blocks, blocks), :] = value
        outer = [outer_shed[0:halo, r * ages : (r + 1) * ages] for r in range(3)]
        if extra > 3 * halo:
            outer.append(jnp.zeros((extra - 3 * halo, ages), jnp.float32))
        grads_ref[part(column, dest, 5 * blocks, extra), :] = jnp.concatenate(outer)
    spans = ((0, half), (half, early + 2 * late - half))
    has_below = age > 0
    has_above = age < count - 1

    def part(column, dest, start, number):
        owner = column * count + dest
        return pl.ds(pl.multiple_of(owner * grad_rows + start, 8), number)

    def mate_copy(dest, piece):
        return pltpu.make_async_remote_copy(
            src_ref=grads_ref.at[part(1 - turb, dest, *pieces[piece])],
            dst_ref=from_mate.at[dest, pl.ds(*pieces[piece])],
            send_sem=mate_sems.at[0, dest, piece],
            recv_sem=mate_sems.at[1, dest, piece],
            device_id=other,
            device_id_type=MESH,
        )

    def chain_copy(dest, piece, upward):
        at = pl.ds(*spans[piece])
        return pltpu.make_async_remote_copy(
            src_ref=work.at[dest, at],
            dst_ref=(from_below if upward else from_above).at[dest, at],
            send_sem=chain_send.at[dest, piece],
            recv_sem=chain_recv.at[0 if upward else 1, dest, piece],
            device_id=above if upward else below,
            device_id_type=MESH,
        )

    order = [jnp.int32(0)] * count
    rank = jnp.int32(0)
    for distance in range(count - 1, -1, -1):
        for sign in (1, -1) if distance else (1,):
            dest = age + sign * distance
            valid = jnp.logical_and(dest >= 0, dest < count)
            order = [
                jnp.where(jnp.logical_and(valid, rank == k), dest, order[k]) for k in range(count)
            ]
            rank = rank + valid.astype(jnp.int32)
    steps = [(order[k], piece) for k in range(count) for piece in range(2)]

    scatter(1 - turb, order[0])
    mate_copy(*steps[0]).start()
    mate_copy(*steps[1]).start()

    def take(number):
        dest, piece = steps[number]
        if piece == 0:
            scatter(turb, dest)
            if number + 2 < len(steps):
                scatter(1 - turb, steps[number + 2][0])
        mate_copy(dest, piece).wait_recv()
        if number + 2 < len(steps):
            mate_copy(*steps[number + 2]).start()
        start, size = pieces[piece]
        if piece == 0:
            work[dest, pl.ds(0, late), :] = grads_ref[part(turb, dest, early, late), :]
            work[dest, pl.ds(late, late), :] = grads_ref[part(1 - turb, dest, early, late), :]
        work[dest, pl.ds(2 * late + start, size), :] = (
            grads_ref[part(turb, dest, start, size), :] + from_mate[dest, pl.ds(start, size), :]
        )
        at = pl.ds(*spans[piece])

        @pl.when(jnp.logical_and(dest >= age, has_below))
        def _():
            chain_copy(dest, piece, True).wait_recv()
            work[dest, at, :] = work[dest, at, :] + from_below[dest, at, :]

        @pl.when(jnp.logical_and(dest <= age, has_above))
        def _():
            chain_copy(dest, piece, False).wait_recv()
            work[dest, at, :] = work[dest, at, :] + from_above[dest, at, :]

        pl.when(dest > age)(lambda: chain_copy(dest, piece, True).start())
        pl.when(dest < age)(lambda: chain_copy(dest, piece, False).start())

    take(0)
    target_sums = exact_dot(select(blocks, target_row[...], target_row[...] >= 0), columns(9, 6))
    for c in range(3):
        at = pl.ds(c * blocks, blocks)
        velocity = target_sums[:, c * ages : (c + 1) * ages]
        here_rows = table_ref[pl.ds(pl.multiple_of(own_rows + c * blocks, 8), blocks), :]
        advected_ref[at, :] = here_rows + time_step * (velocity + 1.0 if c == 0 else velocity)
        base_ref[at, :] = seed_buf[at, :] + target_sums[:, (3 + c) * ages : (4 + c) * ages]
    for number in range(1, len(steps) - 1):
        take(number)
    late_copy = pltpu.make_async_remote_copy(
        src_ref=work.at[age, pl.ds(late, late)],
        dst_ref=late_in,
        send_sem=late_sems.at[0],
        recv_sem=late_sems.at[1],
        device_id=other,
        device_id_type=MESH,
    )
    late_copy.start()
    late_copy.wait_recv()
    work[age, pl.ds(0, late), :] = work[age, pl.ds(0, late), :] + late_in[...]
    halo_out[...] = work[age, pl.ds(5 * blocks - early, grad_rows - 5 * blocks), :]
    halo_copy = pltpu.make_async_remote_copy(
        src_ref=halo_out,
        dst_ref=halo_in,
        send_sem=halo_sems.at[0],
        recv_sem=halo_sems.at[1],
        device_id=following,
        device_id_type=MESH,
    )
    halo_copy.start()
    trail, shed = keeps(stations, ages, (2 * blocks, ages))
    row = lax.broadcasted_iota(jnp.int32, (2 * blocks, ages), 0)
    keep = jnp.where(row < blocks, trail, shed)
    first = early - 3 * blocks
    strengths_grad_ref[pl.ds(first, 2 * blocks - first), :] = (
        work[age, pl.ds(0, 2 * blocks - first), :] * keep[first:]
    )
    take(len(steps) - 1)
    strengths_grad_ref[pl.ds(0, first), :] = (
        work[age, pl.ds(2 * late + 3 * blocks, first), :] * keep[:first]
    )
    positions_grad_ref[...] = base_ref[...] + work[age, pl.ds(2 * late, 3 * blocks), :]
    halo_copy.wait_recv()
    for k in range(3 * halo):
        at = pl.ds(k * stations, 1)
        positions_grad_ref[at, :] = positions_grad_ref[at, :] + halo_in[pl.ds(k, 1), :]
    late_copy.wait_send()
    halo_copy.wait_send()
    for dest in range(count):
        for piece in range(2):
            mate_copy(dest, piece).wait_send()
            pl.when(dest > age)(lambda d=dest, p=piece: chain_copy(d, p, True).wait_send())
            pl.when(dest < age)(lambda d=dest, p=piece: chain_copy(d, p, False).wait_send())


def local_dense(positions, strengths, core_radius, adjoint_seed, pair_target, pair_owner, pair_source):
    shape_here = positions.shape
    stations = shape_here[3]
    ages = shape_here[4]
    blocks = shape_here[1] * shape_here[2] * stations
    halo = blocks // stations
    count = lax.axis_size("age")
    group = lax.axis_size("turb") * count
    pairs = pair_target.shape[-1]
    per_owner = -(-(6 * blocks + 3 * halo) // 8) * 8
    grad_rows = -(-(5 * blocks + 3 * halo) // 8) * 8
    early = grad_rows * 5 // 6 // 8 * 8
    late = grad_rows - early
    extra = grad_rows - 5 * blocks
    vmem = pl.BlockSpec(memory_space=pltpu.VMEM)
    smem = pl.BlockSpec(memory_space=pltpu.SMEM)
    kept = pl.BlockSpec(memory_space=pl.ANY)
    dma = pltpu.SemaphoreType.DMA
    rows_out = jax.ShapeDtypeStruct((3 * blocks, ages), jnp.float32)

    def room(*shape):
        return pltpu.VMEM(shape + (ages,), jnp.float32)

    lists = (pair_target, pair_owner, pair_source)
    advected, grad_positions, grad_strengths = pl.pallas_call(
        functools.partial(step_kernel, blocks, stations, per_owner, grad_rows, early),
        out_shape=(rows_out, rows_out, jax.ShapeDtypeStruct((2 * blocks, ages), jnp.float32)),
        in_specs=[smem] * 3 + [vmem] * 3 + [kept] * 4,
        out_specs=(vmem, vmem, vmem),
        scratch_shapes=[
            room(group * per_owner),
            room(2 * blocks),
            room(per_owner - 6 * blocks),
            room(3 * blocks),
            room(18 * TILE),
            pltpu.VMEM((pairs, 15 * ages), jnp.float32),
            pltpu.VMEM((3, pairs, 15 * ages), jnp.bfloat16),
            room(group * grad_rows),
            room(3 * blocks),
            room(count, early + 2 * late),
            room(count, early),
            room(count, early + 2 * late),
            room(count, early + 2 * late),
            room(late),
            room(extra),
            room(extra),
            dma((4,)),
            dma((2,)),
            dma((3, 3, group)),
            dma((3, group)),
            dma((2, count, 2)),
            dma((count, 2)),
            dma((2, count, 2)),
            dma((2,)),
            dma((2,)),
        ],
        compiler_params=pltpu.CompilerParams(
            collective_id=0, has_side_effects=True, vmem_limit_bytes=60 * 1024 * 1024
        ),
    )(
        *[pair.reshape(pairs) for pair in lists],
        *[pair.reshape(1, pairs) for pair in lists],
        positions.reshape(3 * blocks, ages),
        strengths.reshape(2 * blocks, ages),
        core_radius.reshape(blocks, ages),
        adjoint_seed.reshape(3 * blocks, ages),
    )
    return (
        advected.reshape(shape_here),
        grad_positions.reshape(shape_here),
        grad_strengths.reshape(strengths.shape),
    )


def local(positions, strengths, core_radius, adjoint_seed, pair_target, pair_owner, pair_source):
    blocks = positions.shape[1] * positions.shape[2] * positions.shape[3]
    group = lax.axis_size("turb") * lax.axis_size("age")
    fits = lax.axis_size("turb") == 2 and lax.axis_size("span") > 2 and lax.axis_size("age") > 1
    dense = fits and group * blocks <= 8 * pair_target.shape[-1]
    chosen = local_dense if dense else local_sparse
    return chosen(
        positions, strengths, core_radius, adjoint_seed, pair_target, pair_owner, pair_source
    )


def solution(mesh):
    placed = (
        P(None, "turb", None, "span", "age"),
        P(None, "turb", None, "span", "age"),
        P("turb", None, "span", "age"),
        P(None, "turb", None, "span", "age"),
        P("turb", "age", "span", None),
        P("turb", "age", "span", None),
        P("turb", "age", "span", None),
    )
    return jax.shard_map(
        local,
        mesh=mesh,
        in_specs=placed,
        out_specs=(
            P(None, "turb", None, "span", "age"),
            P(None, "turb", None, "span", "age"),
            P(None, "turb", None, "span", "age"),
        ),
        check_vma=False,
    )
```

```python
import functools
import math

import jax
import jax.numpy as jnp
from jax import lax
from jax.experimental import pallas as pl
from jax.experimental.pallas import tpu as pltpu
from jax.sharding import PartitionSpec as P

REACH = 8


time_step = 0.5
four_pi = 4.0 * math.pi
batch_rows = 16


def shifted_2(value, axis, steps):
    count = lax.axis_size(axis)
    leading, last = (max(0, -steps), min(count, count - steps))
    return lax.ppermute(value, axis, [(source, source + steps) for source in range(leading, last)])


def windows(payload):
    age_count = payload.shape[-1]
    padded = jnp.pad(payload, ((0, 0), (0, 0), (REACH, REACH)))
    stacked = jnp.stack(
        [
            padded[:, :, REACH + offset : REACH + offset + age_count]
            for offset in range(-REACH, REACH)
        ]
    )
    shifted = (
        jnp.arange(-REACH, REACH, dtype=jnp.int32)[:, None]
        + jnp.arange(age_count, dtype=jnp.int32)[None, :]
    )
    inside = ((shifted >= 0) & (shifted < age_count)).astype(payload.dtype)
    return (stacked, inside)


def induced(targets, payload):
    stacked, inside = windows(payload)
    begins = stacked[:, :, 0:3]
    end_points = jnp.stack([stacked[:, :, 3:6], stacked[:, :, 6:9]])
    gammas = jnp.stack([stacked[:, :, 9], stacked[:, :, 10]]) * inside[None, :, None, :]
    core = jnp.where(inside[:, None, :] > 0, stacked[:, :, 11], 1.0)
    core_sq = core * core
    core_quad = core_sq * core_sq
    from_begin = targets[None] - begins
    from_end = targets[None, None] - end_points
    along = end_points - begins[None]
    near = from_begin[None]
    cross_x = near[..., 1, :] * from_end[..., 2, :] - near[..., 2, :] * from_end[..., 1, :]
    cross_y = near[..., 2, :] * from_end[..., 0, :] - near[..., 0, :] * from_end[..., 2, :]
    cross_z = near[..., 0, :] * from_end[..., 1, :] - near[..., 1, :] * from_end[..., 0, :]
    cross_sq = cross_x * cross_x + cross_y * cross_y + cross_z * cross_z
    length_sq = jnp.sum(along * along, axis=-2) + core_sq
    dist_begin = jnp.sqrt(jnp.sum(from_begin * from_begin, axis=-2) + core_sq)
    dist_end = jnp.sqrt(jnp.sum(from_end * from_end, axis=-2) + core_sq)
    projected = jnp.sum(
        along * (near / dist_begin[None, :, :, None, :] - from_end / dist_end[..., None, :]),
        axis=-2,
    )
    factor = (
        gammas
        * projected
        / (four_pi * jnp.sqrt(cross_sq * cross_sq + core_quad * length_sq * length_sq))
    )
    return jnp.stack(
        [
            jnp.sum(cross_x * factor, axis=(0, 1)),
            jnp.sum(cross_y * factor, axis=(0, 1)),
            jnp.sum(cross_z * factor, axis=(0, 1)),
        ],
        axis=1,
    )


def run_pairs(targets, payload, cotangent):
    number = targets.shape[0]
    age_count = targets.shape[-1]

    def one_batch(operands):
        velocity, pullback = jax.vjp(induced, operands[0], operands[1])
        grad_targets, grad_payload = pullback(operands[2])
        return (velocity, grad_targets, grad_payload)

    shaped = (
        targets.reshape(number // batch_rows, batch_rows, 3, age_count),
        payload.reshape(number // batch_rows, batch_rows, 12, age_count),
        cotangent.reshape(number // batch_rows, batch_rows, 3, age_count),
    )
    velocity, grad_targets, grad_payload = lax.map(one_batch, shaped)
    return (
        velocity.reshape(number, 3, age_count),
        grad_targets.reshape(number, 3, age_count),
        grad_payload.reshape(number, 12, age_count),
    )


def onehot_sum(indices, rows, values):
    selector = (jnp.arange(rows, dtype=jnp.int32)[:, None] == indices[None, :]).astype(jnp.float32)
    flat = values.reshape(values.shape[0], -1)
    summed = jnp.dot(
        selector, flat, precision=lax.Precision.HIGHEST, preferred_element_type=jnp.float32
    )
    return summed.reshape((rows,) + values.shape[1:])


def local_sparse(positions, strengths, core_radius, adjoint_seed, pair_target, pair_owner, pair_source):
    shape_here = positions.shape
    station_here = shape_here[3]
    age_here = shape_here[4]
    blocks_here = shape_here[1] * shape_here[2] * station_here
    group_size = lax.axis_size("turb") * lax.axis_size("age")
    pair_count = pair_target.shape[-1]
    capacity = 2 * pair_count // group_size
    target_ids = pair_target.reshape(pair_count)
    owner_ids = pair_owner.reshape(pair_count)
    source_ids = pair_source.reshape(pair_count)
    next_ages = shifted_2(positions[..., 0], "age", -1)
    next_stations = shifted_2(positions[:, :, :, 0, :], "span", -1)
    age_keep = (
        lax.axis_index("age") * age_here + jnp.arange(age_here, dtype=jnp.int32)
        < age_here * lax.axis_size("age") - 1
    ).astype(jnp.float32)
    station_keep = (
        lax.axis_index("span") * station_here + jnp.arange(station_here, dtype=jnp.int32)
        < station_here * lax.axis_size("span") - 1
    ).astype(jnp.float32)

    def build(nodes, after_age, after_station, circulation):
        trail_end = jnp.concatenate([nodes[..., 1:], after_age[..., None]], axis=-1)
        shed_end = jnp.concatenate([nodes[:, :, :, 1:, :], after_station[:, :, :, None, :]], axis=3)
        trail_gamma = circulation[0] * age_keep
        shed_gamma = circulation[1] * station_keep[:, None]
        stacked = jnp.concatenate(
            [nodes, trail_end, shed_end, trail_gamma[None], shed_gamma[None], core_radius[None]],
            axis=0,
        )
        return jnp.transpose(stacked.reshape(12, blocks_here, age_here), (1, 0, 2))

    payload, build_pullback = jax.vjp(build, positions, next_ages, next_stations, strengths)

    def to_rows(array):
        return jnp.transpose(array.reshape(array.shape[0], blocks_here, age_here), (1, 0, 2))

    def from_rows(array):
        return jnp.transpose(array, (1, 0, 2)).reshape(shape_here)

    target_blocks = to_rows(positions)
    seed_blocks = to_rows(adjoint_seed) * time_step
    owner_onehot = (owner_ids[:, None] == jnp.arange(group_size, dtype=jnp.int32)[None, :]).astype(
        jnp.int32
    )
    rank_within = jnp.sum((jnp.cumsum(owner_onehot, axis=0) - owner_onehot) * owner_onehot, axis=1)
    slot_index = owner_ids * capacity + rank_within
    request = (
        jnp.zeros((group_size * capacity,), jnp.int32)
        .at[slot_index]
        .set(source_ids)
        .reshape(group_size, capacity)
    )
    asked = lax.all_to_all(
        request, ("turb", "age"), split_axis=0, concat_axis=0, tiled=True
    ).reshape(group_size * capacity)
    pair_targets = target_blocks[target_ids]
    pair_seed = seed_blocks[target_ids]
    outgoing = (
        jnp.zeros((group_size * capacity, 6, age_here), jnp.float32)
        .at[slot_index]
        .set(jnp.concatenate([pair_targets, pair_seed], axis=1))
    )
    incoming = lax.all_to_all(
        outgoing.reshape(group_size, capacity, 6, age_here),
        ("turb", "age"),
        split_axis=0,
        concat_axis=0,
        tiled=True,
    )
    incoming = incoming.reshape(group_size * capacity, 6, age_here)
    slot_velocity, slot_grad, payload_terms = run_pairs(
        incoming[:, 0:3], payload[asked], incoming[:, 3:6]
    )
    results = jnp.concatenate([slot_velocity, slot_grad], axis=1).reshape(
        group_size, capacity, 6, age_here
    )
    answered = lax.all_to_all(
        results, ("turb", "age"), split_axis=0, concat_axis=0, tiled=True
    ).reshape(group_size * capacity, 6, age_here)[slot_index]
    pair_velocity = answered[:, 0:3]
    pair_grad = answered[:, 3:6]
    payload_grad = onehot_sum(asked, blocks_here, payload_terms)
    velocity = onehot_sum(target_ids, blocks_here, pair_velocity)
    target_grad = onehot_sum(target_ids, blocks_here, pair_grad)
    advected = positions + time_step * from_rows(velocity)
    advected = advected.at[0].add(time_step)
    grad_nodes, grad_after_age, grad_after_station, grad_strengths = build_pullback(payload_grad)
    from_prior_age = shifted_2(grad_after_age, "age", 1)
    from_prior_station = shifted_2(grad_after_station, "span", 1)
    grad_positions = adjoint_seed + grad_nodes + from_rows(target_grad)
    grad_positions = grad_positions.at[..., 0].add(from_prior_age)
    grad_positions = grad_positions.at[:, :, :, 0, :].add(from_prior_station)
    return (advected, grad_positions, grad_strengths)


TILE = 8


def cross(a, b):
    return (
        a[1] * b[2] - a[2] * b[1],
        a[2] * b[0] - a[0] * b[2],
        a[0] * b[1] - a[1] * b[0],
    )


def dot(a, b):
    return a[0] * b[0] + a[1] * b[1] + a[2] * b[2]


def segment(r0, r1, r2, inv1, along_sq, gamma, core_sq, quad, quart, inside, w):
    c = cross(r0, r1)
    c_sq = dot(c, c)
    a = dot(r0, r1)
    b = a - along_sq
    inv2 = lax.rsqrt(dot(r2, r2) + core_sq)
    proj = a * inv1 - b * inv2
    inv_d = lax.rsqrt(c_sq * c_sq + quart)
    inv_d = jnp.where(inside, inv_d, 0.0)
    q = dot(w, c)
    m = gamma * inv_d
    k = m * proj
    gp = m * q
    fd = (k * q) * (2.0 * (inv_d * inv_d))
    grad_gamma = proj * (q * inv_d)
    h = fd * c_sq
    gn2 = gp * b * (inv2 * inv2 * inv2)
    alpha = gp * (inv1 - inv2) - gn2
    delta = gp * (inv2 + inv2) - fd * quad + gn2
    gc = tuple(k * w[i] - h * c[i] for i in range(3))
    left = cross(gc, r0)
    right = cross(r1, gc)
    grad_r1 = tuple(left[i] + alpha * r0[i] for i in range(3))
    grad_r0 = tuple(right[i] + alpha * r1[i] for i in range(3))
    velocity = tuple(k * c[i] for i in range(3))
    return velocity, grad_r1, grad_r0, grad_gamma, delta, gn2, gp * a


def pair_tile(rows, ages):
    lane = lax.broadcasted_iota(jnp.int32, (TILE, ages), 1)
    begin = rows[0:3]
    core = rows[5]
    core_sq = core * core
    trail = [
        jnp.where(
            lane == ages - 1,
            pltpu.roll(rows[6 + i], ages - 1, 1),
            pltpu.roll(begin[i], ages - 1, 1),
        )
        for i in range(3)
    ]
    alongs = [[trail[i] - begin[i] for i in range(3)], [rows[9 + i] - begin[i] for i in range(3)]]
    gammas = [rows[3] * (1.0 / four_pi), rows[4] * (1.0 / four_pi)]
    core_quad = core_sq * core_sq
    alongs_sq = [dot(r0, r0) for r0 in alongs]
    lengths = [along_sq + core_sq for along_sq in alongs_sq]
    quads = [core_quad * length for length in lengths]
    quarts = [quad * length for quad, length in zip(quads, lengths)]
    zero = jnp.zeros((TILE, ages), jnp.float32)
    sum_r1 = [zero] * 3
    sum_r0 = [[zero] * 3, [zero] * 3]
    sum_gamma = [zero, zero]
    sum_delta = [zero, zero]
    out = [zero] * 6
    for offset in range(-REACH, REACH):
        shift = offset % ages
        moved = [pltpu.roll(x, shift, 1) if shift else x for x in rows[12:18]]
        target, w = moved[0:3], moved[3:6]
        if offset >= 0:
            inside = lane >= offset
        else:
            inside = lane < ages + offset
        r1 = [target[i] - begin[i] for i in range(3)]
        inv1 = lax.rsqrt(dot(r1, r1) + core_sq)
        beta = [None, None]
        ga = [None, None]
        vel = [None] * 3
        g1 = [None] * 3
        for kind in range(2):
            r0 = alongs[kind]
            r2 = [r1[i] - r0[i] for i in range(3)]
            v, d1, d0, dg, delta, beta[kind], ga[kind] = segment(
                r0, r1, r2, inv1, alongs_sq[kind], gammas[kind], core_sq,
                quads[kind], quarts[kind], inside, w,
            )
            vel = [v[i] if kind == 0 else vel[i] + v[i] for i in range(3)]
            g1 = [d1[i] if kind == 0 else g1[i] + d1[i] for i in range(3)]
            sum_r0[kind] = [sum_r0[kind][i] + d0[i] for i in range(3)]
            sum_gamma[kind] = sum_gamma[kind] + dg
            sum_delta[kind] = sum_delta[kind] + delta
        pull = (beta[0] + beta[1]) - (ga[0] + ga[1]) * (inv1 * inv1 * inv1)
        g1 = [g1[i] + pull * r1[i] for i in range(3)]
        sum_r1 = [sum_r1[i] + g1[i] for i in range(3)]
        back = (-offset) % ages
        both = vel + g1
        out = [out[i] + (pltpu.roll(both[i], back, 1) if back else both[i]) for i in range(6)]
    sum_r0 = [
        [sum_r0[kind][i] + sum_delta[kind] * alongs[kind][i] for i in range(3)] for kind in range(2)
    ]
    carry = zero
    grad_begin = []
    for i in range(3):
        moved = pltpu.roll(sum_r0[0][i], 1, 1)
        carry = jnp.where(lane == i, pltpu.roll(moved, i, 1) if i else moved, carry)
        moved = jnp.where(lane == 0, 0.0, moved)
        grad_begin.append(moved - (sum_r1[i] + sum_r0[0][i] + sum_r0[1][i]))
    gammas = [g * (1.0 / four_pi) for g in sum_gamma]
    return grad_begin + gammas + sum_r0[1] + [carry] + out


MESH = pl.DeviceIdType.MESH


def place():
    here = (lax.axis_index("turb"), lax.axis_index("age"), lax.axis_index("span"))
    spans = lax.axis_size("span")
    turb, age, span = here
    return (
        here,
        (1 - turb, age, span),
        (turb, age - 1, span),
        (turb, age + 1, span),
        (turb, age, lax.rem(span + spans - 1, spans)),
        (turb, age, lax.rem(span + 1, spans)),
    )


def greet(ages_count):
    here, other, below, above, prior, following = place()
    barrier = pltpu.get_barrier_semaphore()
    for device in (other, prior, following):
        pl.semaphore_signal(barrier, inc=1, device_id=device, device_id_type=MESH)

    @pl.when(here[1] > 0)
    def _():
        pl.semaphore_signal(barrier, inc=1, device_id=below, device_id_type=MESH)

    @pl.when(here[1] < ages_count - 1)
    def _():
        pl.semaphore_signal(barrier, inc=1, device_id=above, device_id_type=MESH)

    inner = (here[1] > 0).astype(jnp.int32) + (here[1] < ages_count - 1).astype(jnp.int32)
    pl.semaphore_wait(barrier, 3 + inner)


def keeps(stations, ages, shape):
    lane = lax.broadcasted_iota(jnp.int32, shape, 1)
    row = lax.broadcasted_iota(jnp.int32, shape, 0)
    last_age = lax.axis_index("age") == lax.axis_size("age") - 1
    last_station = lax.axis_index("span") == lax.axis_size("span") - 1
    trail = jnp.where(jnp.logical_and(last_age, lane == ages - 1), 0.0, 1.0)
    shed = jnp.where(jnp.logical_and(last_station, row % stations == stations - 1), 0.0, 1.0)
    return trail, shed


def gather_all(
    blocks, stations, per_owner, positions_ref, strengths_ref, core_ref, seed_ref, table_ref,
    strengths_buf, halo_buf, seed_buf, load_sems, halo_sems, send_sems, recv_sems,
):
    ages = table_ref.shape[-1]
    count = lax.axis_size("age")
    halo = blocks // stations
    here, other, below, above, prior, following = place()
    turb, age, span = here
    me = turb * count + age
    mate = (1 - turb) * count + age
    extra = per_owner - 6 * blocks
    parts = (
        (0, 3 * blocks),
        (3 * blocks, 2 * blocks),
        (5 * blocks, per_owner - 5 * blocks),
    )
    base = me * per_owner
    loads = [
        pltpu.make_async_copy(source, target, load_sems.at[k])
        for k, (source, target) in enumerate(
            (
                (positions_ref, table_ref.at[pl.ds(pl.multiple_of(base, 8), 3 * blocks)]),
                (strengths_ref, strengths_buf),
                (core_ref, table_ref.at[pl.ds(pl.multiple_of(base + 5 * blocks, 8), blocks)]),
                (seed_ref, seed_buf),
            )
        )
    ]
    for load in loads:
        load.start()
    halo_buf[...] = jnp.zeros_like(halo_buf)
    trail, shed = keeps(stations, ages, (blocks, ages))
    greet(count)

    def rows(owner, part):
        return pl.ds(pl.multiple_of(owner * per_owner + parts[part][0], 8), parts[part][1])

    def copy(owner, part, way):
        at = rows(owner, part)
        return pltpu.make_async_remote_copy(
            src_ref=table_ref.at[at],
            dst_ref=table_ref.at[at],
            send_sem=send_sems.at[way, part, owner],
            recv_sem=recv_sems.at[part, owner],
            device_id=(other, below, above)[way],
            device_id_type=MESH,
        )

    def arrive(owner, part):
        copy(owner, part, 0).wait_recv()

    has_below = age > 0
    has_above = age < count - 1

    def share(owner, part):
        @pl.when(has_below)
        def _():
            copy(owner, part, 1).start()

        @pl.when(has_above)
        def _():
            copy(owner, part, 2).start()

    loads[0].wait()
    share(me, 0)
    copy(me, 0, 0).start()
    for k in range(3 * halo):
        halo_buf[pl.ds(k, 1), :] = table_ref[pl.ds(base + k * stations, 1), :]
    halo_copy = pltpu.make_async_remote_copy(
        src_ref=halo_buf,
        dst_ref=table_ref.at[pl.ds(pl.multiple_of(base + 6 * blocks, 8), extra)],
        send_sem=halo_sems.at[0],
        recv_sem=halo_sems.at[1],
        device_id=prior,
        device_id_type=MESH,
    )
    halo_copy.start()
    loads[1].wait()
    table_ref[pl.ds(pl.multiple_of(base + 3 * blocks, 8), blocks), :] = (
        strengths_buf[pl.ds(0, blocks), :] * trail
    )
    table_ref[pl.ds(pl.multiple_of(base + 4 * blocks, 8), blocks), :] = (
        strengths_buf[pl.ds(blocks, blocks), :] * shed
    )
    share(me, 1)
    copy(me, 1, 0).start()
    loads[2].wait()
    loads[3].wait()
    halo_copy.wait_recv()
    copy(me, 2, 0).start()
    share(me, 2)
    arrive(mate, 2)
    share(mate, 2)
    for step in range(1, count):
        for part in range(3):
            for way, sign in ((2, -1), (1, 1)):
                source = age + sign * step
                onward = has_above if way == 2 else has_below

                @pl.when(source >= 0 if sign < 0 else source < count)
                def _(source=source, way=way, onward=onward, part=part):
                    for column in (turb, 1 - turb)[: 2 if part == 2 else 1]:
                        owner = column * count + source
                        arrive(owner, part)

                        @pl.when(onward)
                        def _(owner=owner):
                            copy(owner, part, way).start()

                        if part < 2:
                            copy(owner, part, 0).start()

    for source in range(count):
        for part in range(2):
            arrive((1 - turb) * count + source, part)
    def finish():
        halo_copy.wait_send()
        copy(me, 2, 0).wait_send()
        for source in range(count):
            sent = [(turb * count + source, part) for part in range(3)]
            sent.append(((1 - turb) * count + source, 2))
            for part in range(2):
                copy(sent[part][0], part, 0).wait_send()

            @pl.when(jnp.logical_and(source >= age, has_below))
            def _(sent=sent):
                for owner, part in sent:
                    copy(owner, part, 1).wait_send()

            @pl.when(jnp.logical_and(source <= age, has_above))
            def _(sent=sent):
                for owner, part in sent:
                    copy(owner, part, 2).wait_send()

    return finish


def exact_dot(selector, terms):
    parts = [jnp.dot(selector, term, preferred_element_type=jnp.float32) for term in terms]
    return (parts[2] + parts[1]) + parts[0]


def split_terms(value):
    high = value.astype(jnp.bfloat16)
    rest = value - high.astype(jnp.float32)
    middle = rest.astype(jnp.bfloat16)
    low = (rest - middle.astype(jnp.float32)).astype(jnp.bfloat16)
    return high, middle, low


def step_kernel(
    blocks, stations, per_owner, grad_rows, early, target_ref, owner_ref, source_ref,
    target_row, owner_row, source_row, positions_ref, strengths_ref, core_ref, seed_ref,
    moved_ref, positions_grad_ref, strengths_grad_ref,
    table_ref, strengths_buf, halo_buf, seed_buf, rows_buf, values, terms, grads_ref, base_ref,
    work, from_mate, from_below, from_above, late_in, halo_out, halo_in,
    load_sems, start_sems, send_sems, recv_sems,
    mate_sems, chain_send, chain_recv, late_sems, halo_sems,
):
    ages = grads_ref.shape[-1]
    count = lax.axis_size("age")
    halo = blocks // stations
    here, other, below, above, prior, following = place()
    turb, age, span = here
    late = grad_rows - early
    half = (early + 2 * late) // 16 * 8
    cut = half - 2 * late
    pieces = ((0, cut), (cut, early - cut))
    group = 2 * count
    pairs = target_ref.shape[0]
    me = turb * count + age
    own_rows = me * per_owner

    finish = gather_all(
        blocks, stations, per_owner, positions_ref, strengths_ref, core_ref, seed_ref, table_ref,
        strengths_buf, halo_buf, seed_buf, load_sems, start_sems, send_sems, recv_sems,
    )

    def fetch(t):
        for j in range(TILE):
            p = t * TILE + j
            tgt = target_ref[p]
            owner = owner_ref[p]
            block = source_ref[p]
            src = owner * per_owner + block
            nxt = jnp.where(owner == group - 1, 0, owner + 1) * per_owner + block
            inner = lax.rem(block, stations) < stations - 1
            shed = jnp.where(inner, src + 1, owner * per_owner + 6 * blocks + lax.div(block, stations))
            shed_step = jnp.where(inner, blocks, halo)
            own = own_rows + tgt
            for r in range(6):
                rows_buf[pl.ds(r * TILE + j, 1), :] = table_ref[pl.ds(src + r * blocks, 1), :]
            for r in range(3):
                rows_buf[pl.ds((6 + r) * TILE + j, 1), :] = table_ref[pl.ds(nxt + r * blocks, 1), :]
                rows_buf[pl.ds((9 + r) * TILE + j, 1), :] = table_ref[pl.ds(shed + r * shed_step, 1), :]
                rows_buf[pl.ds((12 + r) * TILE + j, 1), :] = table_ref[pl.ds(own + r * blocks, 1), :]
                rows_buf[pl.ds((15 + r) * TILE + j, 1), :] = seed_buf[pl.ds(tgt + r * blocks, 1), :]

    def tile(t, _):
        rows = [rows_buf[pl.ds(r * TILE, TILE), :] for r in range(18)]
        rows[15:18] = [seed * time_step for seed in rows[15:18]]
        fetch(jnp.minimum(t + 1, pairs // TILE - 1))
        for r, value in enumerate(pair_tile(rows, ages)):
            values[pl.ds(pl.multiple_of(t * TILE, TILE), TILE), pl.ds(r * ages, ages)] = value
        return 0

    fetch(0)
    lax.fori_loop(0, pairs // TILE, tile, 0)
    for k, term in enumerate(split_terms(values[...])):
        terms[k] = term

    def select(rows, chosen, which):
        row = lax.broadcasted_iota(jnp.int32, (rows, pairs), 0)
        hit = jnp.logical_and(row == chosen, which)
        return jnp.where(hit, 1.0, 0.0).astype(jnp.bfloat16)

    def columns(first, number):
        return [terms[k, :, pl.ds(first * ages, number * ages)] for k in range(3)]

    owners = owner_row[...]
    sources = source_row[...]
    followers = jnp.where(owners == group - 1, 0, owners + 1)
    inner_row = sources % stations < stations - 1
    lane_first = lax.broadcasted_iota(jnp.int32, (blocks, ages), 1) == 0
    extra = grad_rows - 5 * blocks

    def scatter(column, dest):
        owner = column * count + dest
        from_here = owners == owner
        main = exact_dot(select(blocks, sources, from_here), columns(0, 5))
        inner_shed = exact_dot(
            select(blocks, sources + 1, jnp.logical_and(from_here, inner_row)), columns(5, 3)
        )
        outer_shed = exact_dot(
            select(
                -(-halo // 8) * 8,
                sources // stations,
                jnp.logical_and(from_here, jnp.logical_not(inner_row)),
            ),
            columns(5, 3),
        )
        carry = exact_dot(select(blocks, sources, followers == owner), columns(8, 1))
        for r in range(5):
            value = main[:, r * ages : (r + 1) * ages]
            if r < 3:
                lane0 = pltpu.roll(carry, ages - r, 1) if r else carry
                value = value + inner_shed[:, r * ages : (r + 1) * ages]
                value = value + jnp.where(lane_first, lane0, 0.0)
            grads_ref[part(column, dest, r * blocks, blocks), :] = value
        outer = [outer_shed[0:halo, r * ages : (r + 1) * ages] for r in range(3)]
        if extra > 3 * halo:
            outer.append(jnp.zeros((extra - 3 * halo, ages), jnp.float32))
        grads_ref[part(column, dest, 5 * blocks, extra), :] = jnp.concatenate(outer)
    spans = ((0, half), (half, early + 2 * late - half))
    has_below = age > 0
    has_above = age < count - 1

    def part(column, dest, start, number):
        owner = column * count + dest
        return pl.ds(pl.multiple_of(owner * grad_rows + start, 8), number)

    def mate_copy(dest, piece):
        return pltpu.make_async_remote_copy(
            src_ref=grads_ref.at[part(1 - turb, dest, *pieces[piece])],
            dst_ref=from_mate.at[dest, pl.ds(*pieces[piece])],
            send_sem=mate_sems.at[0, dest, piece],
            recv_sem=mate_sems.at[1, dest, piece],
            device_id=other,
            device_id_type=MESH,
        )

    def chain_copy(dest, piece, upward):
        at = pl.ds(*spans[piece])
        return pltpu.make_async_remote_copy(
            src_ref=work.at[dest, at],
            dst_ref=(from_below if upward else from_above).at[dest, at],
            send_sem=chain_send.at[dest, piece],
            recv_sem=chain_recv.at[0 if upward else 1, dest, piece],
            device_id=above if upward else below,
            device_id_type=MESH,
        )

    order = [jnp.int32(0)] * count
    rank = jnp.int32(0)
    for distance in range(count - 1, -1, -1):
        for sign in (1, -1) if distance else (1,):
            dest = age + sign * distance
            valid = jnp.logical_and(dest >= 0, dest < count)
            order = [
                jnp.where(jnp.logical_and(valid, rank == k), dest, order[k]) for k in range(count)
            ]
            rank = rank + valid.astype(jnp.int32)
    steps = [(order[k], piece) for k in range(count) for piece in range(2)]

    scatter(1 - turb, order[0])
    mate_copy(*steps[0]).start()
    mate_copy(*steps[1]).start()

    def take(number):
        dest, piece = steps[number]
        if piece == 0:
            scatter(turb, dest)
            if number + 2 < len(steps):
                scatter(1 - turb, steps[number + 2][0])
        mate_copy(dest, piece).wait_recv()
        if number + 2 < len(steps):
            mate_copy(*steps[number + 2]).start()
        start, size = pieces[piece]
        if piece == 0:
            work[dest, pl.ds(0, late), :] = grads_ref[part(turb, dest, early, late), :]
            work[dest, pl.ds(late, late), :] = grads_ref[part(1 - turb, dest, early, late), :]
        work[dest, pl.ds(2 * late + start, size), :] = (
            grads_ref[part(turb, dest, start, size), :] + from_mate[dest, pl.ds(start, size), :]
        )
        at = pl.ds(*spans[piece])

        @pl.when(jnp.logical_and(dest >= age, has_below))
        def _():
            chain_copy(dest, piece, True).wait_recv()
            work[dest, at, :] = work[dest, at, :] + from_below[dest, at, :]

        @pl.when(jnp.logical_and(dest <= age, has_above))
        def _():
            chain_copy(dest, piece, False).wait_recv()
            work[dest, at, :] = work[dest, at, :] + from_above[dest, at, :]

        pl.when(dest > age)(lambda: chain_copy(dest, piece, True).start())
        pl.when(dest < age)(lambda: chain_copy(dest, piece, False).start())

    take(0)
    target_sums = exact_dot(select(blocks, target_row[...], target_row[...] >= 0), columns(9, 6))
    for c in range(3):
        at = pl.ds(c * blocks, blocks)
        velocity = target_sums[:, c * ages : (c + 1) * ages]
        moved_ref[at, :] = time_step * (velocity + 1.0 if c == 0 else velocity)
        base_ref[at, :] = target_sums[:, (3 + c) * ages : (4 + c) * ages]
    for number in range(1, len(steps) - 1):
        take(number)
    late_copy = pltpu.make_async_remote_copy(
        src_ref=work.at[age, pl.ds(late, late)],
        dst_ref=late_in,
        send_sem=late_sems.at[0],
        recv_sem=late_sems.at[1],
        device_id=other,
        device_id_type=MESH,
    )
    late_copy.start()
    late_copy.wait_recv()
    work[age, pl.ds(0, late), :] = work[age, pl.ds(0, late), :] + late_in[...]
    halo_out[...] = work[age, pl.ds(5 * blocks - early, grad_rows - 5 * blocks), :]
    halo_copy = pltpu.make_async_remote_copy(
        src_ref=halo_out,
        dst_ref=halo_in,
        send_sem=halo_sems.at[0],
        recv_sem=halo_sems.at[1],
        device_id=following,
        device_id_type=MESH,
    )
    halo_copy.start()
    trail, shed = keeps(stations, ages, (2 * blocks, ages))
    row = lax.broadcasted_iota(jnp.int32, (2 * blocks, ages), 0)
    keep = jnp.where(row < blocks, trail, shed)
    first = early - 3 * blocks
    strengths_grad_ref[pl.ds(first, 2 * blocks - first), :] = (
        work[age, pl.ds(0, 2 * blocks - first), :] * keep[first:]
    )
    take(len(steps) - 1)
    strengths_grad_ref[pl.ds(0, first), :] = (
        work[age, pl.ds(2 * late + 3 * blocks, first), :] * keep[:first]
    )
    positions_grad_ref[...] = base_ref[...] + work[age, pl.ds(2 * late, 3 * blocks), :]
    halo_copy.wait_recv()
    for k in range(3 * halo):
        at = pl.ds(k * stations, 1)
        positions_grad_ref[at, :] = positions_grad_ref[at, :] + halo_in[pl.ds(k, 1), :]
    finish()
    late_copy.wait_send()
    halo_copy.wait_send()
    for dest in range(count):
        for piece in range(2):
            mate_copy(dest, piece).wait_send()
            pl.when(dest > age)(lambda d=dest, p=piece: chain_copy(d, p, True).wait_send())
            pl.when(dest < age)(lambda d=dest, p=piece: chain_copy(d, p, False).wait_send())


def local_dense(positions, strengths, core_radius, adjoint_seed, pair_target, pair_owner, pair_source):
    shape_here = positions.shape
    stations = shape_here[3]
    ages = shape_here[4]
    blocks = shape_here[1] * shape_here[2] * stations
    halo = blocks // stations
    count = lax.axis_size("age")
    group = lax.axis_size("turb") * count
    pairs = pair_target.shape[-1]
    per_owner = -(-(6 * blocks + 3 * halo) // 8) * 8
    grad_rows = -(-(5 * blocks + 3 * halo) // 8) * 8
    early = grad_rows * 5 // 6 // 8 * 8
    late = grad_rows - early
    extra = grad_rows - 5 * blocks
    vmem = pl.BlockSpec(memory_space=pltpu.VMEM)
    smem = pl.BlockSpec(memory_space=pltpu.SMEM)
    kept = pl.BlockSpec(memory_space=pl.ANY)
    dma = pltpu.SemaphoreType.DMA
    rows_out = jax.ShapeDtypeStruct((3 * blocks, ages), jnp.float32)

    def room(*shape):
        return pltpu.VMEM(shape + (ages,), jnp.float32)

    lists = (pair_target, pair_owner, pair_source)
    moved, grad_moved, grad_strengths = pl.pallas_call(
        functools.partial(step_kernel, blocks, stations, per_owner, grad_rows, early),
        out_shape=(rows_out, rows_out, jax.ShapeDtypeStruct((2 * blocks, ages), jnp.float32)),
        in_specs=[smem] * 3 + [vmem] * 3 + [kept] * 4,
        out_specs=(vmem, vmem, vmem),
        scratch_shapes=[
            room(group * per_owner),
            room(2 * blocks),
            room(per_owner - 6 * blocks),
            room(3 * blocks),
            room(18 * TILE),
            pltpu.VMEM((pairs, 15 * ages), jnp.float32),
            pltpu.VMEM((3, pairs, 15 * ages), jnp.bfloat16),
            room(group * grad_rows),
            room(3 * blocks),
            room(count, early + 2 * late),
            room(count, early),
            room(count, early + 2 * late),
            room(count, early + 2 * late),
            room(late),
            room(extra),
            room(extra),
            dma((4,)),
            dma((2,)),
            dma((3, 3, group)),
            dma((3, group)),
            dma((2, count, 2)),
            dma((count, 2)),
            dma((2, count, 2)),
            dma((2,)),
            dma((2,)),
        ],
        compiler_params=pltpu.CompilerParams(
            collective_id=0, has_side_effects=True, vmem_limit_bytes=60 * 1024 * 1024
        ),
    )(
        *[pair.reshape(pairs) for pair in lists],
        *[pair.reshape(1, pairs) for pair in lists],
        positions.reshape(3 * blocks, ages),
        strengths.reshape(2 * blocks, ages),
        core_radius.reshape(blocks, ages),
        adjoint_seed.reshape(3 * blocks, ages),
    )
    return (
        positions + moved.reshape(shape_here),
        adjoint_seed + grad_moved.reshape(shape_here),
        grad_strengths.reshape(strengths.shape),
    )


def local(positions, strengths, core_radius, adjoint_seed, pair_target, pair_owner, pair_source):
    blocks = positions.shape[1] * positions.shape[2] * positions.shape[3]
    group = lax.axis_size("turb") * lax.axis_size("age")
    fits = lax.axis_size("turb") == 2 and lax.axis_size("span") > 2 and lax.axis_size("age") > 1
    dense = fits and group * blocks <= 8 * pair_target.shape[-1]
    chosen = local_dense if dense else local_sparse
    return chosen(
        positions, strengths, core_radius, adjoint_seed, pair_target, pair_owner, pair_source
    )


def solution(mesh):
    placed = (
        P(None, "turb", None, "span", "age"),
        P(None, "turb", None, "span", "age"),
        P("turb", None, "span", "age"),
        P(None, "turb", None, "span", "age"),
        P("turb", "age", "span", None),
        P("turb", "age", "span", None),
        P("turb", "age", "span", None),
    )
    return jax.shard_map(
        local,
        mesh=mesh,
        in_specs=placed,
        out_specs=(
            P(None, "turb", None, "span", "age"),
            P(None, "turb", None, "span", "age"),
            P(None, "turb", None, "span", "age"),
        ),
        check_vma=False,
    )
```

```python
import functools
import math

import jax
import jax.numpy as jnp
from jax import lax
from jax.experimental import pallas as pl
from jax.experimental.pallas import tpu as pltpu
from jax.sharding import PartitionSpec as P

REACH = 8


time_step = 0.5
four_pi = 4.0 * math.pi
batch_rows = 16


def shifted_2(value, axis, steps):
    count = lax.axis_size(axis)
    leading, last = (max(0, -steps), min(count, count - steps))
    return lax.ppermute(value, axis, [(source, source + steps) for source in range(leading, last)])


def windows(payload):
    age_count = payload.shape[-1]
    padded = jnp.pad(payload, ((0, 0), (0, 0), (REACH, REACH)))
    stacked = jnp.stack(
        [
            padded[:, :, REACH + offset : REACH + offset + age_count]
            for offset in range(-REACH, REACH)
        ]
    )
    shifted = (
        jnp.arange(-REACH, REACH, dtype=jnp.int32)[:, None]
        + jnp.arange(age_count, dtype=jnp.int32)[None, :]
    )
    inside = ((shifted >= 0) & (shifted < age_count)).astype(payload.dtype)
    return (stacked, inside)


def induced(targets, payload):
    stacked, inside = windows(payload)
    begins = stacked[:, :, 0:3]
    end_points = jnp.stack([stacked[:, :, 3:6], stacked[:, :, 6:9]])
    gammas = jnp.stack([stacked[:, :, 9], stacked[:, :, 10]]) * inside[None, :, None, :]
    core = jnp.where(inside[:, None, :] > 0, stacked[:, :, 11], 1.0)
    core_sq = core * core
    core_quad = core_sq * core_sq
    from_begin = targets[None] - begins
    from_end = targets[None, None] - end_points
    along = end_points - begins[None]
    near = from_begin[None]
    cross_x = near[..., 1, :] * from_end[..., 2, :] - near[..., 2, :] * from_end[..., 1, :]
    cross_y = near[..., 2, :] * from_end[..., 0, :] - near[..., 0, :] * from_end[..., 2, :]
    cross_z = near[..., 0, :] * from_end[..., 1, :] - near[..., 1, :] * from_end[..., 0, :]
    cross_sq = cross_x * cross_x + cross_y * cross_y + cross_z * cross_z
    length_sq = jnp.sum(along * along, axis=-2) + core_sq
    dist_begin = jnp.sqrt(jnp.sum(from_begin * from_begin, axis=-2) + core_sq)
    dist_end = jnp.sqrt(jnp.sum(from_end * from_end, axis=-2) + core_sq)
    projected = jnp.sum(
        along * (near / dist_begin[None, :, :, None, :] - from_end / dist_end[..., None, :]),
        axis=-2,
    )
    factor = (
        gammas
        * projected
        / (four_pi * jnp.sqrt(cross_sq * cross_sq + core_quad * length_sq * length_sq))
    )
    return jnp.stack(
        [
            jnp.sum(cross_x * factor, axis=(0, 1)),
            jnp.sum(cross_y * factor, axis=(0, 1)),
            jnp.sum(cross_z * factor, axis=(0, 1)),
        ],
        axis=1,
    )


def run_pairs(targets, payload, cotangent):
    number = targets.shape[0]
    age_count = targets.shape[-1]

    def one_batch(operands):
        velocity, pullback = jax.vjp(induced, operands[0], operands[1])
        grad_targets, grad_payload = pullback(operands[2])
        return (velocity, grad_targets, grad_payload)

    shaped = (
        targets.reshape(number // batch_rows, batch_rows, 3, age_count),
        payload.reshape(number // batch_rows, batch_rows, 12, age_count),
        cotangent.reshape(number // batch_rows, batch_rows, 3, age_count),
    )
    velocity, grad_targets, grad_payload = lax.map(one_batch, shaped)
    return (
        velocity.reshape(number, 3, age_count),
        grad_targets.reshape(number, 3, age_count),
        grad_payload.reshape(number, 12, age_count),
    )


def onehot_sum(indices, rows, values):
    selector = (jnp.arange(rows, dtype=jnp.int32)[:, None] == indices[None, :]).astype(jnp.float32)
    flat = values.reshape(values.shape[0], -1)
    summed = jnp.dot(
        selector, flat, precision=lax.Precision.HIGHEST, preferred_element_type=jnp.float32
    )
    return summed.reshape((rows,) + values.shape[1:])


def local_sparse(positions, strengths, core_radius, adjoint_seed, pair_target, pair_owner, pair_source):
    shape_here = positions.shape
    station_here = shape_here[3]
    age_here = shape_here[4]
    blocks_here = shape_here[1] * shape_here[2] * station_here
    group_size = lax.axis_size("turb") * lax.axis_size("age")
    pair_count = pair_target.shape[-1]
    capacity = 2 * pair_count // group_size
    target_ids = pair_target.reshape(pair_count)
    owner_ids = pair_owner.reshape(pair_count)
    source_ids = pair_source.reshape(pair_count)
    next_ages = shifted_2(positions[..., 0], "age", -1)
    next_stations = shifted_2(positions[:, :, :, 0, :], "span", -1)
    age_keep = (
        lax.axis_index("age") * age_here + jnp.arange(age_here, dtype=jnp.int32)
        < age_here * lax.axis_size("age") - 1
    ).astype(jnp.float32)
    station_keep = (
        lax.axis_index("span") * station_here + jnp.arange(station_here, dtype=jnp.int32)
        < station_here * lax.axis_size("span") - 1
    ).astype(jnp.float32)

    def build(nodes, after_age, after_station, circulation):
        trail_end = jnp.concatenate([nodes[..., 1:], after_age[..., None]], axis=-1)
        shed_end = jnp.concatenate([nodes[:, :, :, 1:, :], after_station[:, :, :, None, :]], axis=3)
        trail_gamma = circulation[0] * age_keep
        shed_gamma = circulation[1] * station_keep[:, None]
        stacked = jnp.concatenate(
            [nodes, trail_end, shed_end, trail_gamma[None], shed_gamma[None], core_radius[None]],
            axis=0,
        )
        return jnp.transpose(stacked.reshape(12, blocks_here, age_here), (1, 0, 2))

    payload, build_pullback = jax.vjp(build, positions, next_ages, next_stations, strengths)

    def to_rows(array):
        return jnp.transpose(array.reshape(array.shape[0], blocks_here, age_here), (1, 0, 2))

    def from_rows(array):
        return jnp.transpose(array, (1, 0, 2)).reshape(shape_here)

    target_blocks = to_rows(positions)
    seed_blocks = to_rows(adjoint_seed) * time_step
    owner_onehot = (owner_ids[:, None] == jnp.arange(group_size, dtype=jnp.int32)[None, :]).astype(
        jnp.int32
    )
    rank_within = jnp.sum((jnp.cumsum(owner_onehot, axis=0) - owner_onehot) * owner_onehot, axis=1)
    slot_index = owner_ids * capacity + rank_within
    request = (
        jnp.zeros((group_size * capacity,), jnp.int32)
        .at[slot_index]
        .set(source_ids)
        .reshape(group_size, capacity)
    )
    asked = lax.all_to_all(
        request, ("turb", "age"), split_axis=0, concat_axis=0, tiled=True
    ).reshape(group_size * capacity)
    pair_targets = target_blocks[target_ids]
    pair_seed = seed_blocks[target_ids]
    outgoing = (
        jnp.zeros((group_size * capacity, 6, age_here), jnp.float32)
        .at[slot_index]
        .set(jnp.concatenate([pair_targets, pair_seed], axis=1))
    )
    incoming = lax.all_to_all(
        outgoing.reshape(group_size, capacity, 6, age_here),
        ("turb", "age"),
        split_axis=0,
        concat_axis=0,
        tiled=True,
    )
    incoming = incoming.reshape(group_size * capacity, 6, age_here)
    slot_velocity, slot_grad, payload_terms = run_pairs(
        incoming[:, 0:3], payload[asked], incoming[:, 3:6]
    )
    results = jnp.concatenate([slot_velocity, slot_grad], axis=1).reshape(
        group_size, capacity, 6, age_here
    )
    answered = lax.all_to_all(
        results, ("turb", "age"), split_axis=0, concat_axis=0, tiled=True
    ).reshape(group_size * capacity, 6, age_here)[slot_index]
    pair_velocity = answered[:, 0:3]
    pair_grad = answered[:, 3:6]
    payload_grad = onehot_sum(asked, blocks_here, payload_terms)
    velocity = onehot_sum(target_ids, blocks_here, pair_velocity)
    target_grad = onehot_sum(target_ids, blocks_here, pair_grad)
    advected = positions + time_step * from_rows(velocity)
    advected = advected.at[0].add(time_step)
    grad_nodes, grad_after_age, grad_after_station, grad_strengths = build_pullback(payload_grad)
    from_prior_age = shifted_2(grad_after_age, "age", 1)
    from_prior_station = shifted_2(grad_after_station, "span", 1)
    grad_positions = adjoint_seed + grad_nodes + from_rows(target_grad)
    grad_positions = grad_positions.at[..., 0].add(from_prior_age)
    grad_positions = grad_positions.at[:, :, :, 0, :].add(from_prior_station)
    return (advected, grad_positions, grad_strengths)


TILE = 8


def cross(a, b):
    return (
        a[1] * b[2] - a[2] * b[1],
        a[2] * b[0] - a[0] * b[2],
        a[0] * b[1] - a[1] * b[0],
    )


def dot(a, b):
    return a[0] * b[0] + a[1] * b[1] + a[2] * b[2]


def segment(r0, r1, r2, inv1, along_sq, gamma, core_sq, quad, quart, inside, w):
    c = cross(r0, r1)
    c_sq = dot(c, c)
    a = dot(r0, r1)
    b = a - along_sq
    inv2 = lax.rsqrt(dot(r2, r2) + core_sq)
    proj = a * inv1 - b * inv2
    inv_d = lax.rsqrt(c_sq * c_sq + quart)
    inv_d = jnp.where(inside, inv_d, 0.0)
    q = dot(w, c)
    m = gamma * inv_d
    k = m * proj
    gp = m * q
    fd = (k * q) * (2.0 * (inv_d * inv_d))
    grad_gamma = proj * (q * inv_d)
    h = fd * c_sq
    gn2 = gp * b * (inv2 * inv2 * inv2)
    alpha = gp * (inv1 - inv2) - gn2
    delta = gp * (inv2 + inv2) - fd * quad + gn2
    gc = tuple(k * w[i] - h * c[i] for i in range(3))
    left = cross(gc, r0)
    right = cross(r1, gc)
    grad_r1 = tuple(left[i] + alpha * r0[i] for i in range(3))
    grad_r0 = tuple(right[i] + alpha * r1[i] for i in range(3))
    velocity = tuple(k * c[i] for i in range(3))
    return velocity, grad_r1, grad_r0, grad_gamma, delta, gn2, gp * a


def pair_tile(rows, ages):
    lane = lax.broadcasted_iota(jnp.int32, (TILE, ages), 1)
    begin = rows[0:3]
    core = rows[5]
    core_sq = core * core
    trail = [
        jnp.where(
            lane == ages - 1,
            pltpu.roll(rows[6 + i], ages - 1, 1),
            pltpu.roll(begin[i], ages - 1, 1),
        )
        for i in range(3)
    ]
    alongs = [[trail[i] - begin[i] for i in range(3)], [rows[9 + i] - begin[i] for i in range(3)]]
    gammas = [rows[3] * (1.0 / four_pi), rows[4] * (1.0 / four_pi)]
    core_quad = core_sq * core_sq
    alongs_sq = [dot(r0, r0) for r0 in alongs]
    lengths = [along_sq + core_sq for along_sq in alongs_sq]
    quads = [core_quad * length for length in lengths]
    quarts = [quad * length for quad, length in zip(quads, lengths)]
    zero = jnp.zeros((TILE, ages), jnp.float32)
    sum_r1 = [zero] * 3
    sum_r0 = [[zero] * 3, [zero] * 3]
    sum_gamma = [zero, zero]
    sum_delta = [zero, zero]
    out = [zero] * 6
    for offset in range(-REACH, REACH):
        shift = offset % ages
        moved = [pltpu.roll(x, shift, 1) if shift else x for x in rows[12:18]]
        target, w = moved[0:3], moved[3:6]
        if offset >= 0:
            inside = lane >= offset
        else:
            inside = lane < ages + offset
        r1 = [target[i] - begin[i] for i in range(3)]
        inv1 = lax.rsqrt(dot(r1, r1) + core_sq)
        beta = [None, None]
        ga = [None, None]
        vel = [None] * 3
        g1 = [None] * 3
        for kind in range(2):
            r0 = alongs[kind]
            r2 = [r1[i] - r0[i] for i in range(3)]
            v, d1, d0, dg, delta, beta[kind], ga[kind] = segment(
                r0, r1, r2, inv1, alongs_sq[kind], gammas[kind], core_sq,
                quads[kind], quarts[kind], inside, w,
            )
            vel = [v[i] if kind == 0 else vel[i] + v[i] for i in range(3)]
            g1 = [d1[i] if kind == 0 else g1[i] + d1[i] for i in range(3)]
            sum_r0[kind] = [sum_r0[kind][i] + d0[i] for i in range(3)]
            sum_gamma[kind] = sum_gamma[kind] + dg
            sum_delta[kind] = sum_delta[kind] + delta
        pull = (beta[0] + beta[1]) - (ga[0] + ga[1]) * (inv1 * inv1 * inv1)
        g1 = [g1[i] + pull * r1[i] for i in range(3)]
        sum_r1 = [sum_r1[i] + g1[i] for i in range(3)]
        back = (-offset) % ages
        both = vel + g1
        out = [out[i] + (pltpu.roll(both[i], back, 1) if back else both[i]) for i in range(6)]
    sum_r0 = [
        [sum_r0[kind][i] + sum_delta[kind] * alongs[kind][i] for i in range(3)] for kind in range(2)
    ]
    carry = zero
    grad_begin = []
    for i in range(3):
        moved = pltpu.roll(sum_r0[0][i], 1, 1)
        carry = jnp.where(lane == i, pltpu.roll(moved, i, 1) if i else moved, carry)
        moved = jnp.where(lane == 0, 0.0, moved)
        grad_begin.append(moved - (sum_r1[i] + sum_r0[0][i] + sum_r0[1][i]))
    gammas = [g * (1.0 / four_pi) for g in sum_gamma]
    return grad_begin + gammas + sum_r0[1] + [carry] + out


MESH = pl.DeviceIdType.MESH


def place():
    here = (lax.axis_index("turb"), lax.axis_index("age"), lax.axis_index("span"))
    spans = lax.axis_size("span")
    turb, age, span = here
    return (
        here,
        (1 - turb, age, span),
        (turb, age - 1, span),
        (turb, age + 1, span),
        (turb, age, lax.rem(span + spans - 1, spans)),
        (turb, age, lax.rem(span + 1, spans)),
    )


def greet(ages_count):
    here, other, below, above, prior, following = place()
    barrier = pltpu.get_barrier_semaphore()
    for device in (other, prior, following):
        pl.semaphore_signal(barrier, inc=1, device_id=device, device_id_type=MESH)

    @pl.when(here[1] > 0)
    def _():
        pl.semaphore_signal(barrier, inc=1, device_id=below, device_id_type=MESH)

    @pl.when(here[1] < ages_count - 1)
    def _():
        pl.semaphore_signal(barrier, inc=1, device_id=above, device_id_type=MESH)

    inner = (here[1] > 0).astype(jnp.int32) + (here[1] < ages_count - 1).astype(jnp.int32)
    pl.semaphore_wait(barrier, 3 + inner)


def keeps(stations, ages, shape):
    lane = lax.broadcasted_iota(jnp.int32, shape, 1)
    row = lax.broadcasted_iota(jnp.int32, shape, 0)
    last_age = lax.axis_index("age") == lax.axis_size("age") - 1
    last_station = lax.axis_index("span") == lax.axis_size("span") - 1
    trail = jnp.where(jnp.logical_and(last_age, lane == ages - 1), 0.0, 1.0)
    shed = jnp.where(jnp.logical_and(last_station, row % stations == stations - 1), 0.0, 1.0)
    return trail, shed


def gather_all(
    blocks, stations, per_owner, positions_ref, strengths_ref, core_ref, seed_ref, table_ref,
    strengths_buf, halo_buf, seed_buf, load_sems, halo_sems, send_sems, recv_sems,
):
    ages = table_ref.shape[-1]
    count = lax.axis_size("age")
    halo = blocks // stations
    here, other, below, above, prior, following = place()
    turb, age, span = here
    me = turb * count + age
    mate = (1 - turb) * count + age
    extra = per_owner - 6 * blocks
    parts = (
        (0, 3 * blocks),
        (3 * blocks, 2 * blocks),
        (5 * blocks, per_owner - 5 * blocks),
    )
    base = me * per_owner
    loads = [
        pltpu.make_async_copy(source, target, load_sems.at[k])
        for k, (source, target) in enumerate(
            (
                (positions_ref, table_ref.at[pl.ds(pl.multiple_of(base, 8), 3 * blocks)]),
                (strengths_ref, strengths_buf),
                (core_ref, table_ref.at[pl.ds(pl.multiple_of(base + 5 * blocks, 8), blocks)]),
                (seed_ref, seed_buf),
            )
        )
    ]
    for load in loads:
        load.start()
    halo_buf[...] = jnp.zeros_like(halo_buf)
    trail, shed = keeps(stations, ages, (blocks, ages))
    greet(count)

    def rows(owner, part):
        return pl.ds(pl.multiple_of(owner * per_owner + parts[part][0], 8), parts[part][1])

    def copy(owner, part, way):
        at = rows(owner, part)
        return pltpu.make_async_remote_copy(
            src_ref=table_ref.at[at],
            dst_ref=table_ref.at[at],
            send_sem=send_sems.at[way, part, owner],
            recv_sem=recv_sems.at[part, owner],
            device_id=(other, below, above)[way],
            device_id_type=MESH,
        )

    def arrive(owner, part):
        copy(owner, part, 0).wait_recv()

    has_below = age > 0
    has_above = age < count - 1

    def share(owner, part):
        @pl.when(has_below)
        def _():
            copy(owner, part, 1).start()

        @pl.when(has_above)
        def _():
            copy(owner, part, 2).start()

    loads[0].wait()
    share(me, 0)
    copy(me, 0, 0).start()
    for k in range(3 * halo):
        halo_buf[pl.ds(k, 1), :] = table_ref[pl.ds(base + k * stations, 1), :]
    halo_copy = pltpu.make_async_remote_copy(
        src_ref=halo_buf,
        dst_ref=table_ref.at[pl.ds(pl.multiple_of(base + 6 * blocks, 8), extra)],
        send_sem=halo_sems.at[0],
        recv_sem=halo_sems.at[1],
        device_id=prior,
        device_id_type=MESH,
    )
    halo_copy.start()
    loads[1].wait()
    table_ref[pl.ds(pl.multiple_of(base + 3 * blocks, 8), blocks), :] = (
        strengths_buf[pl.ds(0, blocks), :] * trail
    )
    table_ref[pl.ds(pl.multiple_of(base + 4 * blocks, 8), blocks), :] = (
        strengths_buf[pl.ds(blocks, blocks), :] * shed
    )
    share(me, 1)
    copy(me, 1, 0).start()
    loads[2].wait()
    loads[3].wait()
    halo_copy.wait_recv()
    copy(me, 2, 0).start()
    share(me, 2)
    arrive(mate, 2)
    share(mate, 2)
    for step in range(1, count):
        for part in range(3):
            for way, sign in ((2, -1), (1, 1)):
                source = age + sign * step
                onward = has_above if way == 2 else has_below

                @pl.when(source >= 0 if sign < 0 else source < count)
                def _(source=source, way=way, onward=onward, part=part):
                    for column in (turb, 1 - turb)[: 2 if part == 2 else 1]:
                        owner = column * count + source
                        arrive(owner, part)

                        @pl.when(onward)
                        def _(owner=owner):
                            copy(owner, part, way).start()

                        if part < 2:
                            copy(owner, part, 0).start()

    for source in range(count):
        for part in range(2):
            arrive((1 - turb) * count + source, part)
    def finish():
        halo_copy.wait_send()
        copy(me, 2, 0).wait_send()
        for source in range(count):
            sent = [(turb * count + source, part) for part in range(3)]
            sent.append(((1 - turb) * count + source, 2))
            for part in range(2):
                copy(sent[part][0], part, 0).wait_send()

            @pl.when(jnp.logical_and(source >= age, has_below))
            def _(sent=sent):
                for owner, part in sent:
                    copy(owner, part, 1).wait_send()

            @pl.when(jnp.logical_and(source <= age, has_above))
            def _(sent=sent):
                for owner, part in sent:
                    copy(owner, part, 2).wait_send()

    return finish


def exact_dot(selector, terms):
    return jnp.dot(
        jnp.concatenate([selector] * 3, axis=1), terms, preferred_element_type=jnp.float32
    )


def split_terms(value):
    high = value.astype(jnp.bfloat16)
    rest = value - high.astype(jnp.float32)
    middle = rest.astype(jnp.bfloat16)
    low = (rest - middle.astype(jnp.float32)).astype(jnp.bfloat16)
    return high, middle, low


def step_kernel(
    blocks, stations, per_owner, grad_rows, early, target_ref, owner_ref, source_ref,
    target_row, owner_row, source_row, positions_ref, strengths_ref, core_ref, seed_ref,
    moved_ref, positions_grad_ref, strengths_grad_ref,
    table_ref, strengths_buf, halo_buf, seed_buf, rows_buf, values, terms, grads_ref, base_ref,
    work, from_mate, from_below, from_above, late_in, halo_out, halo_in,
    load_sems, start_sems, send_sems, recv_sems,
    mate_sems, chain_send, chain_recv, late_sems, halo_sems,
):
    ages = grads_ref.shape[-1]
    count = lax.axis_size("age")
    halo = blocks // stations
    here, other, below, above, prior, following = place()
    turb, age, span = here
    late = grad_rows - early
    half = (early + 2 * late) // 16 * 8
    cut = half - 2 * late
    pieces = ((0, cut), (cut, early - cut))
    group = 2 * count
    pairs = target_ref.shape[0]
    me = turb * count + age
    own_rows = me * per_owner

    finish = gather_all(
        blocks, stations, per_owner, positions_ref, strengths_ref, core_ref, seed_ref, table_ref,
        strengths_buf, halo_buf, seed_buf, load_sems, start_sems, send_sems, recv_sems,
    )

    def fetch(t):
        for j in range(TILE):
            p = t * TILE + j
            tgt = target_ref[p]
            owner = owner_ref[p]
            block = source_ref[p]
            src = owner * per_owner + block
            nxt = jnp.where(owner == group - 1, 0, owner + 1) * per_owner + block
            inner = lax.rem(block, stations) < stations - 1
            shed = jnp.where(inner, src + 1, owner * per_owner + 6 * blocks + lax.div(block, stations))
            shed_step = jnp.where(inner, blocks, halo)
            own = own_rows + tgt
            for r in range(6):
                rows_buf[pl.ds(r * TILE + j, 1), :] = table_ref[pl.ds(src + r * blocks, 1), :]
            for r in range(3):
                rows_buf[pl.ds((6 + r) * TILE + j, 1), :] = table_ref[pl.ds(nxt + r * blocks, 1), :]
                rows_buf[pl.ds((9 + r) * TILE + j, 1), :] = table_ref[pl.ds(shed + r * shed_step, 1), :]
                rows_buf[pl.ds((12 + r) * TILE + j, 1), :] = table_ref[pl.ds(own + r * blocks, 1), :]
                rows_buf[pl.ds((15 + r) * TILE + j, 1), :] = seed_buf[pl.ds(tgt + r * blocks, 1), :]

    def tile(t, _):
        rows = [rows_buf[pl.ds(r * TILE, TILE), :] for r in range(18)]
        rows[15:18] = [seed * time_step for seed in rows[15:18]]
        fetch(jnp.minimum(t + 1, pairs // TILE - 1))
        for r, value in enumerate(pair_tile(rows, ages)):
            values[pl.ds(pl.multiple_of(t * TILE, TILE), TILE), pl.ds(r * ages, ages)] = value
        return 0

    fetch(0)
    lax.fori_loop(0, pairs // TILE, tile, 0)
    for k, term in enumerate(split_terms(values[...])):
        terms[pl.ds(k * pairs, pairs), :] = term

    def select(rows, chosen, which):
        row = lax.broadcasted_iota(jnp.int32, (rows, pairs), 0)
        hit = jnp.logical_and(row == chosen, which)
        return jnp.where(hit, 1.0, 0.0).astype(jnp.bfloat16)

    def columns(first, number):
        return terms[:, pl.ds(first * ages, number * ages)]

    owners = owner_row[...]
    sources = source_row[...]
    followers = jnp.where(owners == group - 1, 0, owners + 1)
    inner_row = sources % stations < stations - 1
    lane_first = lax.broadcasted_iota(jnp.int32, (blocks, ages), 1) == 0
    extra = grad_rows - 5 * blocks

    def scatter(column, dest):
        owner = column * count + dest
        from_here = owners == owner
        main = exact_dot(select(blocks, sources, from_here), columns(0, 5))
        inner_shed = exact_dot(
            select(blocks, sources + 1, jnp.logical_and(from_here, inner_row)), columns(5, 3)
        )
        outer_shed = exact_dot(
            select(
                -(-halo // 8) * 8,
                sources // stations,
                jnp.logical_and(from_here, jnp.logical_not(inner_row)),
            ),
            columns(5, 3),
        )
        carry = exact_dot(select(blocks, sources, followers == owner), columns(8, 1))
        for r in range(5):
            value = main[:, r * ages : (r + 1) * ages]
            if r < 3:
                lane0 = pltpu.roll(carry, ages - r, 1) if r else carry
                value = value + inner_shed[:, r * ages : (r + 1) * ages]
                value = value + jnp.where(lane_first, lane0, 0.0)
            grads_ref[part(column, dest, r * blocks, blocks), :] = value
        outer = [outer_shed[0:halo, r * ages : (r + 1) * ages] for r in range(3)]
        if extra > 3 * halo:
            outer.append(jnp.zeros((extra - 3 * halo, ages), jnp.float32))
        grads_ref[part(column, dest, 5 * blocks, extra), :] = jnp.concatenate(outer)
    spans = ((0, half), (half, early + 2 * late - half))
    has_below = age > 0
    has_above = age < count - 1

    def part(column, dest, start, number):
        owner = column * count + dest
        return pl.ds(pl.multiple_of(owner * grad_rows + start, 8), number)

    def mate_copy(dest, piece):
        return pltpu.make_async_remote_copy(
            src_ref=grads_ref.at[part(1 - turb, dest, *pieces[piece])],
            dst_ref=from_mate.at[dest, pl.ds(*pieces[piece])],
            send_sem=mate_sems.at[0, dest, piece],
            recv_sem=mate_sems.at[1, dest, piece],
            device_id=other,
            device_id_type=MESH,
        )

    def chain_copy(dest, piece, upward):
        at = pl.ds(*spans[piece])
        return pltpu.make_async_remote_copy(
            src_ref=work.at[dest, at],
            dst_ref=(from_below if upward else from_above).at[dest, at],
            send_sem=chain_send.at[dest, piece],
            recv_sem=chain_recv.at[0 if upward else 1, dest, piece],
            device_id=above if upward else below,
            device_id_type=MESH,
        )

    order = [jnp.int32(0)] * count
    rank = jnp.int32(0)
    for distance in range(count - 1, -1, -1):
        for sign in (1, -1) if distance else (1,):
            dest = age + sign * distance
            valid = jnp.logical_and(dest >= 0, dest < count)
            order = [
                jnp.where(jnp.logical_and(valid, rank == k), dest, order[k]) for k in range(count)
            ]
            rank = rank + valid.astype(jnp.int32)
    steps = [(order[k], piece) for k in range(count) for piece in range(2)]

    scatter(1 - turb, order[0])
    mate_copy(*steps[0]).start()
    mate_copy(*steps[1]).start()

    def take(number):
        dest, piece = steps[number]
        if piece == 0:
            scatter(turb, dest)
            if number + 2 < len(steps):
                scatter(1 - turb, steps[number + 2][0])
        mate_copy(dest, piece).wait_recv()
        if number + 2 < len(steps):
            mate_copy(*steps[number + 2]).start()
        start, size = pieces[piece]
        if piece == 0:
            work[dest, pl.ds(0, late), :] = grads_ref[part(turb, dest, early, late), :]
            work[dest, pl.ds(late, late), :] = grads_ref[part(1 - turb, dest, early, late), :]
        work[dest, pl.ds(2 * late + start, size), :] = (
            grads_ref[part(turb, dest, start, size), :] + from_mate[dest, pl.ds(start, size), :]
        )
        at = pl.ds(*spans[piece])

        @pl.when(jnp.logical_and(dest >= age, has_below))
        def _():
            chain_copy(dest, piece, True).wait_recv()
            work[dest, at, :] = work[dest, at, :] + from_below[dest, at, :]

        @pl.when(jnp.logical_and(dest <= age, has_above))
        def _():
            chain_copy(dest, piece, False).wait_recv()
            work[dest, at, :] = work[dest, at, :] + from_above[dest, at, :]

        pl.when(dest > age)(lambda: chain_copy(dest, piece, True).start())
        pl.when(dest < age)(lambda: chain_copy(dest, piece, False).start())

    take(0)
    target_sums = exact_dot(select(blocks, target_row[...], target_row[...] >= 0), columns(9, 6))
    for c in range(3):
        at = pl.ds(c * blocks, blocks)
        velocity = target_sums[:, c * ages : (c + 1) * ages]
        moved_ref[at, :] = time_step * (velocity + 1.0 if c == 0 else velocity)
        base_ref[at, :] = target_sums[:, (3 + c) * ages : (4 + c) * ages]
    for number in range(1, len(steps) - 1):
        take(number)
    late_copy = pltpu.make_async_remote_copy(
        src_ref=work.at[age, pl.ds(late, late)],
        dst_ref=late_in,
        send_sem=late_sems.at[0],
        recv_sem=late_sems.at[1],
        device_id=other,
        device_id_type=MESH,
    )
    late_copy.start()
    late_copy.wait_recv()
    work[age, pl.ds(0, late), :] = work[age, pl.ds(0, late), :] + late_in[...]
    halo_out[...] = work[age, pl.ds(5 * blocks - early, grad_rows - 5 * blocks), :]
    halo_copy = pltpu.make_async_remote_copy(
        src_ref=halo_out,
        dst_ref=halo_in,
        send_sem=halo_sems.at[0],
        recv_sem=halo_sems.at[1],
        device_id=following,
        device_id_type=MESH,
    )
    halo_copy.start()
    trail, shed = keeps(stations, ages, (2 * blocks, ages))
    row = lax.broadcasted_iota(jnp.int32, (2 * blocks, ages), 0)
    keep = jnp.where(row < blocks, trail, shed)
    first = early - 3 * blocks
    strengths_grad_ref[pl.ds(first, 2 * blocks - first), :] = (
        work[age, pl.ds(0, 2 * blocks - first), :] * keep[first:]
    )
    take(len(steps) - 1)
    strengths_grad_ref[pl.ds(0, first), :] = (
        work[age, pl.ds(2 * late + 3 * blocks, first), :] * keep[:first]
    )
    positions_grad_ref[...] = base_ref[...] + work[age, pl.ds(2 * late, 3 * blocks), :]
    halo_copy.wait_recv()
    for k in range(3 * halo):
        at = pl.ds(k * stations, 1)
        positions_grad_ref[at, :] = positions_grad_ref[at, :] + halo_in[pl.ds(k, 1), :]
    finish()
    late_copy.wait_send()
    halo_copy.wait_send()
    for dest in range(count):
        for piece in range(2):
            mate_copy(dest, piece).wait_send()
            pl.when(dest > age)(lambda d=dest, p=piece: chain_copy(d, p, True).wait_send())
            pl.when(dest < age)(lambda d=dest, p=piece: chain_copy(d, p, False).wait_send())


def local_dense(positions, strengths, core_radius, adjoint_seed, pair_target, pair_owner, pair_source):
    shape_here = positions.shape
    stations = shape_here[3]
    ages = shape_here[4]
    blocks = shape_here[1] * shape_here[2] * stations
    halo = blocks // stations
    count = lax.axis_size("age")
    group = lax.axis_size("turb") * count
    pairs = pair_target.shape[-1]
    per_owner = -(-(6 * blocks + 3 * halo) // 8) * 8
    grad_rows = -(-(5 * blocks + 3 * halo) // 8) * 8
    early = grad_rows * 5 // 6 // 8 * 8
    late = grad_rows - early
    extra = grad_rows - 5 * blocks
    vmem = pl.BlockSpec(memory_space=pltpu.VMEM)
    smem = pl.BlockSpec(memory_space=pltpu.SMEM)
    kept = pl.BlockSpec(memory_space=pl.ANY)
    dma = pltpu.SemaphoreType.DMA
    rows_out = jax.ShapeDtypeStruct((3 * blocks, ages), jnp.float32)

    def room(*shape):
        return pltpu.VMEM(shape + (ages,), jnp.float32)

    lists = (pair_target, pair_owner, pair_source)
    moved, grad_moved, grad_strengths = pl.pallas_call(
        functools.partial(step_kernel, blocks, stations, per_owner, grad_rows, early),
        out_shape=(rows_out, rows_out, jax.ShapeDtypeStruct((2 * blocks, ages), jnp.float32)),
        in_specs=[smem] * 3 + [vmem] * 3 + [kept] * 4,
        out_specs=(vmem, vmem, vmem),
        scratch_shapes=[
            room(group * per_owner),
            room(2 * blocks),
            room(per_owner - 6 * blocks),
            room(3 * blocks),
            room(18 * TILE),
            pltpu.VMEM((pairs, 15 * ages), jnp.float32),
            pltpu.VMEM((3 * pairs, 15 * ages), jnp.bfloat16),
            room(group * grad_rows),
            room(3 * blocks),
            room(count, early + 2 * late),
            room(count, early),
            room(count, early + 2 * late),
            room(count, early + 2 * late),
            room(late),
            room(extra),
            room(extra),
            dma((4,)),
            dma((2,)),
            dma((3, 3, group)),
            dma((3, group)),
            dma((2, count, 2)),
            dma((count, 2)),
            dma((2, count, 2)),
            dma((2,)),
            dma((2,)),
        ],
        compiler_params=pltpu.CompilerParams(
            collective_id=0, has_side_effects=True, vmem_limit_bytes=60 * 1024 * 1024
        ),
    )(
        *[pair.reshape(pairs) for pair in lists],
        *[pair.reshape(1, pairs) for pair in lists],
        positions.reshape(3 * blocks, ages),
        strengths.reshape(2 * blocks, ages),
        core_radius.reshape(blocks, ages),
        adjoint_seed.reshape(3 * blocks, ages),
    )
    return (
        positions + moved.reshape(shape_here),
        adjoint_seed + grad_moved.reshape(shape_here),
        grad_strengths.reshape(strengths.shape),
    )


def local(positions, strengths, core_radius, adjoint_seed, pair_target, pair_owner, pair_source):
    blocks = positions.shape[1] * positions.shape[2] * positions.shape[3]
    group = lax.axis_size("turb") * lax.axis_size("age")
    fits = lax.axis_size("turb") == 2 and lax.axis_size("span") > 2 and lax.axis_size("age") > 1
    dense = fits and group * blocks <= 8 * pair_target.shape[-1]
    chosen = local_dense if dense else local_sparse
    return chosen(
        positions, strengths, core_radius, adjoint_seed, pair_target, pair_owner, pair_source
    )


def solution(mesh):
    placed = (
        P(None, "turb", None, "span", "age"),
        P(None, "turb", None, "span", "age"),
        P("turb", None, "span", "age"),
        P(None, "turb", None, "span", "age"),
        P("turb", "age", "span", None),
        P("turb", "age", "span", None),
        P("turb", "age", "span", None),
    )
    return jax.shard_map(
        local,
        mesh=mesh,
        in_specs=placed,
        out_specs=(
            P(None, "turb", None, "span", "age"),
            P(None, "turb", None, "span", "age"),
            P(None, "turb", None, "span", "age"),
        ),
        check_vma=False,
    )
```

```python
import functools
import math

import jax
import jax.numpy as jnp
from jax import lax
from jax.experimental import pallas as pl
from jax.experimental.pallas import tpu as pltpu
from jax.sharding import PartitionSpec as P

REACH = 8


time_step = 0.5
four_pi = 4.0 * math.pi
batch_rows = 16


def shifted_2(value, axis, steps):
    count = lax.axis_size(axis)
    leading, last = (max(0, -steps), min(count, count - steps))
    return lax.ppermute(value, axis, [(source, source + steps) for source in range(leading, last)])


def windows(payload):
    age_count = payload.shape[-1]
    padded = jnp.pad(payload, ((0, 0), (0, 0), (REACH, REACH)))
    stacked = jnp.stack(
        [
            padded[:, :, REACH + offset : REACH + offset + age_count]
            for offset in range(-REACH, REACH)
        ]
    )
    shifted = (
        jnp.arange(-REACH, REACH, dtype=jnp.int32)[:, None]
        + jnp.arange(age_count, dtype=jnp.int32)[None, :]
    )
    inside = ((shifted >= 0) & (shifted < age_count)).astype(payload.dtype)
    return (stacked, inside)


def induced(targets, payload):
    stacked, inside = windows(payload)
    begins = stacked[:, :, 0:3]
    end_points = jnp.stack([stacked[:, :, 3:6], stacked[:, :, 6:9]])
    gammas = jnp.stack([stacked[:, :, 9], stacked[:, :, 10]]) * inside[None, :, None, :]
    core = jnp.where(inside[:, None, :] > 0, stacked[:, :, 11], 1.0)
    core_sq = core * core
    core_quad = core_sq * core_sq
    from_begin = targets[None] - begins
    from_end = targets[None, None] - end_points
    along = end_points - begins[None]
    near = from_begin[None]
    cross_x = near[..., 1, :] * from_end[..., 2, :] - near[..., 2, :] * from_end[..., 1, :]
    cross_y = near[..., 2, :] * from_end[..., 0, :] - near[..., 0, :] * from_end[..., 2, :]
    cross_z = near[..., 0, :] * from_end[..., 1, :] - near[..., 1, :] * from_end[..., 0, :]
    cross_sq = cross_x * cross_x + cross_y * cross_y + cross_z * cross_z
    length_sq = jnp.sum(along * along, axis=-2) + core_sq
    dist_begin = jnp.sqrt(jnp.sum(from_begin * from_begin, axis=-2) + core_sq)
    dist_end = jnp.sqrt(jnp.sum(from_end * from_end, axis=-2) + core_sq)
    projected = jnp.sum(
        along * (near / dist_begin[None, :, :, None, :] - from_end / dist_end[..., None, :]),
        axis=-2,
    )
    factor = (
        gammas
        * projected
        / (four_pi * jnp.sqrt(cross_sq * cross_sq + core_quad * length_sq * length_sq))
    )
    return jnp.stack(
        [
            jnp.sum(cross_x * factor, axis=(0, 1)),
            jnp.sum(cross_y * factor, axis=(0, 1)),
            jnp.sum(cross_z * factor, axis=(0, 1)),
        ],
        axis=1,
    )


def run_pairs(targets, payload, cotangent):
    number = targets.shape[0]
    age_count = targets.shape[-1]

    def one_batch(operands):
        velocity, pullback = jax.vjp(induced, operands[0], operands[1])
        grad_targets, grad_payload = pullback(operands[2])
        return (velocity, grad_targets, grad_payload)

    shaped = (
        targets.reshape(number // batch_rows, batch_rows, 3, age_count),
        payload.reshape(number // batch_rows, batch_rows, 12, age_count),
        cotangent.reshape(number // batch_rows, batch_rows, 3, age_count),
    )
    velocity, grad_targets, grad_payload = lax.map(one_batch, shaped)
    return (
        velocity.reshape(number, 3, age_count),
        grad_targets.reshape(number, 3, age_count),
        grad_payload.reshape(number, 12, age_count),
    )


def onehot_sum(indices, rows, values):
    selector = (jnp.arange(rows, dtype=jnp.int32)[:, None] == indices[None, :]).astype(jnp.float32)
    flat = values.reshape(values.shape[0], -1)
    summed = jnp.dot(
        selector, flat, precision=lax.Precision.HIGHEST, preferred_element_type=jnp.float32
    )
    return summed.reshape((rows,) + values.shape[1:])


def local_sparse(positions, strengths, core_radius, adjoint_seed, pair_target, pair_owner, pair_source):
    shape_here = positions.shape
    station_here = shape_here[3]
    age_here = shape_here[4]
    blocks_here = shape_here[1] * shape_here[2] * station_here
    group_size = lax.axis_size("turb") * lax.axis_size("age")
    pair_count = pair_target.shape[-1]
    capacity = 2 * pair_count // group_size
    target_ids = pair_target.reshape(pair_count)
    owner_ids = pair_owner.reshape(pair_count)
    source_ids = pair_source.reshape(pair_count)
    next_ages = shifted_2(positions[..., 0], "age", -1)
    next_stations = shifted_2(positions[:, :, :, 0, :], "span", -1)
    age_keep = (
        lax.axis_index("age") * age_here + jnp.arange(age_here, dtype=jnp.int32)
        < age_here * lax.axis_size("age") - 1
    ).astype(jnp.float32)
    station_keep = (
        lax.axis_index("span") * station_here + jnp.arange(station_here, dtype=jnp.int32)
        < station_here * lax.axis_size("span") - 1
    ).astype(jnp.float32)

    def build(nodes, after_age, after_station, circulation):
        trail_end = jnp.concatenate([nodes[..., 1:], after_age[..., None]], axis=-1)
        shed_end = jnp.concatenate([nodes[:, :, :, 1:, :], after_station[:, :, :, None, :]], axis=3)
        trail_gamma = circulation[0] * age_keep
        shed_gamma = circulation[1] * station_keep[:, None]
        stacked = jnp.concatenate(
            [nodes, trail_end, shed_end, trail_gamma[None], shed_gamma[None], core_radius[None]],
            axis=0,
        )
        return jnp.transpose(stacked.reshape(12, blocks_here, age_here), (1, 0, 2))

    payload, build_pullback = jax.vjp(build, positions, next_ages, next_stations, strengths)

    def to_rows(array):
        return jnp.transpose(array.reshape(array.shape[0], blocks_here, age_here), (1, 0, 2))

    def from_rows(array):
        return jnp.transpose(array, (1, 0, 2)).reshape(shape_here)

    target_blocks = to_rows(positions)
    seed_blocks = to_rows(adjoint_seed) * time_step
    owner_onehot = (owner_ids[:, None] == jnp.arange(group_size, dtype=jnp.int32)[None, :]).astype(
        jnp.int32
    )
    rank_within = jnp.sum((jnp.cumsum(owner_onehot, axis=0) - owner_onehot) * owner_onehot, axis=1)
    slot_index = owner_ids * capacity + rank_within
    request = (
        jnp.zeros((group_size * capacity,), jnp.int32)
        .at[slot_index]
        .set(source_ids)
        .reshape(group_size, capacity)
    )
    asked = lax.all_to_all(
        request, ("turb", "age"), split_axis=0, concat_axis=0, tiled=True
    ).reshape(group_size * capacity)
    pair_targets = target_blocks[target_ids]
    pair_seed = seed_blocks[target_ids]
    outgoing = (
        jnp.zeros((group_size * capacity, 6, age_here), jnp.float32)
        .at[slot_index]
        .set(jnp.concatenate([pair_targets, pair_seed], axis=1))
    )
    incoming = lax.all_to_all(
        outgoing.reshape(group_size, capacity, 6, age_here),
        ("turb", "age"),
        split_axis=0,
        concat_axis=0,
        tiled=True,
    )
    incoming = incoming.reshape(group_size * capacity, 6, age_here)
    slot_velocity, slot_grad, payload_terms = run_pairs(
        incoming[:, 0:3], payload[asked], incoming[:, 3:6]
    )
    results = jnp.concatenate([slot_velocity, slot_grad], axis=1).reshape(
        group_size, capacity, 6, age_here
    )
    answered = lax.all_to_all(
        results, ("turb", "age"), split_axis=0, concat_axis=0, tiled=True
    ).reshape(group_size * capacity, 6, age_here)[slot_index]
    pair_velocity = answered[:, 0:3]
    pair_grad = answered[:, 3:6]
    payload_grad = onehot_sum(asked, blocks_here, payload_terms)
    velocity = onehot_sum(target_ids, blocks_here, pair_velocity)
    target_grad = onehot_sum(target_ids, blocks_here, pair_grad)
    advected = positions + time_step * from_rows(velocity)
    advected = advected.at[0].add(time_step)
    grad_nodes, grad_after_age, grad_after_station, grad_strengths = build_pullback(payload_grad)
    from_prior_age = shifted_2(grad_after_age, "age", 1)
    from_prior_station = shifted_2(grad_after_station, "span", 1)
    grad_positions = adjoint_seed + grad_nodes + from_rows(target_grad)
    grad_positions = grad_positions.at[..., 0].add(from_prior_age)
    grad_positions = grad_positions.at[:, :, :, 0, :].add(from_prior_station)
    return (advected, grad_positions, grad_strengths)


TILE = 8


def cross(a, b):
    return (
        a[1] * b[2] - a[2] * b[1],
        a[2] * b[0] - a[0] * b[2],
        a[0] * b[1] - a[1] * b[0],
    )


def dot(a, b):
    return a[0] * b[0] + a[1] * b[1] + a[2] * b[2]


def segment(r0, r1, r2, inv1, along_sq, gamma, core_sq, quad, quart, inside, w):
    c = cross(r0, r1)
    c_sq = dot(c, c)
    a = dot(r0, r1)
    b = a - along_sq
    inv2 = lax.rsqrt(dot(r2, r2) + core_sq)
    proj = a * inv1 - b * inv2
    inv_d = lax.rsqrt(c_sq * c_sq + quart)
    inv_d = jnp.where(inside, inv_d, 0.0)
    q = dot(w, c)
    m = gamma * inv_d
    k = m * proj
    gp = m * q
    fd = (k * q) * (2.0 * (inv_d * inv_d))
    grad_gamma = proj * (q * inv_d)
    h = fd * c_sq
    gn2 = gp * b * (inv2 * inv2 * inv2)
    alpha = gp * (inv1 - inv2) - gn2
    delta = gp * (inv2 + inv2) - fd * quad + gn2
    gc = tuple(k * w[i] - h * c[i] for i in range(3))
    left = cross(gc, r0)
    right = cross(r1, gc)
    grad_r1 = tuple(left[i] + alpha * r0[i] for i in range(3))
    grad_r0 = tuple(right[i] + alpha * r1[i] for i in range(3))
    velocity = tuple(k * c[i] for i in range(3))
    return velocity, grad_r1, grad_r0, grad_gamma, delta, gn2, gp * a


def pair_tile(rows, ages):
    lane = lax.broadcasted_iota(jnp.int32, (TILE, ages), 1)
    begin = rows[0:3]
    core = rows[5]
    core_sq = core * core
    trail = [
        jnp.where(
            lane == ages - 1,
            pltpu.roll(rows[6 + i], ages - 1, 1),
            pltpu.roll(begin[i], ages - 1, 1),
        )
        for i in range(3)
    ]
    alongs = [[trail[i] - begin[i] for i in range(3)], [rows[9 + i] - begin[i] for i in range(3)]]
    gammas = [rows[3] * (1.0 / four_pi), rows[4] * (1.0 / four_pi)]
    core_quad = core_sq * core_sq
    alongs_sq = [dot(r0, r0) for r0 in alongs]
    lengths = [along_sq + core_sq for along_sq in alongs_sq]
    quads = [core_quad * length for length in lengths]
    quarts = [quad * length for quad, length in zip(quads, lengths)]
    zero = jnp.zeros((TILE, ages), jnp.float32)
    sum_r1 = [zero] * 3
    sum_r0 = [[zero] * 3, [zero] * 3]
    sum_gamma = [zero, zero]
    sum_delta = [zero, zero]
    out = [zero] * 6
    for offset in range(-REACH, REACH):
        shift = offset % ages
        moved = [pltpu.roll(x, shift, 1) if shift else x for x in rows[12:18]]
        target, w = moved[0:3], moved[3:6]
        if offset >= 0:
            inside = lane >= offset
        else:
            inside = lane < ages + offset
        r1 = [target[i] - begin[i] for i in range(3)]
        inv1 = lax.rsqrt(dot(r1, r1) + core_sq)
        beta = [None, None]
        ga = [None, None]
        vel = [None] * 3
        g1 = [None] * 3
        for kind in range(2):
            r0 = alongs[kind]
            r2 = [r1[i] - r0[i] for i in range(3)]
            v, d1, d0, dg, delta, beta[kind], ga[kind] = segment(
                r0, r1, r2, inv1, alongs_sq[kind], gammas[kind], core_sq,
                quads[kind], quarts[kind], inside, w,
            )
            vel = [v[i] if kind == 0 else vel[i] + v[i] for i in range(3)]
            g1 = [d1[i] if kind == 0 else g1[i] + d1[i] for i in range(3)]
            sum_r0[kind] = [sum_r0[kind][i] + d0[i] for i in range(3)]
            sum_gamma[kind] = sum_gamma[kind] + dg
            sum_delta[kind] = sum_delta[kind] + delta
        pull = (beta[0] + beta[1]) - (ga[0] + ga[1]) * (inv1 * inv1 * inv1)
        g1 = [g1[i] + pull * r1[i] for i in range(3)]
        sum_r1 = [sum_r1[i] + g1[i] for i in range(3)]
        back = (-offset) % ages
        both = vel + g1
        out = [out[i] + (pltpu.roll(both[i], back, 1) if back else both[i]) for i in range(6)]
    sum_r0 = [
        [sum_r0[kind][i] + sum_delta[kind] * alongs[kind][i] for i in range(3)] for kind in range(2)
    ]
    carry = zero
    grad_begin = []
    for i in range(3):
        moved = pltpu.roll(sum_r0[0][i], 1, 1)
        carry = jnp.where(lane == i, pltpu.roll(moved, i, 1) if i else moved, carry)
        moved = jnp.where(lane == 0, 0.0, moved)
        grad_begin.append(moved - (sum_r1[i] + sum_r0[0][i] + sum_r0[1][i]))
    gammas = [g * (1.0 / four_pi) for g in sum_gamma]
    return grad_begin + gammas + sum_r0[1] + [carry] + out


MESH = pl.DeviceIdType.MESH


def place():
    here = (lax.axis_index("turb"), lax.axis_index("age"), lax.axis_index("span"))
    spans = lax.axis_size("span")
    turb, age, span = here
    return (
        here,
        (1 - turb, age, span),
        (turb, age - 1, span),
        (turb, age + 1, span),
        (turb, age, lax.rem(span + spans - 1, spans)),
        (turb, age, lax.rem(span + 1, spans)),
    )


def greet(ages_count):
    here, other, below, above, prior, following = place()
    barrier = pltpu.get_barrier_semaphore()
    for device in (other, prior, following):
        pl.semaphore_signal(barrier, inc=1, device_id=device, device_id_type=MESH)

    @pl.when(here[1] > 0)
    def _():
        pl.semaphore_signal(barrier, inc=1, device_id=below, device_id_type=MESH)

    @pl.when(here[1] < ages_count - 1)
    def _():
        pl.semaphore_signal(barrier, inc=1, device_id=above, device_id_type=MESH)

    inner = (here[1] > 0).astype(jnp.int32) + (here[1] < ages_count - 1).astype(jnp.int32)
    pl.semaphore_wait(barrier, 3 + inner)


def keeps(stations, ages, shape):
    lane = lax.broadcasted_iota(jnp.int32, shape, 1)
    row = lax.broadcasted_iota(jnp.int32, shape, 0)
    last_age = lax.axis_index("age") == lax.axis_size("age") - 1
    last_station = lax.axis_index("span") == lax.axis_size("span") - 1
    trail = jnp.where(jnp.logical_and(last_age, lane == ages - 1), 0.0, 1.0)
    shed = jnp.where(jnp.logical_and(last_station, row % stations == stations - 1), 0.0, 1.0)
    return trail, shed


def gather_all(
    blocks, stations, per_owner, positions_ref, strengths_ref, core_ref, seed_ref, table_ref,
    strengths_buf, halo_buf, seed_buf, load_sems, halo_sems, send_sems, recv_sems,
):
    ages = table_ref.shape[-1]
    count = lax.axis_size("age")
    halo = blocks // stations
    here, other, below, above, prior, following = place()
    turb, age, span = here
    me = turb * count + age
    mate = (1 - turb) * count + age
    extra = per_owner - 6 * blocks
    parts = (
        (0, 3 * blocks),
        (3 * blocks, 2 * blocks),
        (5 * blocks, per_owner - 5 * blocks),
    )
    base = me * per_owner
    loads = [
        pltpu.make_async_copy(source, target, load_sems.at[k])
        for k, (source, target) in enumerate(
            (
                (positions_ref, table_ref.at[pl.ds(pl.multiple_of(base, 8), 3 * blocks)]),
                (strengths_ref, strengths_buf),
                (core_ref, table_ref.at[pl.ds(pl.multiple_of(base + 5 * blocks, 8), blocks)]),
                (seed_ref, seed_buf),
            )
        )
    ]
    for load in loads:
        load.start()
    halo_buf[...] = jnp.zeros_like(halo_buf)
    trail, shed = keeps(stations, ages, (blocks, ages))
    greet(count)

    def rows(owner, part):
        return pl.ds(pl.multiple_of(owner * per_owner + parts[part][0], 8), parts[part][1])

    def copy(owner, part, way):
        at = rows(owner, part)
        return pltpu.make_async_remote_copy(
            src_ref=table_ref.at[at],
            dst_ref=table_ref.at[at],
            send_sem=send_sems.at[way, part, owner],
            recv_sem=recv_sems.at[part, owner],
            device_id=(other, below, above)[way],
            device_id_type=MESH,
        )

    def arrive(owner, part):
        copy(owner, part, 0).wait_recv()

    has_below = age > 0
    has_above = age < count - 1

    def share(owner, part):
        @pl.when(has_below)
        def _():
            copy(owner, part, 1).start()

        @pl.when(has_above)
        def _():
            copy(owner, part, 2).start()

    loads[0].wait()
    share(me, 0)
    copy(me, 0, 0).start()
    for k in range(3 * halo):
        halo_buf[pl.ds(k, 1), :] = table_ref[pl.ds(base + k * stations, 1), :]
    halo_copy = pltpu.make_async_remote_copy(
        src_ref=halo_buf,
        dst_ref=table_ref.at[pl.ds(pl.multiple_of(base + 6 * blocks, 8), extra)],
        send_sem=halo_sems.at[0],
        recv_sem=halo_sems.at[1],
        device_id=prior,
        device_id_type=MESH,
    )
    halo_copy.start()
    loads[1].wait()
    table_ref[pl.ds(pl.multiple_of(base + 3 * blocks, 8), blocks), :] = (
        strengths_buf[pl.ds(0, blocks), :] * trail
    )
    table_ref[pl.ds(pl.multiple_of(base + 4 * blocks, 8), blocks), :] = (
        strengths_buf[pl.ds(blocks, blocks), :] * shed
    )
    share(me, 1)
    copy(me, 1, 0).start()
    loads[2].wait()
    loads[3].wait()
    halo_copy.wait_recv()
    copy(me, 2, 0).start()
    share(me, 2)
    arrive(mate, 2)
    share(mate, 2)
    for step in range(1, count):
        for part in range(3):
            for way, sign in ((2, -1), (1, 1)):
                source = age + sign * step
                onward = has_above if way == 2 else has_below

                @pl.when(source >= 0 if sign < 0 else source < count)
                def _(source=source, way=way, onward=onward, part=part):
                    for column in (turb, 1 - turb)[: 2 if part == 2 else 1]:
                        owner = column * count + source
                        arrive(owner, part)

                        @pl.when(onward)
                        def _(owner=owner):
                            copy(owner, part, way).start()

                        if part < 2:
                            copy(owner, part, 0).start()

    for source in range(count):
        for part in range(2):
            arrive((1 - turb) * count + source, part)
    def finish():
        halo_copy.wait_send()
        copy(me, 2, 0).wait_send()
        for source in range(count):
            sent = [(turb * count + source, part) for part in range(3)]
            sent.append(((1 - turb) * count + source, 2))
            for part in range(2):
                copy(sent[part][0], part, 0).wait_send()

            @pl.when(jnp.logical_and(source >= age, has_below))
            def _(sent=sent):
                for owner, part in sent:
                    copy(owner, part, 1).wait_send()

            @pl.when(jnp.logical_and(source <= age, has_above))
            def _(sent=sent):
                for owner, part in sent:
                    copy(owner, part, 2).wait_send()

    return finish


def exact_dot(selector, terms):
    return jnp.dot(
        jnp.concatenate([selector] * 3, axis=1), terms, preferred_element_type=jnp.float32
    )


def split_terms(value):
    high = value.astype(jnp.bfloat16)
    rest = value - high.astype(jnp.float32)
    middle = rest.astype(jnp.bfloat16)
    low = (rest - middle.astype(jnp.float32)).astype(jnp.bfloat16)
    return high, middle, low


def step_kernel(
    blocks, stations, per_owner, grad_rows, early, target_ref, owner_ref, source_ref,
    target_row, owner_row, source_row, positions_ref, strengths_ref, core_ref, seed_ref,
    moved_ref, positions_grad_ref, strengths_grad_ref,
    table_ref, strengths_buf, halo_buf, seed_buf, rows_buf, values, terms, grads_ref, base_ref,
    work, from_mate, from_below, from_above, late_in, halo_out, halo_in,
    load_sems, start_sems, send_sems, recv_sems,
    mate_sems, chain_send, chain_recv, late_sems, halo_sems,
):
    ages = grads_ref.shape[-1]
    count = lax.axis_size("age")
    halo = blocks // stations
    here, other, below, above, prior, following = place()
    turb, age, span = here
    late = grad_rows - early
    half = (early + 2 * late) // 16 * 8
    cut = half - 2 * late
    pieces = ((0, cut), (cut, early - cut))
    group = 2 * count
    pairs = target_ref.shape[0]
    me = turb * count + age
    own_rows = me * per_owner

    finish = gather_all(
        blocks, stations, per_owner, positions_ref, strengths_ref, core_ref, seed_ref, table_ref,
        strengths_buf, halo_buf, seed_buf, load_sems, start_sems, send_sems, recv_sems,
    )

    def fetch(t):
        for j in range(TILE):
            p = t * TILE + j
            tgt = target_ref[p]
            owner = owner_ref[p]
            block = source_ref[p]
            src = owner * per_owner + block
            nxt = jnp.where(owner == group - 1, 0, owner + 1) * per_owner + block
            inner = lax.rem(block, stations) < stations - 1
            shed = jnp.where(inner, src + 1, owner * per_owner + 6 * blocks + lax.div(block, stations))
            shed_step = jnp.where(inner, blocks, halo)
            own = own_rows + tgt
            for r in range(6):
                rows_buf[pl.ds(r * TILE + j, 1), :] = table_ref[pl.ds(src + r * blocks, 1), :]
            for r in range(3):
                rows_buf[pl.ds((6 + r) * TILE + j, 1), :] = table_ref[pl.ds(nxt + r * blocks, 1), :]
                rows_buf[pl.ds((9 + r) * TILE + j, 1), :] = table_ref[pl.ds(shed + r * shed_step, 1), :]
                rows_buf[pl.ds((12 + r) * TILE + j, 1), :] = table_ref[pl.ds(own + r * blocks, 1), :]
                rows_buf[pl.ds((15 + r) * TILE + j, 1), :] = seed_buf[pl.ds(tgt + r * blocks, 1), :]

    def tile(t, _):
        rows = [rows_buf[pl.ds(r * TILE, TILE), :] for r in range(18)]
        rows[15:18] = [seed * time_step for seed in rows[15:18]]
        fetch(jnp.minimum(t + 1, pairs // TILE - 1))
        for r, value in enumerate(pair_tile(rows, ages)):
            values[pl.ds(pl.multiple_of(t * TILE, TILE), TILE), pl.ds(r * ages, ages)] = value
        return 0

    fetch(0)
    lax.fori_loop(0, pairs // TILE, tile, 0)
    for k, term in enumerate(split_terms(values[...])):
        terms[pl.ds(k * pairs, pairs), :] = term

    def select(rows, chosen, which):
        row = lax.broadcasted_iota(jnp.int32, (rows, pairs), 0)
        hit = jnp.logical_and(row == chosen, which)
        return jnp.where(hit, 1.0, 0.0).astype(jnp.bfloat16)

    def columns(first, number):
        return terms[:, pl.ds(first * ages, number * ages)]

    owners = owner_row[...]
    sources = source_row[...]
    followers = jnp.where(owners == group - 1, 0, owners + 1)
    inner_row = sources % stations < stations - 1
    lane_first = lax.broadcasted_iota(jnp.int32, (blocks, ages), 1) == 0
    extra = grad_rows - 5 * blocks

    def scatter(column, dest):
        owner = column * count + dest
        from_here = owners == owner
        main = exact_dot(select(blocks, sources, from_here), columns(0, 5))
        inner_shed = exact_dot(
            select(blocks, sources + 1, jnp.logical_and(from_here, inner_row)), columns(5, 3)
        )
        outer_shed = exact_dot(
            select(
                -(-halo // 8) * 8,
                sources // stations,
                jnp.logical_and(from_here, jnp.logical_not(inner_row)),
            ),
            columns(5, 3),
        )
        carry = exact_dot(select(blocks, sources, followers == owner), columns(8, 1))
        for r in range(5):
            value = main[:, r * ages : (r + 1) * ages]
            if r < 3:
                lane0 = pltpu.roll(carry, ages - r, 1) if r else carry
                value = value + inner_shed[:, r * ages : (r + 1) * ages]
                value = value + jnp.where(lane_first, lane0, 0.0)
            grads_ref[part(column, dest, r * blocks, blocks), :] = value
        outer = [outer_shed[0:halo, r * ages : (r + 1) * ages] for r in range(3)]
        if extra > 3 * halo:
            outer.append(jnp.zeros((extra - 3 * halo, ages), jnp.float32))
        grads_ref[part(column, dest, 5 * blocks, extra), :] = jnp.concatenate(outer)
    spans = ((0, half), (half, early + 2 * late - half))
    has_below = age > 0
    has_above = age < count - 1

    def part(column, dest, start, number):
        owner = column * count + dest
        return pl.ds(pl.multiple_of(owner * grad_rows + start, 8), number)

    def mate_copy(dest, piece):
        return pltpu.make_async_remote_copy(
            src_ref=grads_ref.at[part(1 - turb, dest, *pieces[piece])],
            dst_ref=from_mate.at[dest, pl.ds(*pieces[piece])],
            send_sem=mate_sems.at[0, dest, piece],
            recv_sem=mate_sems.at[1, dest, piece],
            device_id=other,
            device_id_type=MESH,
        )

    def chain_copy(dest, piece, upward):
        at = pl.ds(*spans[piece])
        return pltpu.make_async_remote_copy(
            src_ref=work.at[dest, at],
            dst_ref=(from_below if upward else from_above).at[dest, at],
            send_sem=chain_send.at[dest, piece],
            recv_sem=chain_recv.at[0 if upward else 1, dest, piece],
            device_id=above if upward else below,
            device_id_type=MESH,
        )

    order = [jnp.int32(0)] * count
    rank = jnp.int32(0)
    for distance in range(count - 1, -1, -1):
        for sign in (1, -1) if distance else (1,):
            dest = age + sign * distance
            valid = jnp.logical_and(dest >= 0, dest < count)
            order = [
                jnp.where(jnp.logical_and(valid, rank == k), dest, order[k]) for k in range(count)
            ]
            rank = rank + valid.astype(jnp.int32)
    steps = [(order[k], piece) for k in range(count) for piece in range(2)]

    scatter(1 - turb, order[0])
    mate_copy(*steps[0]).start()
    mate_copy(*steps[1]).start()

    def take(number):
        dest, piece = steps[number]
        if piece == 0:
            scatter(turb, dest)
            if number + 2 < len(steps):
                scatter(1 - turb, steps[number + 2][0])
        mate_copy(dest, piece).wait_recv()
        if piece == 0 and number + 2 < len(steps):
            mate_copy(*steps[number + 2]).start()
            mate_copy(*steps[number + 3]).start()
        start, size = pieces[piece]
        if piece == 0:
            work[dest, pl.ds(0, late), :] = grads_ref[part(turb, dest, early, late), :]
            work[dest, pl.ds(late, late), :] = grads_ref[part(1 - turb, dest, early, late), :]
        work[dest, pl.ds(2 * late + start, size), :] = (
            grads_ref[part(turb, dest, start, size), :] + from_mate[dest, pl.ds(start, size), :]
        )
        at = pl.ds(*spans[piece])

        @pl.when(jnp.logical_and(dest >= age, has_below))
        def _():
            chain_copy(dest, piece, True).wait_recv()
            work[dest, at, :] = work[dest, at, :] + from_below[dest, at, :]

        @pl.when(jnp.logical_and(dest <= age, has_above))
        def _():
            chain_copy(dest, piece, False).wait_recv()
            work[dest, at, :] = work[dest, at, :] + from_above[dest, at, :]

        pl.when(dest > age)(lambda: chain_copy(dest, piece, True).start())
        pl.when(dest < age)(lambda: chain_copy(dest, piece, False).start())

    take(0)
    target_sums = exact_dot(select(blocks, target_row[...], target_row[...] >= 0), columns(9, 6))
    for c in range(3):
        at = pl.ds(c * blocks, blocks)
        velocity = target_sums[:, c * ages : (c + 1) * ages]
        moved_ref[at, :] = time_step * (velocity + 1.0 if c == 0 else velocity)
        base_ref[at, :] = target_sums[:, (3 + c) * ages : (4 + c) * ages]
    for number in range(1, len(steps) - 1):
        take(number)
    late_copy = pltpu.make_async_remote_copy(
        src_ref=work.at[age, pl.ds(late, late)],
        dst_ref=late_in,
        send_sem=late_sems.at[0],
        recv_sem=late_sems.at[1],
        device_id=other,
        device_id_type=MESH,
    )
    late_copy.start()
    late_copy.wait_recv()
    work[age, pl.ds(0, late), :] = work[age, pl.ds(0, late), :] + late_in[...]
    halo_out[...] = work[age, pl.ds(5 * blocks - early, grad_rows - 5 * blocks), :]
    halo_copy = pltpu.make_async_remote_copy(
        src_ref=halo_out,
        dst_ref=halo_in,
        send_sem=halo_sems.at[0],
        recv_sem=halo_sems.at[1],
        device_id=following,
        device_id_type=MESH,
    )
    halo_copy.start()
    trail, shed = keeps(stations, ages, (2 * blocks, ages))
    row = lax.broadcasted_iota(jnp.int32, (2 * blocks, ages), 0)
    keep = jnp.where(row < blocks, trail, shed)
    first = early - 3 * blocks
    strengths_grad_ref[pl.ds(first, 2 * blocks - first), :] = (
        work[age, pl.ds(0, 2 * blocks - first), :] * keep[first:]
    )
    take(len(steps) - 1)
    strengths_grad_ref[pl.ds(0, first), :] = (
        work[age, pl.ds(2 * late + 3 * blocks, first), :] * keep[:first]
    )
    positions_grad_ref[...] = base_ref[...] + work[age, pl.ds(2 * late, 3 * blocks), :]
    halo_copy.wait_recv()
    for k in range(3 * halo):
        at = pl.ds(k * stations, 1)
        positions_grad_ref[at, :] = positions_grad_ref[at, :] + halo_in[pl.ds(k, 1), :]
    finish()
    late_copy.wait_send()
    halo_copy.wait_send()
    for dest in range(count):
        for piece in range(2):
            mate_copy(dest, piece).wait_send()
            pl.when(dest > age)(lambda d=dest, p=piece: chain_copy(d, p, True).wait_send())
            pl.when(dest < age)(lambda d=dest, p=piece: chain_copy(d, p, False).wait_send())


def local_dense(positions, strengths, core_radius, adjoint_seed, pair_target, pair_owner, pair_source):
    shape_here = positions.shape
    stations = shape_here[3]
    ages = shape_here[4]
    blocks = shape_here[1] * shape_here[2] * stations
    halo = blocks // stations
    count = lax.axis_size("age")
    group = lax.axis_size("turb") * count
    pairs = pair_target.shape[-1]
    per_owner = -(-(6 * blocks + 3 * halo) // 8) * 8
    grad_rows = -(-(5 * blocks + 3 * halo) // 8) * 8
    early = grad_rows * 5 // 6 // 8 * 8
    late = grad_rows - early
    extra = grad_rows - 5 * blocks
    vmem = pl.BlockSpec(memory_space=pltpu.VMEM)
    smem = pl.BlockSpec(memory_space=pltpu.SMEM)
    kept = pl.BlockSpec(memory_space=pl.ANY)
    dma = pltpu.SemaphoreType.DMA
    rows_out = jax.ShapeDtypeStruct((3 * blocks, ages), jnp.float32)

    def room(*shape):
        return pltpu.VMEM(shape + (ages,), jnp.float32)

    lists = (pair_target, pair_owner, pair_source)
    moved, grad_moved, grad_strengths = pl.pallas_call(
        functools.partial(step_kernel, blocks, stations, per_owner, grad_rows, early),
        out_shape=(rows_out, rows_out, jax.ShapeDtypeStruct((2 * blocks, ages), jnp.float32)),
        in_specs=[smem] * 3 + [vmem] * 3 + [kept] * 4,
        out_specs=(vmem, vmem, vmem),
        scratch_shapes=[
            room(group * per_owner),
            room(2 * blocks),
            room(per_owner - 6 * blocks),
            room(3 * blocks),
            room(18 * TILE),
            pltpu.VMEM((pairs, 15 * ages), jnp.float32),
            pltpu.VMEM((3 * pairs, 15 * ages), jnp.bfloat16),
            room(group * grad_rows),
            room(3 * blocks),
            room(count, early + 2 * late),
            room(count, early),
            room(count, early + 2 * late),
            room(count, early + 2 * late),
            room(late),
            room(extra),
            room(extra),
            dma((4,)),
            dma((2,)),
            dma((3, 3, group)),
            dma((3, group)),
            dma((2, count, 2)),
            dma((count, 2)),
            dma((2, count, 2)),
            dma((2,)),
            dma((2,)),
        ],
        compiler_params=pltpu.CompilerParams(
            collective_id=0, has_side_effects=True, vmem_limit_bytes=60 * 1024 * 1024
        ),
    )(
        *[pair.reshape(pairs) for pair in lists],
        *[pair.reshape(1, pairs) for pair in lists],
        positions.reshape(3 * blocks, ages),
        strengths.reshape(2 * blocks, ages),
        core_radius.reshape(blocks, ages),
        adjoint_seed.reshape(3 * blocks, ages),
    )
    return (
        positions + moved.reshape(shape_here),
        adjoint_seed + grad_moved.reshape(shape_here),
        grad_strengths.reshape(strengths.shape),
    )


def local(positions, strengths, core_radius, adjoint_seed, pair_target, pair_owner, pair_source):
    blocks = positions.shape[1] * positions.shape[2] * positions.shape[3]
    group = lax.axis_size("turb") * lax.axis_size("age")
    fits = lax.axis_size("turb") == 2 and lax.axis_size("span") > 2 and lax.axis_size("age") > 1
    dense = fits and group * blocks <= 8 * pair_target.shape[-1]
    chosen = local_dense if dense else local_sparse
    return chosen(
        positions, strengths, core_radius, adjoint_seed, pair_target, pair_owner, pair_source
    )


def solution(mesh):
    placed = (
        P(None, "turb", None, "span", "age"),
        P(None, "turb", None, "span", "age"),
        P("turb", None, "span", "age"),
        P(None, "turb", None, "span", "age"),
        P("turb", "age", "span", None),
        P("turb", "age", "span", None),
        P("turb", "age", "span", None),
    )
    return jax.shard_map(
        local,
        mesh=mesh,
        in_specs=placed,
        out_specs=(
            P(None, "turb", None, "span", "age"),
            P(None, "turb", None, "span", "age"),
            P(None, "turb", None, "span", "age"),
        ),
        check_vma=False,
    )
```
